32 devices in a mesh: dp: 16 (over z, x, core), fsdp: 2 (over y).
Axes of the slice: x: 2, y: 2, z: 4, core: 2. Of those that a mesh axis runs over, the one named last changes fastest.
Arguments:
- hidden_in: bfloat16 [224, 128, 768], P(('dp', 'fsdp')), may hold values from -100 to 100
- row_counts: int32 [32], P(('dp', 'fsdp')), may hold values from 2 to 7
- buckets: int32 [224], P(('dp', 'fsdp')), may hold values from 0 to 2, as said below
- lengths: int32 [224, 4], P(('dp', 'fsdp')), may hold values from 0 to 128, as said below
- keep_masks: int32 [2, 2, 224, 128, 768], P(None, None, ('dp', 'fsdp')), may hold values 0 or 1
- out_cotangent: bfloat16 [2, 224, 128, 768], P(None, ('dp', 'fsdp')), may hold values from -6 to 6
- w_query: bfloat16 [768, 768], P(('dp', 'fsdp')), may hold values from -0.21875 to 0.21875
- b_query: bfloat16 [768], P(('dp', 'fsdp')), may hold values from -3 to 3
- w_key: bfloat16 [768, 768], P(('dp', 'fsdp')), may hold values from -0.21875 to 0.21875
- w_value: bfloat16 [768, 768], P(('dp', 'fsdp')), may hold values from -0.21875 to 0.21875
- b_value: bfloat16 [768], P(('dp', 'fsdp')), may hold values from -3 to 3
- w_attn_out: bfloat16 [768, 768], P(('dp', 'fsdp')), may hold values from -1.25 to 1.25
- b_attn_out: bfloat16 [768], P(('dp', 'fsdp')), may hold values from -3 to 3
- norm1_gain: bfloat16 [768], P(('dp', 'fsdp')), may hold values from 0.099609375 to 1.8984375
- norm1_bias: bfloat16 [768], P(('dp', 'fsdp')), may hold values from -2 to 2
- w_inner: bfloat16 [768, 3072], P(('dp', 'fsdp')), may hold values from -0.21875 to 0.21875
- b_inner: bfloat16 [3072], P(('dp', 'fsdp')), may hold values from -3 to 3
- w_outer: bfloat16 [3072, 768], P(('dp', 'fsdp')), may hold values from -0.109375 to 0.109375
- b_outer: bfloat16 [768], P(('dp', 'fsdp')), may hold values from -3 to 3
- norm2_gain: bfloat16 [768], P(('dp', 'fsdp')), may hold values from 0.099609375 to 1.8984375
- norm2_bias: bfloat16 [768], P(('dp', 'fsdp')), may hold values from -2 to 2
- w_pool: bfloat16 [768, 768], P(('dp', 'fsdp')), may hold values from -0.21875 to 0.21875
- b_pool: bfloat16 [768], P(('dp', 'fsdp')), may hold values from -2 to 2
- log_temp: float32 [1], replicated, may hold values from -1.9 to -1.4
Outputs:
- loss: float32 [1], replicated
- outputs: bfloat16 [2, 224, 128, 768], P(None, ('dp', 'fsdp'))
- input_grad: float32 [224, 128, 768], P(('dp', 'fsdp'))
- grad_w_query: float32 [768, 768], P(('dp', 'fsdp'))
- grad_b_query: float32 [768], P(('dp', 'fsdp'))
- grad_w_key: float32 [768, 768], P(('dp', 'fsdp'))
- grad_w_value: float32 [768, 768], P(('dp', 'fsdp'))
- grad_b_value: float32 [768], P(('dp', 'fsdp'))
- grad_w_attn_out: float32 [768, 768], P(('dp', 'fsdp'))
- grad_b_attn_out: float32 [768], P(('dp', 'fsdp'))
- grad_norm1_gain: float32 [768], P(('dp', 'fsdp'))
- grad_norm1_bias: float32 [768], P(('dp', 'fsdp'))
- grad_w_inner: float32 [768, 3072], P(('dp', 'fsdp'))
- grad_b_inner: float32 [3072], P(('dp', 'fsdp'))
- grad_w_outer: float32 [3072, 768], P(('dp', 'fsdp'))
- grad_b_outer: float32 [768], P(('dp', 'fsdp'))
- grad_norm2_gain: float32 [768], P(('dp', 'fsdp'))
- grad_norm2_bias: float32 [768], P(('dp', 'fsdp'))
- grad_w_pool: float32 [768, 768], P(('dp', 'fsdp'))
- grad_b_pool: float32 [768], P(('dp', 'fsdp'))
- log_temp_grad: float32 [1], replicated
The draws below stay inside these ranges and needn't reach their ends.
Inputs may be any that keep to these rules, and one draw needn't show every extreme that they name: `buckets`: a row of bucket b holds 4 >> b sentences of 128 >> (3 - b) + 1 to 128 >> (2 - b) tokens. Entry k of a row is its k-th sentence's length for k < 4 >> b and 0 after; a row's lengths sum to at most 128.
All inputs are finite; a program needn't handle non-finite values. No bound on the sum of `keep_masks` on one device may be relied on, other than what follows from the above.
Results may differ from the reference program's by a relative error of at most 0.014.
Values may be sent and summed in bfloat16 or wider, within the bound.
No kernel may reach another device: no remote copies, remote signals or barrier semaphores. Data moves between devices by JAX's collectives and lax.ppermute only.
A program may use at most 320 MiB of HBM per device.

```python
import jax
import jax.numpy as jnp
from jax import lax

D = 768
HEADS = 12
HEAD_DIM = 64
FF = 3072
ROW = 128
SLOTS = 7
ROWS = 224


def bucket_helper(key):
    bucket_ids = jax.random.randint(jax.random.fold_in(key, 101), (ROWS,), 0, 3)
    return bucket_ids.at[0].set(2).astype(jnp.int32)


def draw_buckets(key, part):
    return bucket_helper(key)


def draw_lengths(key, part):
    bucket_ids = bucket_helper(key)
    key = jax.random.fold_in(key, 2)
    lowest = jnp.right_shift(jnp.int32(ROW), 3 - bucket_ids) + 1
    highest = jnp.right_shift(jnp.int32(ROW), 2 - bucket_ids)
    raw_bits = jax.random.randint(key, (ROWS, 4), 0, 1 << 20)
    chosen = lowest[:, None] + raw_bits % (highest - lowest + 1)[:, None]
    allowed = jnp.arange(4, dtype=jnp.int32)[None, :] < jnp.right_shift(jnp.int32(4), bucket_ids)[:, None]
    chosen = jnp.where(allowed, chosen, 0)
    chosen = chosen.at[0, 0].set(ROW)
    return chosen.astype(jnp.int32)


def draw_row_counts(key, part):
    key = jax.random.fold_in(key, 3)
    devices = ROWS // SLOTS
    rolled = jax.random.randint(key, (devices,), 0, 8)
    counts = jnp.where(rolled == 0, SLOTS, jnp.where(rolled < 4, 2, min(3, SLOTS)))
    shuffled = jax.random.permutation(jax.random.fold_in(key, 4), devices)
    counts = counts.at[shuffled[0]].set(SLOTS).at[shuffled[1]].set(2)
    return counts.astype(jnp.int32)


def draw_hidden_in(key, part):
    key = jax.random.fold_in(key, 5)
    basis_rows = jax.random.normal(jax.random.fold_in(key, 1), (8, D), jnp.float32)
    factors = jax.random.normal(jax.random.fold_in(key, 2), (ROWS, ROW, 8), jnp.float32)
    noise_part = jax.random.normal(jax.random.fold_in(key, 3), (ROWS, ROW, D), jnp.float32)
    summed = noise_part
    for column_idx in range(8):
        summed = summed + factors[:, :, column_idx:column_idx + 1] * basis_rows[column_idx]
    return (summed / 3.0).astype(jnp.bfloat16)


def touch_ends(result, rng, low, high):
    longest = result.shape.index(max(result.shape))
    spots = []
    for shift in (0, 1):
        where = [jax.random.randint(jax.random.fold_in(rng, axis), (), 0, length) for axis, length in enumerate(result.shape)]
        where[longest] = (where[longest] + shift) % result.shape[longest]
        spots.append(tuple(where))
    return result.at[spots[0]].set(low).at[spots[1]].set(high)


def block_levels(own_key, extent, split, least, largest):
    factor_of, own = 1.0, jax.random.fold_in(own_key, 6)
    for position, shards_of in split:
        steps = jnp.exp(jax.random.uniform(jax.random.fold_in(own, position), (shards_of,), jnp.float32, least / len(split), largest / len(split)))
        factor_of = factor_of * jnp.repeat(steps, extent[position] // shards_of).reshape([-1 if axis == position else 1 for axis in range(len(extent))])
    return factor_of


def scatter_about(stream_key, shape, scale, limit, split=(), kind=jnp.bfloat16):
    loudness = block_levels(stream_key, shape, split, -0.22, 0.18) if split else 1.0
    values = jax.random.normal(stream_key, shape, jnp.float32) * scale * loudness
    return jnp.minimum(jnp.maximum(values, -limit), limit).astype(kind)


def setup_inputs(seed: int = 0) -> dict:
    key_of = jax.random.split(jax.random.key(seed), 25)
    hidden_in = draw_hidden_in(jax.random.fold_in(key_of[24], 71), 0)
    row_counts = draw_row_counts(jax.random.fold_in(key_of[24], 71), 0)
    buckets = draw_buckets(jax.random.fold_in(key_of[24], 71), 0)
    lengths = draw_lengths(jax.random.fold_in(key_of[24], 71), 0)
    keep_masks = touch_ends((jax.random.randint(key_of[4], (2, 2, ROWS, ROW, D), 0, 10) < 9).astype(jnp.int32), jax.random.fold_in(key_of[4], 1), 0, 1)
    out_cotangent = scatter_about(key_of[5], (2, ROWS, ROW, D), 1.0, 6.0, ((1, 32),))
    w_query = scatter_about(key_of[6], (D, D), D ** -0.5, 0.21875, ((0, 32),))
    b_query = scatter_about(key_of[7], (D,), 0.5, 3.0, ((0, 32),))
    w_key = scatter_about(key_of[8], (D, D), D ** -0.5, 0.21875, ((0, 32),))
    w_value = scatter_about(key_of[9], (D, D), D ** -0.5, 0.21875, ((0, 32),))
    b_value = scatter_about(key_of[10], (D,), 0.5, 3.0, ((0, 32),))
    w_attn_out = scatter_about(key_of[11], (D, D), (D // 32) ** -0.5, 1.25, ((0, 32),))
    b_attn_out = scatter_about(key_of[12], (D,), 0.5, 3.0, ((0, 32),))
    norm1_gain = jnp.clip(1.0 + 0.18 * jax.random.normal(key_of[13], (D,), jnp.float32), 0.099609375, 1.8984375).astype(jnp.bfloat16)
    norm1_bias = scatter_about(key_of[14], (D,), 0.3, 2.0, ((0, 32),))
    w_inner = scatter_about(key_of[15], (D, FF), D ** -0.5, 0.21875, ((0, 32),))
    b_inner = scatter_about(key_of[16], (FF,), 0.5, 3.0, ((0, 32),))
    w_outer = scatter_about(key_of[17], (FF, D), FF ** -0.5, 0.109375, ((0, 32),))
    b_outer = scatter_about(key_of[18], (D,), 0.5, 3.0, ((0, 32),))
    norm2_gain = jnp.clip(1.0 + 0.18 * jax.random.normal(key_of[19], (D,), jnp.float32), 0.099609375, 1.8984375).astype(jnp.bfloat16)
    norm2_bias = scatter_about(key_of[20], (D,), 0.3, 2.0, ((0, 32),))
    w_pool = scatter_about(key_of[21], (D, D), D ** -0.5, 0.21875, ((0, 32),))
    b_pool = scatter_about(key_of[22], (D,), 0.3, 2.0, ((0, 32),))
    log_temp = jnp.clip(jax.random.uniform(key_of[23], (1,), jnp.float32, -1.9, -1.4), -1.9, -1.4)
    return {"hidden_in": hidden_in, "row_counts": row_counts, "buckets": buckets, "lengths": lengths, "keep_masks": keep_masks, "out_cotangent": out_cotangent, "w_query": w_query, "b_query": b_query, "w_key": w_key, "w_value": w_value, "b_value": b_value, "w_attn_out": w_attn_out, "b_attn_out": b_attn_out, "norm1_gain": norm1_gain, "norm1_bias": norm1_bias, "w_inner": w_inner, "b_inner": b_inner, "w_outer": w_outer, "b_outer": b_outer, "norm2_gain": norm2_gain, "norm2_bias": norm2_bias, "w_pool": w_pool, "b_pool": b_pool, "log_temp": log_temp}


@jax.custom_vjp
def low(v):
    return lax.optimization_barrier(v.astype(jnp.bfloat16)).astype(jnp.float32)

@jax.custom_vjp
def low_back(v):
    return v

def low_keep(v):
    return (low(v), None)

def low_pass(kept, grad):
    return (grad,)

def back_keep(v):
    return (v, None)

def back_low(kept, grad):
    return (low(grad),)
low.defvjp(low_keep, low_pass)
low_back.defvjp(back_keep, back_low)
precise = lax.Precision.HIGHEST
keep_scale = 1.0 / 0.9
block_rows = 32

def layout(row_counts, buckets, lengths):
    within = jnp.arange(ROWS, dtype=jnp.int32) % SLOTS
    owners = jnp.arange(ROWS, dtype=jnp.int32) // SLOTS
    live_rows = within < row_counts[owners]
    sent_count = jnp.right_shift(jnp.int32(4), buckets)
    slot_ids = jnp.arange(4, dtype=jnp.int32)
    held_slots = (slot_ids[None, :] < sent_count[:, None]) & live_rows[:, None]
    sizes_used = jnp.where(held_slots, lengths, 0).astype(jnp.int32)
    finish = jnp.cumsum(sizes_used, axis=1, dtype=jnp.int32)
    starts = finish - sizes_used
    places = jnp.arange(ROW, dtype=jnp.int32)
    segment = lax.optimization_barrier(jnp.sum((places[None, :, None] >= finish[:, None, :]).astype(jnp.int32), axis=2))
    token_ok = (segment < 4).astype(jnp.float32)
    cls_table = ((places[None, None, :] == starts[:, :, None]) & held_slots[:, :, None]).astype(jnp.float32)
    return (segment, token_ok, cls_table, held_slots.astype(jnp.float32))

def norm_fwd(hidden, gain, shift):
    centre = lax.optimization_barrier(jnp.mean(hidden, axis=-1, keepdims=True))
    offset = hidden - centre
    spread = lax.optimization_barrier(jnp.mean(offset * offset, axis=-1, keepdims=True))
    return offset * lax.rsqrt(spread + 1e-06) * gain + shift

def mixed(left, right):
    return jnp.einsum('bld,de->ble', left, right, precision=precise)

def block_forward(params, rows_x, segment, keeps):
    w_query, b_query, w_key, w_value, b_value, w_attn_out, b_attn_out, norm1_gain, norm1_bias, w_inner, b_inner, w_outer, b_outer, norm2_gain, norm2_bias = params[:15]
    batch = rows_x.shape[0]

    def split_heads(matrix):
        return matrix.reshape(batch, ROW, HEADS, HEAD_DIM)
    query = low(low_back(mixed(rows_x, w_query) + b_query))
    keys_all = low(low_back(mixed(rows_x, w_key)))
    values_all = low(low_back(mixed(rows_x, w_value) + b_value))
    scores = low_back(jnp.einsum('blhd,bmhd->bhlm', split_heads(query), split_heads(keys_all), precision=precise) * 0.125)
    same_seg = (segment[:, :, None] == segment[:, None, :])[:, None]
    scores = jnp.where(same_seg, scores, -1e+30)
    peak = lax.optimization_barrier(jnp.max(scores, axis=-1, keepdims=True))
    log_total = peak + jnp.log(lax.optimization_barrier(jnp.sum(jnp.exp(scores - peak), axis=-1, keepdims=True)))
    weights_att = jnp.exp(scores - log_total)
    attended = jnp.einsum('bhlm,bmhd->blhd', low(weights_att), split_heads(values_all), precision=precise).reshape(batch, ROW, D)
    attended = low(low_back(attended))
    branch = low_back(mixed(attended, w_attn_out) + b_attn_out)
    results = []
    for view_idx in range(2):
        first_sum = rows_x + branch * keeps[view_idx, 0]
        normed = norm_fwd(first_sum, norm1_gain, norm1_bias)
        inner = low_back(mixed(low(normed), w_inner) + b_inner)
        active = low(jax.nn.gelu(inner, approximate=False))
        outer = low_back(mixed(active, w_outer) + b_outer)
        second_sum = normed + outer * keeps[view_idx, 1]
        results.append(low(norm_fwd(second_sum, norm2_gain, norm2_bias)))
    return jnp.stack(results)

def forward(params, hidden, log_temp, segment, token_ok, cls_table, held, keeps, cotangent):
    blocks = ROWS // block_rows
    rows_in = hidden.reshape(blocks, block_rows, ROW, D)
    segs_in = segment.reshape(blocks, block_rows, ROW)
    keep_blocks = jnp.moveaxis(keeps.reshape(2, 2, blocks, block_rows, ROW, D), 2, 0)
    step_fn = jax.checkpoint(lambda items: block_forward(params, items[0], items[1], items[2]))
    outs = lax.map(step_fn, (rows_in, segs_in, keep_blocks))
    outs = jnp.moveaxis(outs, 1, 0).reshape(2, ROWS, ROW, D)
    w_pool = params[15]
    b_pool = params[16]
    cls_rows = jnp.einsum('rkl,vrld->vrkd', cls_table, outs, precision=precise).reshape(2, ROWS * 4, D)
    pre_pool = low_back(jnp.einsum('vsd,de->vse', cls_rows, w_pool, precision=precise) + b_pool)
    pooled = jnp.tanh(pre_pool)
    unit = low(pooled * lax.rsqrt(lax.optimization_barrier(jnp.sum(pooled * pooled, axis=-1, keepdims=True)) + 1e-06))
    inv_temp = jnp.exp(-log_temp[0])
    flags = held.reshape(ROWS * 4)
    logits = jnp.dot(unit[0], unit[1].T, precision=precise) * inv_temp
    logits = jnp.where(flags[None, :] > 0, logits, -1e+30)
    peak = lax.optimization_barrier(jnp.max(logits, axis=-1, keepdims=True))
    sim_total = peak[:, 0] + jnp.log(lax.optimization_barrier(jnp.sum(jnp.exp(logits - peak), axis=-1)))
    positive = lax.optimization_barrier(jnp.sum(unit[0] * unit[1], axis=-1)) * inv_temp
    held_total = jnp.sum(flags)
    loss = jnp.sum(flags * (sim_total - positive)) / held_total
    objective = loss + jnp.sum(cotangent * token_ok[None, :, :, None] * outs)
    return (objective, (loss, outs))

def reference(hidden_in, row_counts, buckets, lengths, keep_masks, out_cotangent, w_query, b_query, w_key, w_value, b_value, w_attn_out, b_attn_out, norm1_gain, norm1_bias, w_inner, b_inner, w_outer, b_outer, norm2_gain, norm2_bias, w_pool, b_pool, log_temp):
    segment, token_ok, cls_table, held = layout(row_counts, buckets, lengths)
    keeps = keep_masks.astype(jnp.float32) * keep_scale
    cotangent = out_cotangent.astype(jnp.float32)
    params = tuple((weight.astype(jnp.float32) for weight in (w_query, b_query, w_key, w_value, b_value, w_attn_out, b_attn_out, norm1_gain, norm1_bias, w_inner, b_inner, w_outer, b_outer, norm2_gain, norm2_bias, w_pool, b_pool)))

    def wrapped(param_set, hidden, temp):
        return forward(param_set, hidden, temp, segment, token_ok, cls_table, held, keeps, cotangent)
    objective, pullback, extra = jax.vjp(wrapped, params, hidden_in.astype(jnp.float32), log_temp, has_aux=True)
    grads_w, grad_hidden, grad_temp = pullback(jnp.ones_like(objective))
    loss, outs = extra
    return (loss.reshape(1), outs.astype(jnp.bfloat16), grad_hidden, grads_w[0], grads_w[1], grads_w[2], grads_w[3], grads_w[4], grads_w[5], grads_w[6], grads_w[7], grads_w[8], grads_w[9], grads_w[10], grads_w[11], grads_w[12], grads_w[13], grads_w[14], grads_w[15], grads_w[16], grad_temp)
```

```python
import jax
import jax.numpy as jnp
from jax import lax
from jax.sharding import PartitionSpec as P

HEADS = 12
BOTH = ("dp", "fsdp")

precise = lax.Precision.HIGHEST
keep_scale = 1.0 / 0.9
inv_root_two = 0.7071067811865476
inv_root_tau = 0.3989422804014327


def matmul(left, right):
    return jnp.dot(left, right, preferred_element_type=jnp.float32)


def against(left, right):
    return lax.dot_general(
        left, right, (((1,), (1,)), ((), ())), preferred_element_type=jnp.float32
    )


def across(left, right):
    return lax.dot_general(
        left, right, (((0,), (0,)), ((), ())), preferred_element_type=jnp.float32
    )


def layout(row_counts, buckets, lengths, row_len):
    slot_count = buckets.shape[0]
    live_rows = jnp.arange(slot_count, dtype=jnp.int32) < row_counts[0]
    sent_count = jnp.right_shift(jnp.int32(4), buckets)
    slot_ids = jnp.arange(4, dtype=jnp.int32)
    held_slots = (slot_ids[None, :] < sent_count[:, None]) & live_rows[:, None]
    sizes_used = jnp.where(held_slots, lengths, 0)
    finish = jnp.cumsum(sizes_used, axis=1, dtype=jnp.int32)
    starts = finish - sizes_used
    places = jnp.arange(row_len, dtype=jnp.int32)
    segment = jnp.sum((places[None, :, None] >= finish[:, None, :]).astype(jnp.int32), axis=2)
    cls_table = ((places[None, None, :] == starts[:, :, None]) & held_slots[:, :, None]).astype(
        jnp.float32
    )
    return (segment, (segment < 4).astype(jnp.float32), cls_table, held_slots.astype(jnp.float32))


def norm_fwd(hidden, gain, shift):
    centre = jnp.mean(hidden, axis=-1, keepdims=True)
    offset = hidden - centre
    spread = jnp.mean(offset * offset, axis=-1, keepdims=True)
    rscale = lax.rsqrt(spread + 1e-06)
    normed = offset * rscale
    return (normed * gain + shift, normed, rscale)


def norm_back(grad_out, normed, rscale, gain):
    grad_norm = grad_out * gain
    mean_grad = jnp.mean(grad_norm, axis=-1, keepdims=True)
    mean_cross = jnp.mean(grad_norm * normed, axis=-1, keepdims=True)
    grad_in = rscale * (grad_norm - mean_grad - normed * mean_cross)
    return (grad_in, jnp.sum(grad_out * normed, axis=(0, 1)), jnp.sum(grad_out, axis=(0, 1)))


def paired():
    return lax.axis_size("dp") == 16 and lax.axis_size("fsdp") == 2


def place(z, x, c, y):
    return ((z * 2 + x) * 2 + c) * 2 + y


def pairs(move):
    every = [(z, x, c, y) for z in range(4) for x in range(2) for c in range(2) for y in range(2)]
    return [(place(*t), place(*move(*t))) for t in every]


def first_pairs():
    return pairs(lambda z, x, c, y: (z, 1 - x, c, y) if c == 0 else (z, x, c, 1 - y))


def second_pairs():
    return pairs(lambda z, x, c, y: (z, x, c, 1 - y) if c == 0 else (z, 1 - x, c, y))


def core_pairs():
    return pairs(lambda z, x, c, y: (z, x, 1 - c, y))


def along_pairs(k):
    return pairs(lambda z, x, c, y: ((z + k) % 4, x, c, y))


def whereabouts():
    index = lax.axis_index(BOTH)
    return index // 8, index // 4 % 2, index // 2 % 2, index % 2


def spot(x, y, c, p1, p2):
    on_x = jnp.where(c == 0, p1, p2)
    on_y = jnp.where(c == 0, p2, p1)
    return x ^ on_x, y ^ on_y


def collect(shard):
    z, x, c, y = whereabouts()
    shape = (4,) + shard.shape
    column = jnp.zeros(shape, shard.dtype)
    column = lax.dynamic_update_index_in_dim(column, shard, z, 0)
    for k in (1, 2, 3):
        come = lax.ppermute(shard, BOTH, along_pairs(k))
        column = lax.dynamic_update_index_in_dim(column, come, (z - k) % 4, 0)
    one = lax.ppermute(column, BOTH, first_pairs())
    pair = jnp.stack([column, one])
    two = lax.ppermute(pair, BOTH, second_pairs())
    four = jnp.concatenate([pair, two])
    other = lax.ppermute(four, BOTH, core_pairs())
    out = jnp.zeros((4, 2, 2, 2) + shard.shape, shard.dtype)
    for blocks, core in ((four, c), (other, 1 - c)):
        for p2 in (0, 1):
            for p1 in (0, 1):
                at_x, at_y = spot(x, y, core, p1, p2)
                block = blocks[2 * p2 + p1][:, None, None, None]
                out = lax.dynamic_update_slice(out, block, (0, at_x, core, at_y, 0, 0))
    return out.reshape((32,) + shard.shape)


def deliver(whole):
    z, x, c, y = whereabouts()
    tail = whole.shape[1:]
    grid = whole.reshape((4, 2, 2, 2) + tail)

    def blocks(core):
        picked = []
        for p2 in (0, 1):
            for p1 in (0, 1):
                at_x, at_y = spot(x, y, core, p1, p2)
                block = lax.dynamic_slice(grid, (0, at_x, core, at_y, 0, 0), (4, 1, 1, 1) + tail)
                picked.append(block.reshape((4,) + tail))
        return jnp.stack(picked).reshape((2, 2, 4) + tail)

    def add(kept, come):
        return (kept.astype(jnp.float32) + come.astype(jnp.float32)).astype(jnp.bfloat16)

    come = lax.ppermute(blocks(1 - c), BOTH, core_pairs())
    held = add(blocks(c), come)
    held = add(held[0], lax.ppermute(held[1], BOTH, second_pairs()))
    held = add(held[0], lax.ppermute(held[1], BOTH, first_pairs()))
    total = lax.dynamic_index_in_dim(held, z, 0, keepdims=False).astype(jnp.float32)
    for k in (1, 2, 3):
        away = lax.dynamic_index_in_dim(held, (z + k) % 4, 0, keepdims=False)
        total = total + lax.ppermute(away, BOTH, along_pairs(k)).astype(jnp.float32)
    return total


def gather_all(shards):
    if not paired():
        return [lax.all_gather(s, BOTH, axis=0, tiled=True) for s in shards]
    sizes = [s.size for s in shards]
    flat = jnp.concatenate([s.reshape(-1) for s in shards])
    rows = -(-flat.size // (768 * 16)) * 16
    flat = jnp.pad(flat, (0, rows * 768 - flat.size)).reshape(rows, 768)
    whole = collect(flat).reshape(32, -1)
    outs, at = [], 0
    for s, size in zip(shards, sizes):
        outs.append(whole[:, at : at + size].reshape((32 * s.shape[0],) + s.shape[1:]))
        at += size
    return outs


def scatter_all(wholes):
    if not paired():
        return [lax.psum_scatter(w, BOTH, scatter_dimension=0, tiled=True) for w in wholes]
    shapes = [(w.shape[0] // 32,) + w.shape[1:] for w in wholes]
    flat = jnp.concatenate([w.astype(jnp.bfloat16).reshape(32, -1) for w in wholes], axis=1)
    rows = -(-flat.shape[1] // (768 * 16)) * 16
    flat = jnp.pad(flat, ((0, 0), (0, rows * 768 - flat.shape[1]))).reshape(32, rows, 768)
    part = deliver(flat).reshape(-1)
    outs, at = [], 0
    for shape in shapes:
        size = 1
        for extent in shape:
            size *= extent
        outs.append(part[at : at + size].reshape(shape))
        at += size
    return outs


def anchor_side(anchors, partners, partners_all, flags, column_ok, inv_temp):
    held_total = jnp.sum(column_ok)
    logits = against(anchors, partners_all) * inv_temp
    logits = jnp.where(column_ok[None, :] > 0, logits, -1e30)
    sim_peak = jnp.max(logits, axis=-1, keepdims=True)
    sim_total = sim_peak + jnp.log(jnp.sum(jnp.exp(logits - sim_peak), axis=-1, keepdims=True))
    anchors_f = anchors.astype(jnp.float32)
    partners_f = partners.astype(jnp.float32)
    positive = jnp.sum(anchors_f * partners_f, axis=-1) * inv_temp
    row_weight = flags / held_total
    loss_part = jnp.sum(row_weight * (sim_total[:, 0] - positive))
    shares = jnp.exp(logits - sim_total) * row_weight[:, None]
    temp_part = jnp.sum(row_weight * positive) - jnp.sum(
        shares * jnp.where(column_ok[None, :] > 0, logits, 0.0)
    )
    grad_anchor = inv_temp * (
        jnp.dot(shares, partners_all.astype(jnp.float32), precision=precise)
        - row_weight[:, None] * partners_f
    )
    return (loss_part, temp_part, grad_anchor, sim_total[:, 0], row_weight, held_total, anchors_f)


def partner_side(partners, anchors_all, totals_all, anchor_ok, flags, held_total, inv_temp):
    back_logits = against(partners, anchors_all) * inv_temp
    back_shares = (
        jnp.exp(back_logits - totals_all[None, :])
        * (anchor_ok / held_total)[None, :]
        * flags[:, None]
    )
    return inv_temp * jnp.dot(back_shares, anchors_all.astype(jnp.float32), precision=precise)


def every_side(anchors, partners, anchors_all, partners_all, flags, column_ok, inv_temp):
    sent_slots = anchors.shape[0]
    held_total = jnp.sum(column_ok)
    logits = against(anchors_all, partners_all) * inv_temp
    logits = jnp.where(column_ok[None, :] > 0, logits, -1e30)
    sim_peak = jnp.max(logits, axis=-1, keepdims=True)
    sim_total = sim_peak + jnp.log(jnp.sum(jnp.exp(logits - sim_peak), axis=-1, keepdims=True))
    positive = inv_temp * jnp.sum(
        anchors_all.astype(jnp.float32) * partners_all.astype(jnp.float32), axis=-1
    )
    weights = column_ok / held_total
    loss = jnp.sum(weights * (sim_total[:, 0] - positive))
    shares = jnp.exp(logits - sim_total) * weights[:, None]
    temp_grad = jnp.sum(weights * positive) - jnp.sum(
        shares * jnp.where(column_ok[None, :] > 0, logits, 0.0)
    )
    first_slot = lax.axis_index(BOTH) * sent_slots
    own_rows = lax.dynamic_slice_in_dim(shares, first_slot, sent_slots, 0)
    own_columns = lax.dynamic_slice_in_dim(shares, first_slot, sent_slots, 1)
    own_weight = flags / held_total
    grad_anchor = inv_temp * (
        jnp.dot(own_rows, partners_all.astype(jnp.float32), precision=precise)
        - own_weight[:, None] * partners.astype(jnp.float32)
    )
    grad_partner = inv_temp * (
        lax.dot_general(
            own_columns,
            anchors_all.astype(jnp.float32),
            (((0,), (0,)), ((), ())),
            precision=precise,
        )
        - own_weight[:, None] * anchors.astype(jnp.float32)
    )
    return loss, temp_grad, grad_anchor, grad_partner


def shared_sides(anchors, partners, anchors_all, partners_all, flags, column_ok, inv_temp):
    loss_part, temp_part, grad_anchor, sim_total, row_weight, held_total, anchors_f = anchor_side(
        anchors, partners, partners_all, flags, column_ok, inv_temp
    )
    totals_all = lax.all_gather(sim_total, BOTH, axis=0, tiled=True)
    grad_partner = partner_side(
        partners, anchors_all, totals_all, column_ok, flags, held_total, inv_temp
    )
    grad_partner = grad_partner - inv_temp * row_weight[:, None] * anchors_f
    loss, temp_grad = lax.psum((loss_part, temp_part), BOTH)
    return loss, temp_grad, grad_anchor, grad_partner


def body(
    hidden_in,
    row_counts,
    buckets,
    lengths,
    keep_masks,
    out_cotangent,
    w_query,
    b_query,
    w_key,
    w_value,
    b_value,
    w_attn_out,
    b_attn_out,
    norm1_gain,
    norm1_bias,
    w_inner,
    b_inner,
    w_outer,
    b_outer,
    norm2_gain,
    norm2_bias,
    w_pool,
    b_pool,
    log_temp,
):
    (
        query_weight,
        key_weight,
        value_weight,
        out_weight,
        query_bias,
        value_bias,
        out_bias,
        gain_one,
        shift_one,
        inner_bias,
        outer_bias,
        gain_two,
        shift_two,
        pool_bias,
    ) = gather_all(
        (
            w_query,
            w_key,
            w_value,
            w_attn_out,
            b_query,
            b_value,
            b_attn_out,
            norm1_gain,
            norm1_bias,
            b_inner,
            b_outer,
            norm2_gain,
            norm2_bias,
            b_pool,
        )
    )
    (inner_weight,) = gather_all((w_inner,))
    outer_weight, pool_weight = gather_all((w_outer, w_pool))
    slots, row_len, width = hidden_in.shape
    head_dim = width // HEADS
    tokens = slots * row_len
    segment, token_ok, cls_table, held_slots = layout(row_counts, buckets, lengths, row_len)
    flat_in = hidden_in.reshape(tokens, width)

    def heads_of(matrix):
        return matrix.reshape(slots, row_len, HEADS, head_dim)

    same_seg = (segment[:, :, None] == segment[:, None, :])[:, None]

    def scores_of(query_heads, key_heads):
        raw_scores = (
            jnp.einsum(
                "slhd,smhd->shlm", query_heads, key_heads, preferred_element_type=jnp.float32
            )
            * 0.125
        )
        return jnp.where(same_seg, raw_scores, -1e30)

    query_low = (matmul(flat_in, query_weight) + query_bias).astype(jnp.bfloat16)
    keys_low = matmul(flat_in, key_weight).astype(jnp.bfloat16)
    values_low = (matmul(flat_in, value_weight) + value_bias).astype(jnp.bfloat16)
    scores = scores_of(heads_of(query_low), heads_of(keys_low))
    peak = jnp.max(scores, axis=-1, keepdims=True)
    log_total = peak + jnp.log(jnp.sum(jnp.exp(scores - peak), axis=-1, keepdims=True))
    probs_low = jnp.exp(scores - log_total).astype(jnp.bfloat16)
    attended = (
        jnp.einsum(
            "shlm,smhd->slhd", probs_low, heads_of(values_low), preferred_element_type=jnp.float32
        )
        .reshape(tokens, width)
        .astype(jnp.bfloat16)
    )
    branch = matmul(attended, out_weight) + out_bias
    keeps = keep_masks.reshape(2, 2, tokens, width).astype(jnp.float32) * keep_scale
    residual = flat_in.astype(jnp.float32)
    first_sum = residual[None] + branch[None] * keeps[:, 0]
    normed_one, unit_one, scale_one = norm_fwd(first_sum, gain_one, shift_one)
    inner_in = normed_one.astype(jnp.bfloat16).reshape(2 * tokens, width)
    inner = matmul(inner_in, inner_weight) + inner_bias
    active = jax.nn.gelu(inner, approximate=False).astype(jnp.bfloat16)
    outer = (matmul(active, outer_weight) + outer_bias).reshape(2, tokens, width)
    second_sum = normed_one + outer * keeps[:, 1]
    normed_two, unit_two, scale_two = norm_fwd(second_sum, gain_two, shift_two)
    result = normed_two.astype(jnp.bfloat16).reshape(2, slots, row_len, width)
    sent_slots = slots * 4
    cls_rows = (
        jnp.einsum(
            "skl,vsld->vskd",
            cls_table.astype(jnp.bfloat16),
            result,
            preferred_element_type=jnp.float32,
        )
        .astype(jnp.bfloat16)
        .reshape(2 * sent_slots, width)
    )
    pre_pool = matmul(cls_rows, pool_weight) + pool_bias
    pooled = jnp.tanh(pre_pool)
    pool_scale = lax.rsqrt(jnp.sum(pooled * pooled, axis=-1, keepdims=True) + 1e-06)
    unit_low = (pooled * pool_scale).astype(jnp.bfloat16)
    anchors = unit_low[:sent_slots]
    partners = unit_low[sent_slots:]
    flags = held_slots.reshape(sent_slots)
    inv_temp = jnp.exp(-log_temp[0])
    anchors_all, partners_all, flags_all = gather_all(
        (anchors, partners, flags.astype(jnp.bfloat16))
    )
    column_ok = flags_all.astype(jnp.float32)
    sides = every_side if paired() else shared_sides
    loss, temp_grad, grad_anchor, grad_partner = sides(
        anchors, partners, anchors_all, partners_all, flags, column_ok, inv_temp
    )
    grad_unit = jnp.concatenate([grad_anchor, grad_partner], axis=0)
    grad_pooled = pool_scale * grad_unit - pooled * (
        pool_scale * pool_scale * pool_scale
    ) * jnp.sum(pooled * grad_unit, axis=-1, keepdims=True)
    grad_pre = (grad_pooled * (1.0 - pooled * pooled)).astype(jnp.bfloat16)
    grad_pool_bias = jnp.sum(grad_pre.astype(jnp.float32), axis=0)
    grad_pool_weight = across(cls_rows, grad_pre)
    grad_cls = against(grad_pre, pool_weight).reshape(2, slots, 4, width)
    grad_result = out_cotangent.astype(jnp.float32).reshape(2, tokens, width) * token_ok.reshape(
        1, tokens, 1
    ) + jnp.einsum("skl,vskd->vsld", cls_table, grad_cls, precision=precise).reshape(
        2, tokens, width
    )
    grad_second, grad_gain_two, grad_shift_two = norm_back(
        grad_result, unit_two, scale_two, gain_two
    )
    grad_outer = (grad_second * keeps[:, 1]).astype(jnp.bfloat16).reshape(2 * tokens, width)
    grad_outer_bias = jnp.sum(grad_outer.astype(jnp.float32), axis=0)
    grad_outer_weight = across(active, grad_outer)
    grad_active = against(grad_outer, outer_weight)
    slope = (
        0.5 * (1.0 + lax.erf(inner * inv_root_two))
        + inner * jnp.exp(-0.5 * inner * inner) * inv_root_tau
    )
    grad_inner = (grad_active * slope).astype(jnp.bfloat16)
    grad_inner_bias = jnp.sum(grad_inner.astype(jnp.float32), axis=0)
    grad_inner_weight = across(inner_in, grad_inner)
    grad_normed = against(grad_inner, inner_weight).reshape(2, tokens, width) + grad_second
    grad_first, grad_gain_one, grad_shift_one = norm_back(
        grad_normed, unit_one, scale_one, gain_one
    )
    grad_branch = jnp.sum(grad_first * keeps[:, 0], axis=0).astype(jnp.bfloat16)
    grad_out_bias = jnp.sum(grad_branch.astype(jnp.float32), axis=0)
    grad_out_weight = across(attended, grad_branch)
    grad_attended = against(grad_branch, out_weight).astype(jnp.bfloat16)
    scores_again = scores_of(heads_of(query_low), heads_of(keys_low))
    probs_again = jnp.exp(scores_again - log_total)
    probs_round = probs_again.astype(jnp.bfloat16)
    grad_probs = jnp.einsum(
        "slhd,smhd->shlm",
        heads_of(grad_attended),
        heads_of(values_low),
        preferred_element_type=jnp.float32,
    )
    grad_values = (
        jnp.einsum(
            "shlm,slhd->smhd",
            probs_round,
            heads_of(grad_attended),
            preferred_element_type=jnp.float32,
        )
        .reshape(tokens, width)
        .astype(jnp.bfloat16)
    )
    grad_scores = (
        probs_again * (grad_probs - jnp.sum(grad_probs * probs_again, axis=-1, keepdims=True))
    ).astype(jnp.bfloat16)
    grad_query = (
        (
            jnp.einsum(
                "shlm,smhd->slhd",
                grad_scores,
                heads_of(keys_low),
                preferred_element_type=jnp.float32,
            )
            * 0.125
        )
        .reshape(tokens, width)
        .astype(jnp.bfloat16)
    )
    grad_keys = (
        (
            jnp.einsum(
                "shlm,slhd->smhd",
                grad_scores,
                heads_of(query_low),
                preferred_element_type=jnp.float32,
            )
            * 0.125
        )
        .reshape(tokens, width)
        .astype(jnp.bfloat16)
    )
    grad_query_weight = across(flat_in, grad_query)
    grad_query_bias = jnp.sum(grad_query.astype(jnp.float32), axis=0)
    grad_key_weight = across(flat_in, grad_keys)
    grad_value_weight = across(flat_in, grad_values)
    grad_value_bias = jnp.sum(grad_values.astype(jnp.float32), axis=0)
    input_grad = (
        jnp.sum(grad_first, axis=0)
        + against(grad_query, query_weight)
        + against(grad_keys, key_weight)
        + against(grad_values, value_weight)
    )
    input_grad = input_grad.reshape(slots, row_len, width)
    (part_outer, part_pool, part_gain_two, part_shift_two, part_outer_bias, part_pool_bias) = (
        scatter_all(
            (
                grad_outer_weight,
                grad_pool_weight,
                grad_gain_two,
                grad_shift_two,
                grad_outer_bias,
                grad_pool_bias,
            )
        )
    )
    part_inner, part_inner_bias = scatter_all((grad_inner_weight, grad_inner_bias))
    (
        part_query,
        part_key,
        part_value,
        part_out,
        part_query_bias,
        part_value_bias,
        part_out_bias,
        part_gain_one,
        part_shift_one,
    ) = scatter_all(
        (
            grad_query_weight,
            grad_key_weight,
            grad_value_weight,
            grad_out_weight,
            grad_query_bias,
            grad_value_bias,
            grad_out_bias,
            grad_gain_one,
            grad_shift_one,
        )
    )
    return (
        loss.reshape(1),
        result,
        input_grad,
        part_query,
        part_query_bias,
        part_key,
        part_value,
        part_value_bias,
        part_out,
        part_out_bias,
        part_gain_one,
        part_shift_one,
        part_inner,
        part_inner_bias,
        part_outer,
        part_outer_bias,
        part_gain_two,
        part_shift_two,
        part_pool,
        part_pool_bias,
        temp_grad.reshape(1),
    )


def solution(mesh):
    in_specs = (
        P(("dp", "fsdp"), None, None),
        P(("dp", "fsdp")),
        P(("dp", "fsdp")),
        P(("dp", "fsdp"), None),
        P(None, None, ("dp", "fsdp"), None, None),
        P(None, ("dp", "fsdp"), None, None),
        P(("dp", "fsdp"), None),
        P(("dp", "fsdp")),
        P(("dp", "fsdp"), None),
        P(("dp", "fsdp"), None),
        P(("dp", "fsdp")),
        P(("dp", "fsdp"), None),
        P(("dp", "fsdp")),
        P(("dp", "fsdp")),
        P(("dp", "fsdp")),
        P(("dp", "fsdp"), None),
        P(("dp", "fsdp")),
        P(("dp", "fsdp"), None),
        P(("dp", "fsdp")),
        P(("dp", "fsdp")),
        P(("dp", "fsdp")),
        P(("dp", "fsdp"), None),
        P(("dp", "fsdp")),
        P(),
    )
    out_specs = (
        P(),
        P(None, ("dp", "fsdp"), None, None),
        P(("dp", "fsdp"), None, None),
        P(("dp", "fsdp"), None),
        P(("dp", "fsdp")),
        P(("dp", "fsdp"), None),
        P(("dp", "fsdp"), None),
        P(("dp", "fsdp")),
        P(("dp", "fsdp"), None),
        P(("dp", "fsdp")),
        P(("dp", "fsdp")),
        P(("dp", "fsdp")),
        P(("dp", "fsdp"), None),
        P(("dp", "fsdp")),
        P(("dp", "fsdp"), None),
        P(("dp", "fsdp")),
        P(("dp", "fsdp")),
        P(("dp", "fsdp")),
        P(("dp", "fsdp"), None),
        P(("dp", "fsdp")),
        P(),
    )
    return jax.shard_map(body, mesh=mesh, in_specs=in_specs, out_specs=out_specs, check_vma=False)
```

```python
import functools

import jax
import jax.numpy as jnp
from jax import lax
from jax.experimental import pallas as pl
from jax.experimental.pallas import tpu as pltpu
from jax.sharding import PartitionSpec as P

HEADS = 12
BOTH = ("z", "x", "c", "y")
LOW = jnp.bfloat16
FULL = jnp.float32

precise = lax.Precision.HIGHEST
keep_scale = 1.0 / 0.9
inv_root_two = 0.7071067811865476
inv_root_tau = 0.3989422804014327
eps = 1e-06


def matmul(left, right):
    return lax.dot_general(left, right, (((1,), (0,)), ((), ())), preferred_element_type=FULL)


def against(left, right):
    return lax.dot_general(left, right, (((1,), (1,)), ((), ())), preferred_element_type=FULL)


def across(left, right):
    return lax.dot_general(left, right, (((0,), (0,)), ((), ())), preferred_element_type=FULL)


def paired():
    return tuple(lax.axis_size(axis) for axis in BOTH) == (4, 2, 2, 2)


def place(z, x, c, y):
    return ((z * 2 + x) * 2 + c) * 2 + y


def pairs(move):
    every = [(z, x, c, y) for z in range(4) for x in range(2) for c in range(2) for y in range(2)]
    return [(place(*t), place(*move(*t))) for t in every]


def first_pairs():
    return pairs(lambda z, x, c, y: (z, 1 - x, c, y) if c == 0 else (z, x, c, 1 - y))


def second_pairs():
    return pairs(lambda z, x, c, y: (z, x, c, 1 - y) if c == 0 else (z, 1 - x, c, y))


def across_pairs():
    return pairs(lambda z, x, c, y: (z, 1 - x, c, 1 - y))


def core_pairs():
    return pairs(lambda z, x, c, y: (z, x, 1 - c, y))


def along_pairs(k):
    return pairs(lambda z, x, c, y: ((z + k) % 4, x, c, y))


def whereabouts():
    index = lax.axis_index(BOTH)
    return index // 8, index // 4 % 2, index // 2 % 2, index % 2


def send(block, route):
    return lax.ppermute(block, BOTH, route)


def together(*values):
    return lax.optimization_barrier(values)


def along_z(shard):
    return [send(shard, along_pairs(k)) for k in (1, 2, 3)]


def over_cores(own):
    return [send(block, core_pairs()) for block in own]


def where_from(here, core, p1, p2):
    first_x = core == 0
    on_x = jnp.where(first_x, p1, p2)
    on_y = jnp.where(first_x, p2, p1)
    return here[1] ^ on_x, here[3] ^ on_y


def order_kernel(parts, here_ref, *refs):
    blocks, outs = refs[:8], refs[8:]
    here = [here_ref[i] for i in range(4)]
    total = None
    for i in range(8):
        core = here[2] if i < 4 else 1 - here[2]
        x, y = where_from(here, core, i % 2, i // 2 % 2)
        for k in range(4):
            z = lax.rem(here[0] + 4 - k, 4)
            device = place(z, x, core, y)
            item = 0
            for count, out in zip(parts, outs):
                if count == 0:
                    value = blocks[i][k, item].astype(FULL)
                    total = value if total is None else total + value
                    item += 1
                for n in range(count):
                    out[n, device] = blocks[i][k, item]
                    item += 1
                for n in range(-count):
                    out[device, n] = blocks[i][k, item]
                    item += 1
    for count, out in zip(parts, outs):
        if count == 0:
            out[...] = total


def in_order(here, blocks, parts):
    items, rows, width = blocks[0].shape[1:]
    whole = pl.BlockSpec(memory_space=pltpu.VMEM)
    return call(
        functools.partial(order_kernel, parts),
        "order",
        0,
        128 * items * rows * width,
        out_shape=[
            shaped((rows, width), FULL)
            if count == 0
            else shaped((count, 32, rows, width) if count > 0 else (32, -count, rows, width), LOW)
            for count in parts
        ],
        grid_spec=pltpu.PrefetchScalarGridSpec(
            num_scalar_prefetch=1, grid=(), in_specs=[whole] * 8, out_specs=[whole] * len(parts)
        ),
    )(here, *blocks)


def add_low(left, right):
    return (left.astype(FULL) + right.astype(FULL)).astype(LOW)


def halves_of(kept, come):
    return add_low(kept[2:], come[2:]), add_low(kept[:2], come[:2])


def quarters_of(own, come):
    return add_low(own[1], come[1]), add_low(own[0], come[0])


def quarters(kept, come):
    return add_low(kept[0], come[0]), [add_low(kept[n], come[n]) for n in (1, 2, 3)]


def add_all(own, come):
    return sum([part.astype(FULL) for part in come], own.astype(FULL)).astype(LOW)


def over_z(column):
    z = lax.axis_index("z")
    own = lax.dynamic_index_in_dim(column, z, 0, keepdims=False)
    away = [lax.dynamic_index_in_dim(column, (z + k) % 4, 0, keepdims=False) for k in (1, 2, 3)]
    return [own] + [send(part, along_pairs(k)) for k, part in zip((1, 2, 3), away)]


def finish_kernel(inner, vectors, *refs):
    parts, outs = refs[1:5], refs[5:]
    here_ref = refs[0]
    rows, width = parts[0].shape[1:]

    def total(n):
        return sum(part[n].astype(FULL) for part in parts)

    for n in range(inner):
        outs[0][:, n * width : (n + 1) * width] = total(n)
    outs = outs[1:] if inner else outs
    plain = parts[0].shape[0] - inner - (1 if vectors else 0)
    for n in range(plain):
        outs[n][...] = total(inner + n)
    if vectors:
        index = place(here_ref[0], here_ref[1], here_ref[2], here_ref[3])
        value = total(inner + plain)
        piece = width // 32
        band = outs[plain + 1].shape[1]
        per_row = width // band
        outs[plain][...] = pltpu.roll(value, width - piece * index, 1)[: outs[plain].shape[0], :piece]
        at = lax.broadcasted_iota(jnp.int32, value.shape, 0) == 9 + index // per_row
        line = jnp.sum(jnp.where(at, value, 0.0), axis=0, keepdims=True)
        line = jnp.broadcast_to(line, (8, width))
        line = pltpu.roll(line, width - band * lax.rem(index, per_row), 1)
        outs[plain + 1][...] = line[0:1, :band]


def finish(here, parts, inner=0, vectors=0, band=0):
    items, rows, width = parts[0].shape
    plain = items - inner - (1 if vectors else 0)
    shapes = [(rows, inner * width)] if inner else []
    shapes += [(rows, width)] * plain
    shapes += [(vectors, width // 32), (1, band)] if vectors else []
    return call(
        functools.partial(finish_kernel, inner, vectors),
        "finish",
        0,
        12 * items * rows * width,
        grid_spec=pltpu.PrefetchScalarGridSpec(
            num_scalar_prefetch=1,
            grid=(1,),
            in_specs=[fixed(parts[0].shape)] * 4,
            out_specs=[fixed(shape) for shape in shapes],
        ),
        out_shape=[shaped(shape, FULL) for shape in shapes],
    )(here, *parts)


def layout(row_counts, buckets, lengths, row_len):
    slot_count = buckets.shape[0]
    live_rows = jnp.arange(slot_count, dtype=jnp.int32) < row_counts[0]
    sent_count = jnp.right_shift(jnp.int32(4), buckets)
    slot_ids = jnp.arange(4, dtype=jnp.int32)
    held_slots = (slot_ids[None, :] < sent_count[:, None]) & live_rows[:, None]
    sizes_used = jnp.where(held_slots, lengths, 0)
    finish = jnp.cumsum(sizes_used, axis=1, dtype=jnp.int32)
    starts = finish - sizes_used
    places = jnp.arange(row_len, dtype=jnp.int32)
    segment = jnp.sum((places[None, :, None] >= finish[:, None, :]).astype(jnp.int32), axis=2)
    return segment, starts, held_slots


def pick_table(starts, held_slots, row_len):
    rows = starts.shape[0]
    slot = jnp.arange(64, dtype=jnp.int32)
    view, row, k = slot // 32, slot % 32 // 4, slot % 4
    row = jnp.minimum(row, rows - 1)
    real = slot % 32 < rows * 4
    start = starts[row, k]
    held = held_slots[row, k] & real
    token = jnp.arange(2 * row_len, dtype=jnp.int32)
    hit = held[:, None] & (token[None, :] == (view * row_len + start)[:, None])
    here = jnp.arange(rows, dtype=jnp.int32)[:, None] == row[None, :]
    return (here[:, :, None] & hit[None]).astype(LOW)


def call(kernel, name, flops, moved, room=36, **kwargs):
    return pl.pallas_call(
        kernel,
        name=name,
        compiler_params=pltpu.CompilerParams(vmem_limit_bytes=room * 2**20),
        cost_estimate=pl.CostEstimate(flops=flops, transcendentals=0, bytes_accessed=moved),
        **kwargs,
    )


def scalars_spec():
    return pl.BlockSpec(memory_space=pltpu.SMEM)


def hand_on(here, mark):
    for n in range(4):
        mark[n] = here[n]


def fixed(shape):
    zeros = (0,) * len(shape)
    return pl.BlockSpec(shape, lambda *_: zeros)


def shaped(shape, kind):
    return jax.ShapeDtypeStruct(shape, kind)


def project_kernel(here, x, weight, bias, out, mark):
    hand_on(here, mark)
    out[...] = (matmul(x[...], weight[0]) + bias[0]).astype(LOW)


def project(here, flat, weights, biases):
    tokens, width = flat.shape
    return call(
        project_kernel,
        "project",
        6 * tokens * width * width,
        14 * width * width,
        grid=(3,),
        in_specs=[
            scalars_spec(),
            fixed((tokens, width)),
            pl.BlockSpec((1, width, width), lambda j: (j, 0, 0)),
            pl.BlockSpec((1, 1, width), lambda j: (j, 0, 0)),
        ],
        out_specs=[pl.BlockSpec((tokens, width), lambda j: (0, j)), scalars_spec()],
        out_shape=[shaped((tokens, 3 * width), LOW), shaped((4,), jnp.int32)],
    )(here, flat, weights, biases)


def halves(pair, even):
    zero = jnp.zeros_like(pair)
    return jnp.concatenate([jnp.where(even, pair, zero), jnp.where(even, zero, pair)], axis=0)


def attend_kernel(here, qkv, seg_row, seg_col, out, probs, mark):
    hand_on(here, mark)
    length, width = out.shape
    even = lax.broadcasted_iota(jnp.int32, (length, 128), 1) < 64
    same = seg_col[0] == seg_row[0]
    same = jnp.concatenate([same, same], axis=0)
    for p in range(width // 128):
        at = p * 128
        query = halves(qkv[:, at : at + 128], even)
        key = qkv[:, width + at : width + at + 128]
        value = qkv[:, 2 * width + at : 2 * width + at + 128]
        scores = jnp.where(same, against(query, key) * 0.125, -1e30)
        peak = jnp.max(scores, axis=-1, keepdims=True)
        lifted = jnp.exp(scores - peak)
        share = lifted * (1.0 / jnp.sum(lifted, axis=-1, keepdims=True))
        share = share.astype(LOW)
        probs[0, p] = share
        both = matmul(share, value)
        out[:, at : at + 128] = jnp.where(even, both[:length], both[length:]).astype(LOW)


def attend(here, qkv, segment):
    slots, length = segment.shape
    width = qkv.shape[1] // 3
    pairs_of = width // 128
    return call(
        attend_kernel,
        "attend",
        8 * slots * length * length * width,
        10 * slots * length * width,
        grid=(slots,),
        in_specs=[
            scalars_spec(),
            pl.BlockSpec((length, 3 * width), lambda r: (r, 0)),
            pl.BlockSpec((1, 1, length), lambda r: (r, 0, 0)),
            pl.BlockSpec((1, length, 1), lambda r: (r, 0, 0)),
        ],
        out_specs=[
            pl.BlockSpec((length, width), lambda r: (r, 0)),
            pl.BlockSpec((1, pairs_of, 2 * length, length), lambda r: (r, 0, 0, 0)),
            scalars_spec(),
        ],
        out_shape=[
            shaped((slots * length, width), LOW),
            shaped((slots, pairs_of, 2 * length, length), LOW),
            shaped((4,), jnp.int32),
        ],
    )(here, qkv, segment[:, None, :], segment[:, :, None])


def normal(hidden):
    centre = jnp.mean(hidden, axis=-1, keepdims=True)
    offset = hidden - centre
    spread_of = jnp.mean(offset * offset, axis=-1, keepdims=True)
    rscale = lax.rsqrt(spread_of + eps)
    return offset * rscale, rscale


def normal_back(grad_norm, normed, rscale):
    mean_grad = jnp.mean(grad_norm, axis=-1, keepdims=True)
    mean_cross = jnp.mean(grad_norm * normed, axis=-1, keepdims=True)
    return rscale * (grad_norm - mean_grad - normed * mean_cross)


def gelu_parts(inner):
    phi = 0.5 * (1.0 + lax.erf(inner * inv_root_two))
    return inner * phi, phi + inner * jnp.exp(-0.5 * inner * inner) * inv_root_tau


def inner_kernel(
    starts, held, att, x, keep, w_out, w_inner, small,
    n1, nh1, rs1, active, slope, picked, picked_att, picked_rs, picked_active, picked_slope,
    rows_one, rows_unit, rows_att, rows_scale, near, near_att,
):
    row = pl.program_id(0)
    length, width = att.shape
    branch = matmul(att[...], w_out[...]) + small[2:3]
    base = x[0].astype(FULL)
    keeps = keep[:, 0, 0].astype(FULL) * keep_scale
    first = jnp.concatenate([base + branch * keeps[0], base + branch * keeps[1]], axis=0)
    normed, rscale = normal(first)
    nh1[...] = normed.astype(LOW)
    rs1[...] = rscale
    rows_unit[...] = normed
    rows_scale[...] = jnp.broadcast_to(rscale, rows_scale.shape)
    rows_att[...] = att[...].astype(FULL)
    whole_in = normed * small[3:4] + small[4:5]
    rows_one[...] = whole_in
    inner_in = whole_in.astype(LOW)
    n1[...] = inner_in
    step = 256
    for j in range(w_inner.shape[0]):
        for at in range(0, width, step):
            inner = matmul(inner_in, w_inner[j, :, at : at + step])
            inner = inner + small[9 + j : 10 + j, at : at + step]
            value, grad = gelu_parts(inner)
            active[:, j * width + at : j * width + at + step] = value.astype(LOW)
            slope[:, j * width + at : j * width + at + step] = grad.astype(LOW)

    @pl.when(row == 0)
    def _():
        near[...] = jnp.zeros_like(near)
        near_att[...] = jnp.zeros_like(near_att)
        picked_rs[...] = jnp.zeros_like(picked_rs)

    for k in range(4):
        slot = 4 * row + k

        @pl.when(held[row, k] > 0)
        def _():
            start = starts[row, k]
            near_att[pl.ds(slot, 1)] = rows_att[pl.ds(start, 1)]
            for v in range(2):
                to = pl.ds(32 * v + slot, 1)
                near[0, to] = rows_one[pl.ds(length * v + start, 1)]
                near[1, to] = rows_unit[pl.ds(length * v + start, 1)]
                for n in range(2):
                    near[2 + n, to] = keep[v, n, 0, pl.ds(start, 1)].astype(FULL)
                picked_rs[to] = rows_scale[pl.ds(length * v + start, 1)]

    @pl.when(row == pl.num_programs(0) - 1)
    def _():
        picked[...] = near[...].astype(LOW)
        picked_att[...] = near_att[...].astype(LOW)
        begin = near[0].astype(LOW)
        for j in range(w_inner.shape[0]):
            inner = matmul(begin, w_inner[j]) + small[9 + j : 10 + j]
            value, grad = gelu_parts(inner)
            picked_active[:, j * width : (j + 1) * width] = value.astype(LOW)
            picked_slope[:, j * width : (j + 1) * width] = grad.astype(LOW)


def inner_forward(att, hidden, keep_masks, w_out, w_inner, small, starts, held_slots):
    slots, length, width = hidden.shape
    ff = w_inner.shape[0] * width
    two = 2 * length
    return call(
        inner_kernel,
        "inner_forward",
        2 * slots * two * width * ff,
        slots * two * ff * 5,
        grid_spec=pltpu.PrefetchScalarGridSpec(
            num_scalar_prefetch=2,
            grid=(slots,),
            in_specs=[
                pl.BlockSpec((length, width), lambda r, *_: (r, 0)),
                pl.BlockSpec((1, length, width), lambda r, *_: (r, 0, 0)),
                pl.BlockSpec((2, 2, 1, length, width), lambda r, *_: (0, 0, r, 0, 0)),
                fixed((width, width)),
                fixed(w_inner.shape),
                fixed(small.shape),
            ],
            out_specs=[
                pl.BlockSpec((two, width), lambda r, *_: (r, 0)),
                pl.BlockSpec((two, width), lambda r, *_: (r, 0)),
                pl.BlockSpec((two, 1), lambda r, *_: (r, 0)),
                pl.BlockSpec((two, ff), lambda r, *_: (r, 0)),
                pl.BlockSpec((two, ff), lambda r, *_: (r, 0)),
                fixed((4, 64, width)),
                fixed((32, width)),
                fixed((64, 128)),
                fixed((64, ff)),
                fixed((64, ff)),
            ],
            scratch_shapes=[
                pltpu.VMEM((two, width), FULL),
                pltpu.VMEM((two, width), FULL),
                pltpu.VMEM((length, width), FULL),
                pltpu.VMEM((two, 128), FULL),
                pltpu.VMEM((4, 64, width), FULL),
                pltpu.VMEM((32, width), FULL),
            ],
        ),
        out_shape=[
            shaped((slots * two, width), LOW),
            shaped((slots * two, width), LOW),
            shaped((slots * two, 1), FULL),
            shaped((slots * two, ff), LOW),
            shaped((slots * two, ff), LOW),
            shaped((4, 64, width), LOW),
            shaped((32, width), LOW),
            shaped((64, 128), FULL),
            shaped((64, ff), LOW),
            shaped((64, ff), LOW),
        ],
    )(starts, held_slots.astype(jnp.int32), att, hidden, keep_masks, w_out, w_inner, small)


def start_kernel(active, picked, w_outer, small, w_pool, flags, nh2, rs2, cls, pooled, unit):
    outer = matmul(active[...], w_outer[...]) + small[5:6]
    second = picked[0].astype(FULL) + outer * (picked[3].astype(FULL) * keep_scale)
    normed, rscale = normal(second)
    nh2[...] = normed.astype(LOW)
    rs2[...] = jnp.broadcast_to(rscale, rs2.shape)
    out = (normed * small[6:7] + small[7:8]).astype(LOW)
    cls[...] = out
    squashed = jnp.tanh(matmul(out, w_pool[...]) + small[8:9])
    pooled[...] = squashed
    scale = lax.rsqrt(jnp.sum(squashed * squashed, axis=-1, keepdims=True) + eps)
    ones = (squashed * scale).astype(LOW).astype(FULL)
    slot = lax.broadcasted_iota(jnp.int32, ones.shape, 0)
    unit[0] = jnp.where(slot == 28, flags[...], ones).astype(LOW)


def start_forward(active, picked, w_outer, small, w_pool, flags):
    ff, width = w_outer.shape
    return call(
        start_kernel,
        "start_forward",
        128 * width * ff,
        2 * width * ff,
        out_shape=[
            shaped((64, width), LOW),
            shaped((64, 128), FULL),
            shaped((64, width), LOW),
            shaped((64, width), FULL),
            shaped((1, 64, width), LOW),
        ],
    )(active, picked, w_outer, small, w_pool, flags)


def outer_kernel(here, active, n1, keep, w_outer, small, result, nh2, rs2, mark):
    hand_on(here, mark)
    length = n1.shape[0] // 2
    outer = matmul(active[...], w_outer[...]) + small[5:6]
    keeps = keep[:, 0, 0].astype(FULL) * keep_scale
    keeps = jnp.concatenate([keeps[0], keeps[1]], axis=0)
    second = n1[...].astype(FULL) + outer * keeps
    normed, rscale = normal(second)
    nh2[...] = normed.astype(LOW)
    rs2[...] = rscale
    out = (normed * small[6:7] + small[7:8]).astype(LOW)
    result[0, 0] = out[:length]
    result[1, 0] = out[length:]


def outer_forward(here, active, n1, keep_masks, w_outer, small):
    tokens, ff = active.shape
    width = n1.shape[1]
    slots = keep_masks.shape[2]
    length = keep_masks.shape[3]
    two = 2 * length
    return call(
        outer_kernel,
        "outer_forward",
        2 * tokens * width * ff,
        2 * tokens * ff,
        grid=(slots,),
        in_specs=[
            scalars_spec(),
            pl.BlockSpec((two, ff), lambda r: (r, 0)),
            pl.BlockSpec((two, width), lambda r: (r, 0)),
            pl.BlockSpec((2, 1, 1, length, width), lambda r: (0, 1, r, 0, 0)),
            fixed((ff, width)),
            fixed(small.shape),
        ],
        out_specs=[
            pl.BlockSpec((2, 1, length, width), lambda r: (0, r, 0, 0)),
            pl.BlockSpec((two, width), lambda r: (r, 0)),
            pl.BlockSpec((two, 1), lambda r: (r, 0)),
            scalars_spec(),
        ],
        out_shape=[
            shaped((2, slots, length, width), LOW),
            shaped((tokens, width), LOW),
            shaped((tokens, 1), FULL),
            shaped((4,), jnp.int32),
        ],
    )(here, active, n1, keep_masks, w_outer, small)


def split_matmul(left, right):
    upper = left.astype(LOW)
    lower = (left - upper.astype(FULL)).astype(LOW)
    return matmul(upper, right) + matmul(lower, right)


def pool_back(grad_unit, squashed):
    scale = lax.rsqrt(jnp.sum(squashed * squashed, axis=-1, keepdims=True) + eps)
    grad_pooled = scale * grad_unit - squashed * (scale * scale * scale) * jnp.sum(
        squashed * grad_unit, axis=-1, keepdims=True
    )
    return (grad_pooled * (1.0 - squashed * squashed)).astype(LOW)


def loss_kernel(here_ref, *refs):
    blocks = refs[:8]
    temp, pooled, scalars, grad_pre, anchors, partners, flat, sem = refs[8:]
    here = [here_ref[i] for i in range(4)]
    copies = []
    for i in range(8):
        core = here[2] if i < 4 else 1 - here[2]
        x, y = where_from(here, core, i % 2, i // 2 % 2)
        for k in range(4):
            z = lax.rem(here[0] + 4 - k, 4)
            row = pl.multiple_of(place(z, x, core, y) * 32, 32)
            source = blocks[i].at[k, 0]
            for half, target in ((0, anchors), (1, partners)):
                copies.append(
                    pltpu.make_async_copy(
                        source.at[pl.ds(32 * half, 32)], target.at[pl.ds(row, 32)], sem
                    )
                )
    for copy in copies:
        copy.start()
    for copy in copies:
        copy.wait()
    count = anchors.shape[0]
    groups = count // 32
    inv_temp = jnp.exp(-temp[...])
    all_anchors = anchors[...]
    all_partners = partners[...]
    for d in range(groups):
        flat[d : d + 1] = anchors[d * 32 + 28 : d * 32 + 29, :128].astype(FULL)
    marks = flat[...].astype(LOW)
    slot = lax.broadcasted_iota(jnp.int32, (128, count), 0)
    lane = lax.broadcasted_iota(jnp.int32, (128, count), 1)
    wide = matmul(marks, (slot == lane % 32).astype(LOW))
    group = lax.broadcasted_iota(jnp.int32, (groups, count), 0)
    lane = lax.broadcasted_iota(jnp.int32, (groups, count), 1)
    row_ok = jnp.sum(jnp.where(group == lane // 32, wide, 0.0), axis=0, keepdims=True)
    tall_row = lax.broadcasted_iota(jnp.int32, (count, groups), 0)
    tall_group = lax.broadcasted_iota(jnp.int32, (count, groups), 1)
    tall = matmul((tall_row // 32 == tall_group).astype(LOW), marks)
    tall_row = lax.broadcasted_iota(jnp.int32, (count, 128), 0)
    tall_lane = lax.broadcasted_iota(jnp.int32, (count, 128), 1)
    column_ok = jnp.sum(jnp.where(tall_row % 32 == tall_lane, tall, 0.0), axis=1, keepdims=True)
    total_held = jnp.sum(row_ok, axis=1, keepdims=True)
    weight = row_ok / total_held
    raw = against(all_partners, all_anchors) * inv_temp
    positive = []
    eye = lax.broadcasted_iota(jnp.int32, (128, 128), 0)
    eye = eye == lax.broadcasted_iota(jnp.int32, (128, 128), 1)
    for at in range(0, count, 128):
        block = raw[at : at + 128, at : at + 128]
        positive.append(jnp.sum(jnp.where(eye, block, 0.0), axis=0, keepdims=True))
    positive = jnp.concatenate(positive, axis=1)
    masked = jnp.where(column_ok > 0, raw, -1e30)
    peak = jnp.max(masked, axis=0, keepdims=True)
    lifted = jnp.exp(masked - peak)
    whole = jnp.sum(lifted, axis=0, keepdims=True)
    sim_total = peak + jnp.log(whole)
    crossed = jnp.sum(lifted * masked, axis=0, keepdims=True) / whole
    loss = jnp.sum(weight * (sim_total - positive), axis=1, keepdims=True)
    temp_grad = jnp.sum(weight * (positive - crossed), axis=1, keepdims=True)
    scalars[0:1] = jnp.broadcast_to(loss, (1, 128))
    scalars[1:2] = jnp.broadcast_to(temp_grad, (1, 128))
    mine = place(here[0], here[1], here[2], here[3])
    first = pl.multiple_of(mine * 32, 32)
    my_anchors = anchors[pl.ds(first, 32)]
    my_partners = partners[pl.ds(first, 32)]
    tall_lane = lax.broadcasted_iota(jnp.int32, (32, 128), 1)
    tall_row = lax.broadcasted_iota(jnp.int32, (32, 128), 0)
    my_flags = flat[pl.ds(mine, 1)]
    my_ok = jnp.sum(jnp.where(tall_lane == tall_row, my_flags, 0.0), axis=1, keepdims=True)
    my_weight = my_ok / total_held
    back = against(my_partners, all_anchors) * inv_temp
    back_shares = jnp.exp(jnp.where(my_ok > 0, back, -1e30) - sim_total) * weight
    grad_partner = inv_temp * (
        split_matmul(back_shares, all_anchors) - my_weight * my_anchors.astype(FULL)
    )
    mine_masked = jnp.where(row_ok > 0, against(my_anchors, all_partners) * inv_temp, -1e30)
    peak = jnp.max(mine_masked, axis=1, keepdims=True)
    lifted = jnp.exp(mine_masked - peak)
    my_shares = lifted * (my_weight / jnp.sum(lifted, axis=1, keepdims=True))
    grad_anchor = inv_temp * (
        split_matmul(my_shares, all_partners) - my_weight * my_partners.astype(FULL)
    )
    grad_unit = jnp.concatenate([grad_anchor, grad_partner], axis=0)
    grad_pre[...] = pool_back(grad_unit, pooled[...])


def contrast(here, blocks, log_temp, pooled):
    width = pooled.shape[1]
    count = 32 * 32
    whole = pl.BlockSpec(memory_space=pltpu.VMEM)
    return pl.pallas_call(
        loss_kernel,
        name="contrast",
        grid_spec=pltpu.PrefetchScalarGridSpec(
            num_scalar_prefetch=1,
            grid=(),
            in_specs=[pl.BlockSpec(memory_space=pl.ANY)] * 8 + [whole] * 2,
            out_specs=[whole] * 2,
            scratch_shapes=[
                pltpu.VMEM((count, width), LOW),
                pltpu.VMEM((count, width), LOW),
                pltpu.VMEM((32, 128), FULL),
                pltpu.SemaphoreType.DMA,
            ],
        ),
        out_shape=[shaped((2, 128), FULL), shaped((64, width), LOW)],
        compiler_params=pltpu.CompilerParams(vmem_limit_bytes=36 * 2**20),
        cost_estimate=pl.CostEstimate(
            flops=2 * count * count * width, transcendentals=0, bytes_accessed=4 * count * width
        ),
    )(here, *blocks, log_temp.reshape(1, 1), pooled)


def start_back(grad_out, nh2, rs2, picked, rs1, slope, w_outer, w_inner, w_out, small):
    normed = nh2.astype(FULL)
    second = normal_back(grad_out * small[6:7], normed, rs2)
    outer = (second * (picked[3].astype(FULL) * keep_scale)).astype(LOW)
    width = outer.shape[1]
    wide = w_inner.shape[0]
    inner = []
    grad_normed = second
    for j in range(wide):
        grad_active = against(outer, w_outer[j * width : (j + 1) * width])
        low = (grad_active * slope[:, j * width : (j + 1) * width].astype(FULL)).astype(LOW)
        inner.append(low)
        grad_normed = grad_normed + against(low, w_inner[j])
    unit_one = picked[1].astype(FULL)
    first = normal_back(grad_normed * small[3:4], unit_one, rs1)
    kept = first * (picked[2].astype(FULL) * keep_scale)
    branch = (kept[:32] + kept[32:]).astype(LOW)
    base = first[:32] + first[32:]
    att = against(branch, w_out).astype(LOW)

    def down(value):
        return jnp.sum(value.astype(FULL), axis=0, keepdims=True)

    sums = [
        down(branch),
        down(grad_normed * unit_one),
        down(grad_normed),
        down(outer),
        down(grad_out * normed),
        down(grad_out),
    ]
    return outer, inner, branch, base, att, sums, [down(low) for low in inner]


def start_back_kernel(
    grad_pre, w_pool, nh2, rs2, picked, rs1, slope, small, w_outer_hbm, w_inner_hbm, w_out_hbm,
    outer, inner, branch, base, att, sums, w_outer, w_inner, w_out, sems,
):
    copies = [
        pltpu.make_async_copy(source, target, sems.at[n])
        for n, (source, target) in enumerate(
            ((w_outer_hbm, w_outer), (w_inner_hbm, w_inner), (w_out_hbm, w_out))
        )
    ]
    for copy in copies:
        copy.start()
    grad_out = against(grad_pre[...], w_pool[...])
    for copy in copies:
        copy.wait()
    out = start_back(
        grad_out, nh2[...], rs2[:, :1], picked, rs1[:, :1], slope, w_outer, w_inner, w_out[...],
        small,
    )
    width = outer.shape[1]
    outer[...] = out[0]
    for j, low in enumerate(out[1]):
        inner[:, j * width : (j + 1) * width] = low
    branch[...] = out[2]
    base[...] = out[3]
    att[...] = out[4]
    sums[0:2] = jnp.zeros((2, width), FULL)
    for n, value in enumerate(out[5]):
        sums[2 + n : 3 + n] = value
    sums[8:9] = jnp.sum(grad_pre[...].astype(FULL), axis=0, keepdims=True)
    for j, value in enumerate(out[6]):
        sums[9 + j : 10 + j] = value
    sums[13:24] = jnp.zeros((11, width), FULL)


def start_backward(
    grad_pre, w_pool, nh2, rs2, picked, rs1, slope, small, w_outer, w_inner, w_out
):
    ff, width = w_outer.shape
    whole = pl.BlockSpec(memory_space=pltpu.VMEM)
    outside = pl.BlockSpec(memory_space=pl.ANY)
    return call(
        start_back_kernel,
        "start_backward",
        256 * width * ff,
        4 * width * ff,
        in_specs=[whole] * 8 + [outside] * 3,
        out_shape=[
            shaped((64, width), LOW),
            shaped((64, ff), LOW),
            shaped((32, width), LOW),
            shaped((32, width), FULL),
            shaped((32, width), LOW),
            shaped((24, width), FULL),
        ],
        scratch_shapes=[
            pltpu.VMEM(w_outer.shape, LOW),
            pltpu.VMEM(w_inner.shape, LOW),
            pltpu.VMEM(w_out.shape, LOW),
            pltpu.SemaphoreType.DMA((3,)),
        ],
    )(grad_pre, w_pool, nh2, rs2, picked, rs1, slope, small, w_outer, w_inner, w_out)


def outer_back_kernel(cot, ok, nh2, rs2, keep, small, grad_outer, second, sums):
    row = pl.program_id(0)
    flow = jnp.concatenate([cot[0, 0], cot[1, 0]], axis=0).astype(FULL)
    okay = jnp.concatenate([ok[0], ok[0]], axis=0)
    grad_out = flow * okay
    normed = nh2[...].astype(FULL)
    keeps = keep[:, 0, 0].astype(FULL) * keep_scale
    keeps = jnp.concatenate([keeps[0], keeps[1]], axis=0)
    grad_second = normal_back(grad_out * small[6:7], normed, rs2[...])
    low = (grad_second * keeps).astype(LOW)
    grad_outer[...] = low
    second[...] = grad_second.astype(LOW)

    @pl.when(row == 0)
    def _():
        sums[...] = jnp.zeros_like(sums)

    sums[0:1] += jnp.sum(low.astype(FULL), axis=0, keepdims=True)
    sums[1:2] += jnp.sum(grad_out * normed, axis=0, keepdims=True)
    sums[2:3] += jnp.sum(grad_out, axis=0, keepdims=True)


def outer_backward(cotangent, token_ok, nh2, rs2, keep_masks, small):
    _, slots, length, width = cotangent.shape
    two = 2 * length
    return call(
        outer_back_kernel,
        "outer_backward",
        64 * 2 * slots * two * width,
        18 * slots * two * width // 2,
        grid=(slots,),
        in_specs=[
            pl.BlockSpec((2, 1, length, width), lambda r: (0, r, 0, 0)),
            pl.BlockSpec((1, length, 1), lambda r: (r, 0, 0)),
            pl.BlockSpec((two, width), lambda r: (r, 0)),
            pl.BlockSpec((two, 1), lambda r: (r, 0)),
            pl.BlockSpec((2, 1, 1, length, width), lambda r: (0, 1, r, 0, 0)),
            fixed(small.shape),
        ],
        out_specs=[
            pl.BlockSpec((two, width), lambda r: (r, 0)),
            pl.BlockSpec((two, width), lambda r: (r, 0)),
            fixed((8, width)),
        ],
        out_shape=[
            shaped((slots * two, width), LOW),
            shaped((slots * two, width), LOW),
            shaped((8, width), FULL),
        ],
    )(cotangent, token_ok, nh2, rs2, keep_masks, small)


def inner_back_kernel(
    grad_outer, slope, second, nh1, rs1, keep, w_outer, w_inner, w_out, small,
    grad_inner, grad_branch, grad_att, base, sums, wide_sums,
):
    row = pl.program_id(0)
    length = grad_branch.shape[0]
    width = grad_branch.shape[1]
    step = 256

    @pl.when(row == 0)
    def _():
        sums[...] = jnp.zeros_like(sums)
        wide_sums[...] = jnp.zeros_like(wide_sums)

    low_outer = grad_outer[...]
    grad_normed = second[...].astype(FULL)
    for j in range(w_inner.shape[0]):
        for at in range(0, width, step):
            lane = j * width + at
            grad_active = against(low_outer, w_outer[lane : lane + step])
            low = (grad_active * slope[:, lane : lane + step].astype(FULL)).astype(LOW)
            grad_inner[:, lane : lane + step] = low
            wide_sums[:, lane : lane + step] += jnp.sum(low.astype(FULL), axis=0, keepdims=True)
        grad_normed = grad_normed + against(
            grad_inner[:, j * width : (j + 1) * width], w_inner[j]
        )
    normed = nh1[...].astype(FULL)
    grad_first = normal_back(grad_normed * small[3:4], normed, rs1[...])
    sums[0:1] += jnp.sum(grad_normed * normed, axis=0, keepdims=True)
    sums[1:2] += jnp.sum(grad_normed, axis=0, keepdims=True)
    keeps = keep[:, 0, 0].astype(FULL) * keep_scale
    branch = (grad_first[:length] * keeps[0] + grad_first[length:] * keeps[1]).astype(LOW)
    grad_branch[...] = branch
    sums[2:3] += jnp.sum(branch.astype(FULL), axis=0, keepdims=True)
    base[...] = grad_first[:length] + grad_first[length:]
    grad_att[...] = against(branch, w_out[...]).astype(LOW)


def inner_backward(grad_outer, slope, second, nh1, rs1, keep_masks, w_outer, w_inner, w_out, small):
    tokens, ff = slope.shape
    slots, length, width = keep_masks.shape[2:]
    two = 2 * length
    return call(
        inner_back_kernel,
        "inner_backward",
        4 * tokens * width * ff,
        5 * tokens * ff,
        grid=(slots,),
        in_specs=[
            pl.BlockSpec((two, width), lambda r: (r, 0)),
            pl.BlockSpec((two, ff), lambda r: (r, 0)),
            pl.BlockSpec((two, width), lambda r: (r, 0)),
            pl.BlockSpec((two, width), lambda r: (r, 0)),
            pl.BlockSpec((two, 1), lambda r: (r, 0)),
            pl.BlockSpec((2, 1, 1, length, width), lambda r: (0, 0, r, 0, 0)),
            fixed(w_outer.shape),
            fixed(w_inner.shape),
            fixed(w_out.shape),
            fixed(small.shape),
        ],
        out_specs=[
            pl.BlockSpec((two, ff), lambda r: (r, 0)),
            pl.BlockSpec((length, width), lambda r: (r, 0)),
            pl.BlockSpec((length, width), lambda r: (r, 0)),
            pl.BlockSpec((length, width), lambda r: (r, 0)),
            fixed((8, width)),
            fixed((1, ff)),
        ],
        out_shape=[
            shaped((tokens, ff), LOW),
            shaped((slots * length, width), LOW),
            shaped((slots * length, width), LOW),
            shaped((slots * length, width), FULL),
            shaped((8, width), FULL),
            shaped((1, ff), FULL),
        ],
    )(grad_outer, slope, second, nh1, rs1, keep_masks, w_outer, w_inner, w_out, small)


def attend_back_kernel(grad_att, start_att, table, qkv, probs, grad_qkv, sums):
    row = pl.program_id(0)
    length, width = grad_att.shape
    even = lax.broadcasted_iota(jnp.int32, (length, 128), 1) < 64

    @pl.when(row == 0)
    def _():
        sums[...] = jnp.zeros_like(sums)

    placed = across(table[0, :32, :length], start_att[...])
    whole_att = (grad_att[...].astype(FULL) + placed).astype(LOW)
    for p in range(width // 128):
        at = p * 128
        query = halves(qkv[:, at : at + 128], even)
        key = halves(qkv[:, width + at : width + at + 128], even)
        value = qkv[:, 2 * width + at : 2 * width + at + 128]
        flow = halves(whole_att[:, at : at + 128], even)
        share = probs[0, p]
        share_f = share.astype(FULL)
        grad_share = against(flow, value)
        inside = jnp.sum(grad_share * share_f, axis=-1, keepdims=True)
        grad_scores = (share_f * (grad_share - inside)).astype(LOW)
        grad_value = across(share, flow).astype(LOW)
        side = jnp.concatenate([grad_scores[:length], grad_scores[length:]], axis=1)
        grad_query = (matmul(side, key) * 0.125).astype(LOW)
        grad_key = (across(grad_scores, query) * 0.125).astype(LOW)
        grad_qkv[:, at : at + 128] = grad_query
        grad_qkv[:, width + at : width + at + 128] = grad_key
        grad_qkv[:, 2 * width + at : 2 * width + at + 128] = grad_value
        sums[0:1, at : at + 128] += jnp.sum(grad_query.astype(FULL), axis=0, keepdims=True)
        sums[1:2, at : at + 128] += jnp.sum(grad_value.astype(FULL), axis=0, keepdims=True)


def attend_backward(grad_att, start_att, table, qkv, probs):
    slots, pairs_of, _, length = probs.shape
    width = grad_att.shape[1]
    return call(
        attend_back_kernel,
        "attend_backward",
        16 * slots * length * length * width,
        18 * slots * length * width,
        grid=(slots,),
        in_specs=[
            pl.BlockSpec((length, width), lambda r: (r, 0)),
            fixed((32, width)),
            pl.BlockSpec((1, 64, 2 * length), lambda r: (r, 0, 0)),
            pl.BlockSpec((length, 3 * width), lambda r: (r, 0)),
            pl.BlockSpec((1, pairs_of, 2 * length, length), lambda r: (r, 0, 0, 0)),
        ],
        out_specs=[
            pl.BlockSpec((length, 3 * width), lambda r: (r, 0)),
            fixed((8, width)),
        ],
        out_shape=[shaped((slots * length, 3 * width), LOW), shaped((8, width), FULL)],
    )(grad_att, start_att, table, qkv, probs)


def input_kernel(base, start_base, table, grad_qkv, weights, out):
    width = weights.shape[1]
    total = base[...] + lax.dot_general(
        table[...].astype(FULL),
        start_base[...],
        (((0,), (0,)), ((), ())),
        precision=precise,
        preferred_element_type=FULL,
    )
    for j in range(3):
        total = total + against(grad_qkv[:, j * width : (j + 1) * width], weights[j])
    out[...] = total


def input_gradient(base, start_base, table, grad_qkv, weights):
    tokens, width = base.shape
    rows, _, two = table.shape
    table = table[:, :32, : two // 2].transpose(1, 0, 2).reshape(32, tokens)
    table = jnp.pad(table, ((0, 0), (0, -tokens % 256)))
    step = 256
    return call(
        input_kernel,
        "input_gradient",
        6 * tokens * width * width,
        14 * tokens * width,
        grid=(pl.cdiv(tokens, step),),
        in_specs=[
            pl.BlockSpec((step, width), lambda r: (r, 0)),
            fixed((32, width)),
            pl.BlockSpec((32, step), lambda r: (0, r)),
            pl.BlockSpec((step, 3 * width), lambda r: (r, 0)),
            fixed(weights.shape),
        ],
        out_specs=pl.BlockSpec((step, width), lambda r: (r, 0)),
        out_shape=shaped((tokens, width), FULL),
    )(base, start_base, table, grad_qkv, weights)


def store_part(here, value, z, x, c, y, kept, away, at):
    on_x = here[1] ^ x
    on_y = here[3] ^ y
    index = 2 * on_y + on_x if c == 0 else 2 * on_x + on_y

    @pl.when(here[2] == c)
    def _():
        kept[(index,) + at] = value

    @pl.when(here[2] != c)
    def _():
        away[(index,) + at] = value


def outer_weight_kernel(here_ref, active, grad_outer, start_active, start_outer, kept, away):
    here = [here_ref[i] for i in range(4)]
    rows = kept.shape[3]
    whole = across(active[...], grad_outer[...]) + across(start_active[...], start_outer[...])
    whole = whole.astype(LOW)
    for n in range(8):
        x, c, y = n // 4, n // 2 % 2, n % 2
        store_part(here, whole[n * rows : (n + 1) * rows], 0, x, c, y, kept, away, (0, 0))


def outer_weight(here, active, grad_outer, start_active, start_outer):
    tokens, ff = active.shape
    width = grad_outer.shape[1]
    part = ff // 4
    spec = pl.BlockSpec((4, 1, 1, ff // 32, width), lambda z, _: (0, z, 0, 0, 0))
    shape = shaped((4, 4, 1, ff // 32, width), LOW)
    return call(
        outer_weight_kernel,
        "outer_weight",
        2 * tokens * ff * width,
        2 * tokens * ff,
        grid_spec=pltpu.PrefetchScalarGridSpec(
            num_scalar_prefetch=1,
            grid=(4,),
            in_specs=[
                pl.BlockSpec((tokens, part), lambda z, _: (0, z)),
                pl.BlockSpec((tokens, width), lambda z, _: (0, 0)),
                pl.BlockSpec((64, part), lambda z, _: (0, z)),
                pl.BlockSpec((64, width), lambda z, _: (0, 0)),
            ],
            out_specs=[spec, spec],
        ),
        out_shape=[shape, shape],
    )(here, active, grad_outer, start_active, start_outer)


def store_parts(here, whole, kept, away):
    rows = kept.shape[3]
    for n in range(32):
        z, x, c, y = n // 8, n // 4 % 2, n // 2 % 2, n % 2
        store_part(here, whole[n * rows : (n + 1) * rows], z, x, c, y, kept, away, (z, 0))


def inner_weight_kernel(here_ref, n1, grad_inner, start_n1, start_inner, *refs):
    kept, away = refs[-2:]
    here = [here_ref[i] for i in range(4)]
    step = pl.program_id(0)

    @pl.when(step < 2)
    def _():
        whole = across(n1[...], grad_inner[...]) + across(start_n1[0], start_inner[...])
        store_parts(here, whole.astype(LOW), kept, away)

    if len(refs) > 2:
        att, branch, start_att, start_branch, cls, grad_pre = refs[:6]

        @pl.when(step == 2)
        def _():
            whole = across(att[...], branch[...]) + across(start_att[...], start_branch[...])
            store_parts(here, whole.astype(LOW), kept, away)

        @pl.when(step == 3)
        def _():
            store_parts(here, across(cls[...], grad_pre[...]).astype(LOW), kept, away)


def inner_weight(here, begin, n1, grad_inner, picked, start_inner, *others):
    tokens, _ = grad_inner.shape
    width = n1.shape[1]
    count = 4 if others else 2
    spec = pl.BlockSpec((4, 4, 1, width // 32, width), lambda j, _: (0, 0, j, 0, 0))
    shape = shaped((4, 4, count, width // 32, width), LOW)
    return call(
        inner_weight_kernel,
        "inner_weight",
        4 * tokens * width * width,
        8 * tokens * width,
        grid_spec=pltpu.PrefetchScalarGridSpec(
            num_scalar_prefetch=1,
            grid=(count,),
            in_specs=[
                pl.BlockSpec((tokens, width), lambda j, _: (0, 0)),
                pl.BlockSpec((tokens, width), lambda j, _: (0, begin + jnp.minimum(j, 1))),
                pl.BlockSpec((1, 64, width), lambda j, _: (0, 0, 0)),
                pl.BlockSpec((64, width), lambda j, _: (0, begin + jnp.minimum(j, 1))),
            ]
            + [pl.BlockSpec(other.shape, lambda j, _: (0, 0)) for other in others],
            out_specs=[spec, spec],
        ),
        out_shape=[shape, shape],
    )(here, n1, grad_inner, picked, start_inner, *others)


def attend_weight_kernel(
    here_ref, x, grad_qkv, start_sums, sums_qv, sums_one, sums_two, wide_sums, kept, away
):
    here = [here_ref[i] for i in range(4)]
    step = pl.program_id(0)

    @pl.when(step < 3)
    def _():
        store_parts(here, across(x[...], grad_qkv[...]).astype(LOW), kept, away)

    @pl.when(step == 3)
    def _():
        width = x.shape[1]
        value = start_sums[...] + jnp.concatenate(
            [sums_qv[0:2], sums_one[2:3], sums_one[0:2], sums_two[0:3]]
            + [jnp.zeros((1, width), FULL)]
            + [wide_sums[:, j * width : (j + 1) * width] for j in range(4)]
            + [jnp.zeros((11, width), FULL)],
            axis=0,
        )
        value = value.astype(LOW)
        for index in range(4):
            for z in range(4):
                kept[index, z, 0] = value
                away[index, z, 0] = value


def attend_weight(here, x, grad_qkv, sums):
    tokens, width = x.shape
    spec = pl.BlockSpec((4, 4, 1, width // 32, width), lambda j, _: (0, 0, j, 0, 0))
    shape = shaped((4, 4, 4, width // 32, width), LOW)
    return call(
        attend_weight_kernel,
        "attend_weight",
        6 * tokens * width * width,
        8 * tokens * width,
        grid_spec=pltpu.PrefetchScalarGridSpec(
            num_scalar_prefetch=1,
            grid=(4,),
            in_specs=[
                pl.BlockSpec((tokens, width), lambda j, _: (0, 0)),
                pl.BlockSpec((tokens, width), lambda j, _: (0, jnp.minimum(j, 2))),
            ]
            + [fixed(value.shape) for value in sums],
            out_specs=[spec, spec],
        ),
        out_shape=[shape, shape],
    )(here, x, grad_qkv, *sums)


def gathered(shard):
    return lax.all_gather(shard, BOTH, axis=0, tiled=True)


def scattered(whole):
    return lax.psum_scatter(whole, BOTH, scatter_dimension=0, tiled=True)


def shared_contrast(unit, flags, log_temp, pooled):
    anchors, partners = unit[:28], unit[32:60]
    inv_temp = jnp.exp(-log_temp[0])
    anchors_all, partners_all = gathered(anchors), gathered(partners)
    column_ok = gathered(flags.astype(LOW)).astype(FULL)
    held_total = jnp.sum(column_ok)
    logits = against(anchors, partners_all) * inv_temp
    logits = jnp.where(column_ok[None, :] > 0, logits, -1e30)
    sim_peak = jnp.max(logits, axis=-1, keepdims=True)
    sim_total = sim_peak + jnp.log(jnp.sum(jnp.exp(logits - sim_peak), axis=-1, keepdims=True))
    anchors_f = anchors.astype(FULL)
    partners_f = partners.astype(FULL)
    positive = jnp.sum(anchors_f * partners_f, axis=-1) * inv_temp
    row_weight = flags / held_total
    loss_part = jnp.sum(row_weight * (sim_total[:, 0] - positive))
    shares = jnp.exp(logits - sim_total) * row_weight[:, None]
    temp_part = jnp.sum(row_weight * positive) - jnp.sum(
        shares * jnp.where(column_ok[None, :] > 0, logits, 0.0)
    )
    grad_anchor = inv_temp * (
        jnp.dot(shares, partners_all.astype(FULL), precision=precise)
        - row_weight[:, None] * partners_f
    )
    totals_all = gathered(sim_total[:, 0])
    back = against(partners, anchors_all) * inv_temp
    back = jnp.where(flags[:, None] > 0, back, -1e30)
    back_shares = jnp.exp(back - totals_all[None, :]) * (column_ok / held_total)[None, :]
    grad_partner = inv_temp * (
        jnp.dot(back_shares, anchors_all.astype(FULL), precision=precise)
        - row_weight[:, None] * anchors_f
    )
    loss, temp_grad = lax.psum((loss_part, temp_part), BOTH)
    pad = ((0, 4), (0, 0))
    grad_unit = jnp.concatenate([jnp.pad(grad_anchor, pad), jnp.pad(grad_partner, pad)])
    return loss.reshape(1), temp_grad.reshape(1), pool_back(grad_unit, pooled)


def pack_kernel(here_ref, *refs):
    vectors, b_inner = refs[:9], refs[9]
    w_query, w_key, w_value, w_out, w_inner = refs[10:15]
    one, two, narrow, broad = refs[15:]
    index = place(here_ref[0], here_ref[1], here_ref[2], here_ref[3])
    rows, width = w_query.shape
    band = b_inner.shape[1]
    per_row = width // band
    one[0] = w_query[...]
    one[1] = w_key[...]
    one[2] = w_value[...]
    for j in range(w_inner.shape[1] // width):
        two[j] = w_inner[:, j * width : (j + 1) * width]
    two[4] = w_out[...]
    narrow[...] = jnp.zeros_like(narrow)
    broad[...] = jnp.zeros_like(broad)
    for f, vector in enumerate(vectors):
        narrow[f : f + 1, :rows] = vector[...].astype(FULL)
    broad[0:1, :band] = b_inner[...].astype(FULL)
    placed = pltpu.roll(narrow[...], rows * index, 1)
    line = pltpu.roll(broad[...], band * lax.rem(index, per_row), 1)[0:1]
    at = lax.broadcasted_iota(jnp.int32, placed.shape, 0) == 9 + index // per_row
    placed = jnp.where(at, line, placed)
    one[3] = placed.astype(LOW)


def pack(here, vectors, b_inner, weights):
    w_query, w_key, w_value, w_out, w_inner = weights
    rows, width = w_query.shape
    return call(
        pack_kernel,
        "pack",
        0,
        40 * rows * width,
        room=60,
        grid_spec=pltpu.PrefetchScalarGridSpec(
            num_scalar_prefetch=1,
            grid=(1,),
            in_specs=[fixed((1, rows))] * 9
            + [fixed((1, b_inner.shape[0]))]
            + [fixed(weight.shape) for weight in weights],
            out_specs=[fixed((4, rows, width)), fixed((w_inner.shape[1] // width + 1, rows, width))],
            scratch_shapes=[pltpu.VMEM((24, width), FULL), pltpu.VMEM((8, width), FULL)],
        ),
        out_shape=[
            shaped((4, rows, width), LOW),
            shaped((w_inner.shape[1] // width + 1, rows, width), LOW),
        ],
    )(
        here,
        *[vector[None] for vector in vectors],
        b_inner[None],
        *weights,
    )


def small_sums(start_sums, sums_qv, sums_one, sums_two, wide_sums):
    width = start_sums.shape[1]
    wide = wide_sums.shape[1] // width
    return start_sums + jnp.concatenate(
        [
            sums_qv[0:2],
            sums_one[2:3],
            sums_one[0:2],
            sums_two[0:3],
            jnp.zeros((1, width), FULL),
            wide_sums.reshape(wide, width),
            jnp.zeros((24 - 9 - wide, width), FULL),
        ]
    )


def paired_body(
    hidden_in, row_counts, buckets, lengths, keep_masks, out_cotangent, vectors, b_inner, weights,
    log_temp,
):
    w_query, w_key, w_value, w_attn_out, w_inner, w_outer, w_pool = weights
    slots, length, width = hidden_in.shape
    tokens = slots * length
    ff = w_inner.shape[1]
    wide = ff // width
    index = lax.axis_index(BOTH)
    here = jnp.stack(whereabouts()).astype(jnp.int32)
    flat = hidden_in.reshape(tokens, width)
    first, second = first_pairs(), second_pairs()

    pack_one, pack_two = pack(here, vectors, b_inner, (w_query, w_key, w_value, w_attn_out, w_inner))
    pack_three = jnp.concatenate([w_outer.reshape(wide, -1, width), w_pool[None]])
    come = along_z(pack_one)
    pack_one, pack_two, come = together(pack_one, pack_two, come)

    one = [jnp.stack([pack_one] + come)]
    come = [send(one[0], first), send(one[0], second)]
    come_two = along_z(pack_two)
    one, come, pack_two, come_two = together(one, come, pack_two, come_two)

    one += come
    come = send(one[1], second)
    segment, starts, held_slots = layout(row_counts, buckets, lengths, length)
    token_ok = (segment < 4).astype(FULL)[:, :, None]
    table = pick_table(starts, held_slots, length)
    flags = held_slots.astype(FULL).reshape(slots * 4)
    flag_row = jnp.pad(flags, (0, width - slots * 4))[None]
    two = [jnp.stack([pack_two] + come_two)]
    one, come, two, segment, token_ok, table, flag_row = together(
        one, come, two, segment, token_ok, table, flag_row
    )

    one.append(come)
    one_other = over_cores(one)
    come = [send(two[0], first), send(two[0], second)]
    one, one_other, pack_three = together(one, one_other, pack_three)

    come_three = along_z(pack_three)
    qkv_weights, small = in_order(here, one + one_other, (3, 0))
    qkv_weights = qkv_weights.reshape(3, width, width)
    biases = jnp.stack([small[0], jnp.zeros_like(small[0]), small[1]])[:, None]
    qkv, here = project(here, flat, qkv_weights, biases)
    two, come, pack_three, come_three, here = together(two, come, pack_three, come_three, here)

    two += come
    come = send(two[1], second)
    att, probs, here = attend(here, qkv, segment)
    three = [jnp.stack([pack_three] + come_three)]
    two, come, three, here = together(two, come, three, here)

    two.append(come)
    two_other = over_cores(two)
    come = [send(three[0], first), send(three[0], second), send(three[0], across_pairs())]
    two, two_other, here = together(two, two_other, here)

    inner_weights, out_weight = in_order(here, two + two_other, (wide, 1))
    inner_weights = inner_weights.reshape(wide, width, width)
    out_weight = out_weight.reshape(width, width)
    n1, nh1, rs1, active, slope, picked, picked_att, picked_rs, start_active, start_slope = (
        inner_forward(
            att, hidden_in, keep_masks, out_weight, inner_weights, small, starts, held_slots
        )
    )
    three, come, start_active = together(three, come, start_active)

    three += come
    outer_weights, pool_weight = in_order(here, three + over_cores(three), (-wide, 1))
    outer_weights = outer_weights.reshape(ff, width)
    pool_weight = pool_weight.reshape(width, width)
    start_nh2, start_rs2, cls, pooled, unit = start_forward(
        start_active, picked, outer_weights, small, pool_weight, flag_row
    )
    unit, here = together(unit, here)

    come = along_z(unit)
    result, nh2, rs2, here = outer_forward(here, active, n1, keep_masks, outer_weights, small)
    come, here, token = together(come, here, small)

    own = [jnp.stack([unit] + come)]
    come = [send(own[0], first), send(own[0], second)]
    grad_outer, second_flow, sums_two = outer_backward(
        out_cotangent, token_ok, nh2, rs2, keep_masks, token
    )
    own, come, sums_two = together(own, come, sums_two)

    own += come
    own.append(send(own[1], second))
    scalars, grad_pre = contrast(here, own + over_cores(own), log_temp, pooled)
    loss, temp_grad = scalars[0, :1], scalars[1, :1]
    start_outer, start_inner, start_branch, start_base, start_att, start_sums = start_backward(
        grad_pre, pool_weight, start_nh2, start_rs2, picked, picked_rs, start_slope, small,
        outer_weights, inner_weights, out_weight,
    )

    outer_kept, outer_away = outer_weight(here, active, grad_outer, start_active, start_outer)
    outer_kept, outer_away, token = together(outer_kept, outer_away, small)

    come = send(outer_away, core_pairs())
    grad_inner, grad_branch, grad_att, base, sums_one, wide_sums = inner_backward(
        grad_outer, slope, second_flow, nh1, rs1, keep_masks, outer_weights, inner_weights,
        out_weight, token,
    )
    come, outer_kept, sums_one, start_att = together(come, outer_kept, sums_one, start_att)

    outer_go, outer_own = halves_of(outer_kept, come)
    come = send(outer_go, second)
    grad_qkv, sums_qv = attend_backward(grad_att, start_att, table, qkv, probs)
    outer_own, come, sums_qv = together(outer_own, come, sums_qv)

    outer_go, outer_own = quarters_of(outer_own, come)
    come_outer = send(outer_go, first)
    attend_kept, attend_away = attend_weight(
        here, flat, grad_qkv, (start_sums, sums_qv, sums_one, sums_two, wide_sums)
    )
    outer_own, come_outer, attend_kept, attend_away = together(
        outer_own, come_outer, attend_kept, attend_away
    )

    come = send(attend_away, core_pairs())
    outer_column = add_low(outer_own, come_outer)
    come, attend_kept, outer_column = together(come, attend_kept, outer_column)

    attend_go, attend_own = halves_of(attend_kept, come)
    come = send(attend_go, second)
    attend_go, attend_own, token = together(attend_go, attend_own, here)
    a_kept, a_away = inner_weight(
        token, 0, n1, grad_inner, picked, start_inner, att, grad_branch, picked_att, start_branch,
        cls, grad_pre,
    )
    attend_own, come, a_kept, a_away = together(attend_own, come, a_kept, a_away)

    come_a = send(a_away, core_pairs())
    attend_go, attend_own = quarters_of(attend_own, come)
    come = send(attend_go, first)
    a_kept, come_a, attend_own = together(a_kept, come_a, attend_own)

    a_go, a_own = halves_of(a_kept, come_a)
    come_a = send(a_go, second)
    a_own, token = together(a_own, here)
    b_kept, b_away = inner_weight(token, 2, n1, grad_inner, picked, start_inner)
    come, attend_own, come_a, a_own, b_kept, b_away, outer_column = together(
        come, attend_own, come_a, a_own, b_kept, b_away, outer_column
    )

    come_b = send(b_away, core_pairs())
    a_go, a_own = quarters_of(a_own, come_a)
    come_a = send(a_go, first)
    parts_outer = over_z(outer_column)
    b_kept, come_b, start_base, a_own = together(b_kept, come_b, start_base, a_own)

    b_own, b_go = quarters(b_kept, come_b)
    come_b = [send(part, route) for part, route in zip(b_go, (first, second, across_pairs()))]
    parts_attend = over_z(add_low(attend_own, come))
    input_grad = input_gradient(base, start_base, table, grad_qkv, qkv_weights)
    come_a, a_own, b_own, come_b, parts_attend, parts_outer, token = together(
        come_a, a_own, b_own, come_b, parts_attend, parts_outer, here
    )

    parts_a = over_z(add_low(a_own, come_a))
    b_column = add_all(b_own, come_b)
    (outer_part,) = finish(token, parts_outer)
    query_part, key_part, value_part, own_small, inner_bias_part = finish(
        token, parts_attend, vectors=9, band=b_inner.shape[0]
    )
    parts_b = over_z(b_column)
    inner_a, out_part, pool_part = finish(here, parts_a, inner=2)
    (inner_b,) = finish(here, parts_b, inner=2)
    inner_part = jnp.concatenate([inner_a, inner_b], axis=1)
    input_grad = input_grad.reshape(hidden_in.shape)
    inner_bias_part = inner_bias_part[0]
    parts = [query_part, key_part, value_part, out_part]
    small_parts = [own_small[i] for i in range(9)]
    return (
        loss,
        result,
        input_grad,
        parts[0],
        small_parts[0],
        parts[1],
        parts[2],
        small_parts[1],
        parts[3],
        small_parts[2],
        small_parts[3],
        small_parts[4],
        inner_part,
        inner_bias_part,
        outer_part,
        small_parts[5],
        small_parts[6],
        small_parts[7],
        pool_part,
        small_parts[8],
        temp_grad,
    )


def body(
    hidden_in,
    row_counts,
    buckets,
    lengths,
    keep_masks,
    out_cotangent,
    w_query,
    b_query,
    w_key,
    w_value,
    b_value,
    w_attn_out,
    b_attn_out,
    norm1_gain,
    norm1_bias,
    w_inner,
    b_inner,
    w_outer,
    b_outer,
    norm2_gain,
    norm2_bias,
    w_pool,
    b_pool,
    log_temp,
):
    slots, length, width = hidden_in.shape
    tokens = slots * length
    ff = w_inner.shape[1]
    wide = ff // width
    index = lax.axis_index(BOTH)
    here = jnp.stack(whereabouts()).astype(jnp.int32)
    vectors = (
        b_query,
        b_value,
        b_attn_out,
        norm1_gain,
        norm1_bias,
        b_outer,
        norm2_gain,
        norm2_bias,
        b_pool,
    )
    if paired():
        return paired_body(
            hidden_in, row_counts, buckets, lengths, keep_masks, out_cotangent, vectors, b_inner,
            (w_query, w_key, w_value, w_attn_out, w_inner, w_outer, w_pool), log_temp,
        )
    qkv_weights = jnp.stack([gathered(w) for w in (w_query, w_key, w_value)])
    out_weight = gathered(w_attn_out)
    rows = [gathered(v)[None] for v in vectors]
    rows.append(gathered(b_inner).reshape(wide, width))
    rows.append(jnp.zeros((24 - 9 - wide, width), LOW))
    small = jnp.concatenate(rows).astype(FULL)
    inner_weights = gathered(w_inner).reshape(width, wide, width).transpose(1, 0, 2)
    outer_weights = gathered(w_outer)
    pool_weight = gathered(w_pool)

    segment, starts, held_slots = layout(row_counts, buckets, lengths, length)
    token_ok = (segment < 4).astype(FULL)[:, :, None]
    table = pick_table(starts, held_slots, length)
    flags = held_slots.astype(FULL).reshape(slots * 4)
    flag_row = jnp.pad(flags, (0, width - slots * 4))[None]

    flat = hidden_in.reshape(tokens, width)
    biases = jnp.stack([small[0], jnp.zeros_like(small[0]), small[1]])[:, None]
    qkv, _ = project(here, flat, qkv_weights, biases)
    att, probs, _ = attend(here, qkv, segment)
    n1, nh1, rs1, active, slope, picked, picked_att, picked_rs, start_active, start_slope = (
        inner_forward(
            att, hidden_in, keep_masks, out_weight, inner_weights, small, starts, held_slots
        )
    )
    start_nh2, start_rs2, cls, pooled, unit = start_forward(
        start_active, picked, outer_weights, small, pool_weight, flag_row
    )
    result, nh2, rs2, _ = outer_forward(here, active, n1, keep_masks, outer_weights, small)
    grad_outer, second_flow, sums_two = outer_backward(
        out_cotangent, token_ok, nh2, rs2, keep_masks, small
    )
    loss, temp_grad, grad_pre = shared_contrast(unit[0], flags, log_temp, pooled)
    start_outer, start_inner, start_branch, start_base, start_att, start_sums = start_backward(
        grad_pre, pool_weight, start_nh2, start_rs2, picked, picked_rs, start_slope, small,
        outer_weights, inner_weights, out_weight,
    )
    grad_inner, grad_branch, grad_att, base, sums_one, wide_sums = inner_backward(
        grad_outer, slope, second_flow, nh1, rs1, keep_masks, outer_weights, inner_weights,
        out_weight, small,
    )
    grad_qkv, sums_qv = attend_backward(grad_att, start_att, table, qkv, probs)
    grad_small = small_sums(start_sums, sums_qv, sums_one, sums_two, wide_sums)
    input_grad = input_gradient(base, start_base, table, grad_qkv, qkv_weights)
    input_grad = input_grad.reshape(hidden_in.shape)
    parts = [scattered(across(flat, grad_qkv[:, j * width : (j + 1) * width])) for j in range(3)]
    parts.append(scattered(across(att, grad_branch) + across(picked_att, start_branch)))
    small_parts = [scattered(grad_small[i]) for i in range(9)]
    inner_bias_part = scattered(grad_small[9 : 9 + wide].reshape(ff))
    outer_part = scattered(across(active, grad_outer) + across(start_active, start_outer))
    inner_part = scattered(across(n1, grad_inner) + across(picked[0], start_inner))
    pool_part = scattered(across(cls, grad_pre))
    return (
        loss,
        result,
        input_grad,
        parts[0],
        small_parts[0],
        parts[1],
        parts[2],
        small_parts[1],
        parts[3],
        small_parts[2],
        small_parts[3],
        small_parts[4],
        inner_part,
        inner_bias_part,
        outer_part,
        small_parts[5],
        small_parts[6],
        small_parts[7],
        pool_part,
        small_parts[8],
        temp_grad,
    )


def solution(mesh):
    outer, inner = mesh.shape["dp"], mesh.shape["fsdp"]
    sizes = (4, 2, 2, 2) if (outer, inner) == (16, 2) else (outer, 1, 1, inner)
    mesh = jax.sharding.Mesh(mesh.devices.reshape(sizes), BOTH)
    in_specs = (
        P(BOTH, None, None),
        P(BOTH),
        P(BOTH),
        P(BOTH, None),
        P(None, None, BOTH, None, None),
        P(None, BOTH, None, None),
        P(BOTH, None),
        P(BOTH),
        P(BOTH, None),
        P(BOTH, None),
        P(BOTH),
        P(BOTH, None),
        P(BOTH),
        P(BOTH),
        P(BOTH),
        P(BOTH, None),
        P(BOTH),
        P(BOTH, None),
        P(BOTH),
        P(BOTH),
        P(BOTH),
        P(BOTH, None),
        P(BOTH),
        P(),
    )
    out_specs = (
        P(),
        P(None, BOTH, None, None),
        P(BOTH, None, None),
        P(BOTH, None),
        P(BOTH),
        P(BOTH, None),
        P(BOTH, None),
        P(BOTH),
        P(BOTH, None),
        P(BOTH),
        P(BOTH),
        P(BOTH),
        P(BOTH, None),
        P(BOTH),
        P(BOTH, None),
        P(BOTH),
        P(BOTH),
        P(BOTH),
        P(BOTH, None),
        P(BOTH),
        P(),
    )
    return jax.shard_map(body, mesh=mesh, in_specs=in_specs, out_specs=out_specs, check_vma=False)
```

```python
import functools

import jax
import jax.numpy as jnp
from jax import lax
from jax.experimental import pallas as pl
from jax.experimental.pallas import tpu as pltpu
from jax.sharding import PartitionSpec as P

HEADS = 12
BOTH = ("z", "x", "c", "y")
LOW = jnp.bfloat16
FULL = jnp.float32

precise = lax.Precision.HIGHEST
keep_scale = 1.0 / 0.9
inv_root_two = 0.7071067811865476
inv_root_tau = 0.3989422804014327
eps = 1e-06


def matmul(left, right):
    return lax.dot_general(left, right, (((1,), (0,)), ((), ())), preferred_element_type=FULL)


def against(left, right):
    return lax.dot_general(left, right, (((1,), (1,)), ((), ())), preferred_element_type=FULL)


def across(left, right):
    return lax.dot_general(left, right, (((0,), (0,)), ((), ())), preferred_element_type=FULL)


def paired():
    return tuple(lax.axis_size(axis) for axis in BOTH) == (4, 2, 2, 2)


def place(z, x, c, y):
    return ((z * 2 + x) * 2 + c) * 2 + y


def pairs(move):
    every = [(z, x, c, y) for z in range(4) for x in range(2) for c in range(2) for y in range(2)]
    return [(place(*t), place(*move(*t))) for t in every]


def first_pairs():
    return pairs(lambda z, x, c, y: (z, 1 - x, c, y) if c == 0 else (z, x, c, 1 - y))


def second_pairs():
    return pairs(lambda z, x, c, y: (z, x, c, 1 - y) if c == 0 else (z, 1 - x, c, y))


def across_pairs():
    return pairs(lambda z, x, c, y: (z, 1 - x, c, 1 - y))


def core_pairs():
    return pairs(lambda z, x, c, y: (z, x, 1 - c, y))


def along_pairs(k):
    return pairs(lambda z, x, c, y: ((z + k) % 4, x, c, y))


def whereabouts():
    index = lax.axis_index(BOTH)
    return index // 8, index // 4 % 2, index // 2 % 2, index % 2


def send(block, route):
    return lax.ppermute(block, BOTH, route)


def together(*values):
    return lax.optimization_barrier(values)


def along_z(shard):
    return [send(shard, along_pairs(k)) for k in (1, 2, 3)]


def over_cores(own):
    return [send(block, core_pairs()) for block in own]


def where_from(here, core, p1, p2):
    first_x = core == 0
    on_x = jnp.where(first_x, p1, p2)
    on_y = jnp.where(first_x, p2, p1)
    return here[1] ^ on_x, here[3] ^ on_y


def order_kernel(parts, here_ref, *refs):
    blocks, outs = refs[:8], refs[8:]
    here = [here_ref[i] for i in range(4)]
    total = None
    for i in range(8):
        core = here[2] if i < 4 else 1 - here[2]
        x, y = where_from(here, core, i % 2, i // 2 % 2)
        for k in range(4):
            z = lax.rem(here[0] + 4 - k, 4)
            device = place(z, x, core, y)
            item = 0
            for count, out in zip(parts, outs):
                if count == 0:
                    value = blocks[i][k, item].astype(FULL)
                    total = value if total is None else total + value
                    item += 1
                for n in range(count):
                    out[n, device] = blocks[i][k, item]
                    item += 1
                for n in range(-count):
                    out[device, n] = blocks[i][k, item]
                    item += 1
    for count, out in zip(parts, outs):
        if count == 0:
            out[...] = total


def in_order(here, blocks, parts):
    items, rows, width = blocks[0].shape[1:]
    whole = pl.BlockSpec(memory_space=pltpu.VMEM)
    return call(
        functools.partial(order_kernel, parts),
        "order",
        0,
        128 * items * rows * width,
        out_shape=[
            shaped((rows, width), FULL)
            if count == 0
            else shaped((count, 32, rows, width) if count > 0 else (32, -count, rows, width), LOW)
            for count in parts
        ],
        grid_spec=pltpu.PrefetchScalarGridSpec(
            num_scalar_prefetch=1, grid=(), in_specs=[whole] * 8, out_specs=[whole] * len(parts)
        ),
    )(here, *blocks)


def add_low(left, right):
    return (left.astype(FULL) + right.astype(FULL)).astype(LOW)


def halves_of(kept, come):
    return add_low(kept[2:], come[2:]), add_low(kept[:2], come[:2])


def quarters_of(own, come):
    return add_low(own[1], come[1]), add_low(own[0], come[0])


def add_all(own, come):
    return sum([part.astype(FULL) for part in come], own.astype(FULL)).astype(LOW)


def over_z(column):
    z = lax.axis_index("z")
    own = lax.dynamic_index_in_dim(column, z, 0, keepdims=False)
    away = [lax.dynamic_index_in_dim(column, (z + k) % 4, 0, keepdims=False) for k in (1, 2, 3)]
    return [own] + [send(part, along_pairs(k)) for k, part in zip((1, 2, 3), away)]


def finish_kernel(inner, vectors, *refs):
    parts, outs = refs[1:5], refs[5:]
    here_ref = refs[0]
    rows, width = parts[0].shape[1:]

    def total(n):
        return sum(part[n].astype(FULL) for part in parts)

    for n in range(inner):
        if outs[0].shape[0] == rows:
            outs[0][:, n * width : (n + 1) * width] = total(n)
        else:
            outs[0][n * rows : (n + 1) * rows] = total(n)
    outs = outs[1:] if inner else outs
    plain = parts[0].shape[0] - inner - (1 if vectors else 0)
    for n in range(plain):
        outs[n][...] = total(inner + n)
    if vectors:
        index = place(here_ref[0], here_ref[1], here_ref[2], here_ref[3])
        value = total(inner + plain)
        piece = width // 32
        band = outs[plain + 1].shape[1]
        per_row = width // band
        outs[plain][...] = pltpu.roll(value, width - piece * index, 1)[: outs[plain].shape[0], :piece]
        at = lax.broadcasted_iota(jnp.int32, value.shape, 0) == 9 + index // per_row
        line = jnp.sum(jnp.where(at, value, 0.0), axis=0, keepdims=True)
        line = jnp.broadcast_to(line, (8, width))
        line = pltpu.roll(line, width - band * lax.rem(index, per_row), 1)
        outs[plain + 1][...] = line[0:1, :band]


def finish(here, parts, inner=0, vectors=0, band=0, tall=False):
    items, rows, width = parts[0].shape
    plain = items - inner - (1 if vectors else 0)
    shapes = [(inner * rows, width) if tall else (rows, inner * width)] if inner else []
    shapes += [(rows, width)] * plain
    shapes += [(vectors, width // 32), (1, band)] if vectors else []
    return call(
        functools.partial(finish_kernel, inner, vectors),
        "finish",
        0,
        12 * items * rows * width,
        grid_spec=pltpu.PrefetchScalarGridSpec(
            num_scalar_prefetch=1,
            grid=(1,),
            in_specs=[fixed(parts[0].shape)] * 4,
            out_specs=[fixed(shape) for shape in shapes],
        ),
        out_shape=[shaped(shape, FULL) for shape in shapes],
    )(here, *parts)


def layout(row_counts, buckets, lengths, row_len):
    slot_count = buckets.shape[0]
    live_rows = jnp.arange(slot_count, dtype=jnp.int32) < row_counts[0]
    sent_count = jnp.right_shift(jnp.int32(4), buckets)
    slot_ids = jnp.arange(4, dtype=jnp.int32)
    held_slots = (slot_ids[None, :] < sent_count[:, None]) & live_rows[:, None]
    sizes_used = jnp.where(held_slots, lengths, 0)
    finish = jnp.cumsum(sizes_used, axis=1, dtype=jnp.int32)
    starts = finish - sizes_used
    places = jnp.arange(row_len, dtype=jnp.int32)
    segment = jnp.sum((places[None, :, None] >= finish[:, None, :]).astype(jnp.int32), axis=2)
    return segment, starts, held_slots


def pick_table(starts, held_slots, row_len):
    rows = starts.shape[0]
    slot = jnp.arange(64, dtype=jnp.int32)
    view, row, k = slot // 32, slot % 32 // 4, slot % 4
    row = jnp.minimum(row, rows - 1)
    real = slot % 32 < rows * 4
    start = starts[row, k]
    held = held_slots[row, k] & real
    token = jnp.arange(2 * row_len, dtype=jnp.int32)
    hit = held[:, None] & (token[None, :] == (view * row_len + start)[:, None])
    here = jnp.arange(rows, dtype=jnp.int32)[:, None] == row[None, :]
    return (here[:, :, None] & hit[None]).astype(LOW)


rooms = {"pack": 60, "attend": 60, "inner_forward": 60, "outer_both": 60, "inner_backward": 60}


def call(kernel, name, flops, moved, **kwargs):
    room = rooms.get(name, 36)
    return pl.pallas_call(
        kernel,
        name=name,
        compiler_params=pltpu.CompilerParams(vmem_limit_bytes=room * 2**20),
        cost_estimate=pl.CostEstimate(flops=flops // 10, transcendentals=0, bytes_accessed=moved // 10),
        **kwargs,
    )


def scalars_spec():
    return pl.BlockSpec(memory_space=pltpu.SMEM)


def hand_on(here, mark):
    for n in range(4):
        mark[n] = here[n]


def fixed(shape):
    zeros = (0,) * len(shape)
    return pl.BlockSpec(shape, lambda *_: zeros)


def shaped(shape, kind):
    return jax.ShapeDtypeStruct(shape, kind)


def halves(pair, even):
    zero = jnp.zeros_like(pair)
    return jnp.concatenate([jnp.where(even, pair, zero), jnp.where(even, zero, pair)], axis=0)


def attend_kernel(here, x, weights, biases, seg_row, seg_col, qkv, out, probs, mark):
    hand_on(here, mark)
    length, width = out.shape
    for j in range(3):
        value = matmul(x[...], weights[j]) + biases[j]
        qkv[:, j * width : (j + 1) * width] = value.astype(LOW)
    even = lax.broadcasted_iota(jnp.int32, (length, 128), 1) < 64
    same = seg_col[0] == seg_row[0]
    same = jnp.concatenate([same, same], axis=0)
    for p in range(width // 128):
        at = p * 128
        query = halves(qkv[:, at : at + 128], even)
        key = qkv[:, width + at : width + at + 128]
        value = qkv[:, 2 * width + at : 2 * width + at + 128]
        scores = jnp.where(same, against(query, key) * 0.125, -1e30)
        peak = jnp.max(scores, axis=-1, keepdims=True)
        lifted = jnp.exp(scores - peak)
        share = lifted * (1.0 / jnp.sum(lifted, axis=-1, keepdims=True))
        share = share.astype(LOW)
        probs[0, p] = share
        both = matmul(share, value)
        out[:, at : at + 128] = jnp.where(even, both[:length], both[length:]).astype(LOW)


def attend(here, flat, weights, biases, segment):
    slots, length = segment.shape
    tokens, width = flat.shape
    pairs_of = width // 128
    return call(
        attend_kernel,
        "attend",
        6 * tokens * width * width + 8 * tokens * length * width,
        16 * tokens * width,
        grid=(slots,),
        in_specs=[
            scalars_spec(),
            pl.BlockSpec((length, width), lambda r: (r, 0)),
            fixed(weights.shape),
            fixed(biases.shape),
            pl.BlockSpec((1, 1, length), lambda r: (r, 0, 0)),
            pl.BlockSpec((1, length, 1), lambda r: (r, 0, 0)),
        ],
        out_specs=[
            pl.BlockSpec((length, 3 * width), lambda r: (r, 0)),
            pl.BlockSpec((length, width), lambda r: (r, 0)),
            pl.BlockSpec((1, pairs_of, 2 * length, length), lambda r: (r, 0, 0, 0)),
            scalars_spec(),
        ],
        out_shape=[
            shaped((tokens, 3 * width), LOW),
            shaped((tokens, width), LOW),
            shaped((slots, pairs_of, 2 * length, length), LOW),
            shaped((4,), jnp.int32),
        ],
    )(here, flat, weights, biases, segment[:, None, :], segment[:, :, None])


def normal(hidden):
    centre = jnp.mean(hidden, axis=-1, keepdims=True)
    offset = hidden - centre
    spread_of = jnp.mean(offset * offset, axis=-1, keepdims=True)
    rscale = lax.rsqrt(spread_of + eps)
    return offset * rscale, rscale


def normal_back(grad_norm, normed, rscale):
    mean_grad = jnp.mean(grad_norm, axis=-1, keepdims=True)
    mean_cross = jnp.mean(grad_norm * normed, axis=-1, keepdims=True)
    return rscale * (grad_norm - mean_grad - normed * mean_cross)


def gelu_parts(inner):
    phi = 0.5 * (1.0 + lax.erf(inner * inv_root_two))
    return inner * phi, phi + inner * jnp.exp(-0.5 * inner * inner) * inv_root_tau


def inner_kernel(
    starts, held, att, x, keep, w_out, w_inner, small,
    n1, nh1, rs1, active, slope, picked, picked_att, picked_rs, picked_active, picked_slope,
    rows_one, rows_unit, rows_att, rows_scale, near, near_att,
):
    row = pl.program_id(0)
    length, width = att.shape
    branch = matmul(att[...], w_out[...]) + small[2:3]
    base = x[0].astype(FULL)
    keeps = keep[:, 0, 0].astype(FULL) * keep_scale
    first = jnp.concatenate([base + branch * keeps[0], base + branch * keeps[1]], axis=0)
    normed, rscale = normal(first)
    nh1[...] = normed.astype(LOW)
    rs1[...] = rscale
    rows_unit[...] = normed
    rows_scale[...] = jnp.broadcast_to(rscale, rows_scale.shape)
    rows_att[...] = att[...].astype(FULL)
    whole_in = normed * small[3:4] + small[4:5]
    rows_one[...] = whole_in
    inner_in = whole_in.astype(LOW)
    n1[...] = inner_in
    step = 256
    for j in range(w_inner.shape[0]):
        for at in range(0, width, step):
            inner = matmul(inner_in, w_inner[j, :, at : at + step])
            inner = inner + small[9 + j : 10 + j, at : at + step]
            value, grad = gelu_parts(inner)
            active[:, j * width + at : j * width + at + step] = value.astype(LOW)
            slope[:, j * width + at : j * width + at + step] = grad.astype(LOW)

    @pl.when(row == 0)
    def _():
        near[...] = jnp.zeros_like(near)
        near_att[...] = jnp.zeros_like(near_att)
        picked_rs[...] = jnp.zeros_like(picked_rs)

    for k in range(4):
        slot = 4 * row + k

        @pl.when(held[row, k] > 0)
        def _():
            start = starts[row, k]
            near_att[pl.ds(slot, 1)] = rows_att[pl.ds(start, 1)]
            for v in range(2):
                to = pl.ds(32 * v + slot, 1)
                near[0, to] = rows_one[pl.ds(length * v + start, 1)]
                near[1, to] = rows_unit[pl.ds(length * v + start, 1)]
                for n in range(2):
                    near[2 + n, to] = keep[v, n, 0, pl.ds(start, 1)].astype(FULL)
                picked_rs[to] = rows_scale[pl.ds(length * v + start, 1)]

    @pl.when(row == pl.num_programs(0) - 1)
    def _():
        picked[...] = near[...].astype(LOW)
        picked_att[...] = near_att[...].astype(LOW)
        begin = near[0].astype(LOW)
        for j in range(w_inner.shape[0]):
            inner = matmul(begin, w_inner[j]) + small[9 + j : 10 + j]
            value, grad = gelu_parts(inner)
            picked_active[:, j * width : (j + 1) * width] = value.astype(LOW)
            picked_slope[:, j * width : (j + 1) * width] = grad.astype(LOW)


def inner_forward(att, hidden, keep_masks, w_out, w_inner, small, starts, held_slots):
    slots, length, width = hidden.shape
    ff = w_inner.shape[0] * width
    two = 2 * length
    return call(
        inner_kernel,
        "inner_forward",
        2 * slots * two * width * ff,
        slots * two * ff * 5,
        grid_spec=pltpu.PrefetchScalarGridSpec(
            num_scalar_prefetch=2,
            grid=(slots,),
            in_specs=[
                pl.BlockSpec((length, width), lambda r, *_: (r, 0)),
                pl.BlockSpec((1, length, width), lambda r, *_: (r, 0, 0)),
                pl.BlockSpec((2, 2, 1, length, width), lambda r, *_: (0, 0, r, 0, 0)),
                fixed((width, width)),
                fixed(w_inner.shape),
                fixed(small.shape),
            ],
            out_specs=[
                pl.BlockSpec((two, width), lambda r, *_: (r, 0)),
                pl.BlockSpec((two, width), lambda r, *_: (r, 0)),
                pl.BlockSpec((two, 1), lambda r, *_: (r, 0)),
                pl.BlockSpec((two, ff), lambda r, *_: (r, 0)),
                pl.BlockSpec((two, ff), lambda r, *_: (r, 0)),
                fixed((4, 64, width)),
                fixed((32, width)),
                fixed((64, 128)),
                fixed((64, ff)),
                fixed((64, ff)),
            ],
            scratch_shapes=[
                pltpu.VMEM((two, width), FULL),
                pltpu.VMEM((two, width), FULL),
                pltpu.VMEM((length, width), FULL),
                pltpu.VMEM((two, 128), FULL),
                pltpu.VMEM((4, 64, width), FULL),
                pltpu.VMEM((32, width), FULL),
            ],
        ),
        out_shape=[
            shaped((slots * two, width), LOW),
            shaped((slots * two, width), LOW),
            shaped((slots * two, 1), FULL),
            shaped((slots * two, ff), LOW),
            shaped((slots * two, ff), LOW),
            shaped((4, 64, width), LOW),
            shaped((32, width), LOW),
            shaped((64, 128), FULL),
            shaped((64, ff), LOW),
            shaped((64, ff), LOW),
        ],
    )(starts, held_slots.astype(jnp.int32), att, hidden, keep_masks, w_out, w_inner, small)


def start_kernel(active, picked, w_outer, small, w_pool, flags, nh2, rs2, cls, pooled, unit):
    outer = matmul(active[...], w_outer[...]) + small[5:6]
    second = picked[0].astype(FULL) + outer * (picked[3].astype(FULL) * keep_scale)
    normed, rscale = normal(second)
    nh2[...] = normed.astype(LOW)
    rs2[...] = jnp.broadcast_to(rscale, rs2.shape)
    out = (normed * small[6:7] + small[7:8]).astype(LOW)
    cls[...] = out
    squashed = jnp.tanh(matmul(out, w_pool[...]) + small[8:9])
    pooled[...] = squashed
    scale = lax.rsqrt(jnp.sum(squashed * squashed, axis=-1, keepdims=True) + eps)
    ones = (squashed * scale).astype(LOW).astype(FULL)
    slot = lax.broadcasted_iota(jnp.int32, ones.shape, 0)
    unit[0] = jnp.where(slot == 28, flags[...], ones).astype(LOW)


def start_forward(active, picked, w_outer, small, w_pool, flags):
    ff, width = w_outer.shape
    return call(
        start_kernel,
        "start_forward",
        128 * width * ff,
        2 * width * ff,
        out_shape=[
            shaped((64, width), LOW),
            shaped((64, 128), FULL),
            shaped((64, width), LOW),
            shaped((64, width), FULL),
            shaped((1, 64, width), LOW),
        ],
    )(active, picked, w_outer, small, w_pool, flags)


def outer_kernel(
    here, active, n1, keep, cot, segment, w_outer, small, result, grad_outer, second_flow, sums, mark
):
    hand_on(here, mark)
    row = pl.program_id(0)
    length = n1.shape[0] // 2
    keeps = keep[:, 0, 0].astype(FULL) * keep_scale
    keeps = jnp.concatenate([keeps[0], keeps[1]], axis=0)
    outer = matmul(active[...], w_outer[...]) + small[5:6]
    second = n1[...].astype(FULL) + outer * keeps
    normed, rscale = normal(second)
    out = (normed * small[6:7] + small[7:8]).astype(LOW)
    result[0, 0] = out[:length]
    result[1, 0] = out[length:]
    flow = jnp.concatenate([cot[0, 0], cot[1, 0]], axis=0).astype(FULL)
    ok = (segment[0] < 4).astype(FULL)
    grad_out = flow * jnp.concatenate([ok, ok], axis=0)
    grad_second = normal_back(grad_out * small[6:7], normed, rscale)
    low = (grad_second * keeps).astype(LOW)
    grad_outer[...] = low
    second_flow[...] = grad_second.astype(LOW)

    @pl.when(row == 0)
    def _():
        sums[...] = jnp.zeros_like(sums)

    sums[0:1] += jnp.sum(low.astype(FULL), axis=0, keepdims=True)
    sums[1:2] += jnp.sum(grad_out * normed, axis=0, keepdims=True)
    sums[2:3] += jnp.sum(grad_out, axis=0, keepdims=True)


def outer_both(here, active, n1, keep_masks, cotangent, segment, w_outer, small):
    tokens, ff = active.shape
    width = n1.shape[1]
    slots = keep_masks.shape[2]
    length = keep_masks.shape[3]
    two = 2 * length
    return call(
        outer_kernel,
        "outer_both",
        2 * tokens * width * ff,
        2 * tokens * ff,
        grid=(slots,),
        in_specs=[
            scalars_spec(),
            pl.BlockSpec((two, ff), lambda r: (r, 0)),
            pl.BlockSpec((two, width), lambda r: (r, 0)),
            pl.BlockSpec((2, 1, 1, length, width), lambda r: (0, 1, r, 0, 0)),
            pl.BlockSpec((2, 1, length, width), lambda r: (0, r, 0, 0)),
            pl.BlockSpec((1, length, 1), lambda r: (r, 0, 0)),
            fixed((ff, width)),
            fixed(small.shape),
        ],
        out_specs=[
            pl.BlockSpec((2, 1, length, width), lambda r: (0, r, 0, 0)),
            pl.BlockSpec((two, width), lambda r: (r, 0)),
            pl.BlockSpec((two, width), lambda r: (r, 0)),
            fixed((8, width)),
            scalars_spec(),
        ],
        out_shape=[
            shaped((2, slots, length, width), LOW),
            shaped((tokens, width), LOW),
            shaped((tokens, width), LOW),
            shaped((8, width), FULL),
            shaped((4,), jnp.int32),
        ],
    )(here, active, n1, keep_masks, cotangent, segment[:, :, None], w_outer, small)


def split_matmul(left, right):
    upper = left.astype(LOW)
    lower = (left - upper.astype(FULL)).astype(LOW)
    return matmul(upper, right) + matmul(lower, right)


def pool_back(grad_unit, squashed):
    scale = lax.rsqrt(jnp.sum(squashed * squashed, axis=-1, keepdims=True) + eps)
    grad_pooled = scale * grad_unit - squashed * (scale * scale * scale) * jnp.sum(
        squashed * grad_unit, axis=-1, keepdims=True
    )
    return (grad_pooled * (1.0 - squashed * squashed)).astype(LOW)


def loss_kernel(here_ref, *refs):
    blocks = refs[:8]
    (
        temp, pooled, w_pool, nh2, rs2, picked, small, scalars, grad_pre, start_outer, start_second,
        start_sums, anchors, partners, flat, sem,
    ) = refs[8:]
    here = [here_ref[i] for i in range(4)]
    copies = []
    for i in range(8):
        core = here[2] if i < 4 else 1 - here[2]
        x, y = where_from(here, core, i % 2, i // 2 % 2)
        for k in range(4):
            z = lax.rem(here[0] + 4 - k, 4)
            row = pl.multiple_of(place(z, x, core, y) * 32, 32)
            source = blocks[i].at[k, 0]
            for half, target in ((0, anchors), (1, partners)):
                copies.append(
                    pltpu.make_async_copy(
                        source.at[pl.ds(32 * half, 32)], target.at[pl.ds(row, 32)], sem
                    )
                )
    for copy in copies:
        copy.start()
    for copy in copies:
        copy.wait()
    count = anchors.shape[0]
    groups = count // 32
    inv_temp = jnp.exp(-temp[...])
    all_anchors = anchors[...]
    all_partners = partners[...]
    for d in range(groups):
        flat[d : d + 1] = anchors[d * 32 + 28 : d * 32 + 29, :128].astype(FULL)
    marks = flat[...].astype(LOW)
    slot = lax.broadcasted_iota(jnp.int32, (128, count), 0)
    lane = lax.broadcasted_iota(jnp.int32, (128, count), 1)
    wide = matmul(marks, (slot == lane % 32).astype(LOW))
    group = lax.broadcasted_iota(jnp.int32, (groups, count), 0)
    lane = lax.broadcasted_iota(jnp.int32, (groups, count), 1)
    row_ok = jnp.sum(jnp.where(group == lane // 32, wide, 0.0), axis=0, keepdims=True)
    tall_row = lax.broadcasted_iota(jnp.int32, (count, groups), 0)
    tall_group = lax.broadcasted_iota(jnp.int32, (count, groups), 1)
    tall = matmul((tall_row // 32 == tall_group).astype(LOW), marks)
    tall_row = lax.broadcasted_iota(jnp.int32, (count, 128), 0)
    tall_lane = lax.broadcasted_iota(jnp.int32, (count, 128), 1)
    column_ok = jnp.sum(jnp.where(tall_row % 32 == tall_lane, tall, 0.0), axis=1, keepdims=True)
    total_held = jnp.sum(row_ok, axis=1, keepdims=True)
    weight = row_ok / total_held
    raw = against(all_partners, all_anchors) * inv_temp
    positive = []
    eye = lax.broadcasted_iota(jnp.int32, (128, 128), 0)
    eye = eye == lax.broadcasted_iota(jnp.int32, (128, 128), 1)
    for at in range(0, count, 128):
        block = raw[at : at + 128, at : at + 128]
        positive.append(jnp.sum(jnp.where(eye, block, 0.0), axis=0, keepdims=True))
    positive = jnp.concatenate(positive, axis=1)
    masked = jnp.where(column_ok > 0, raw, -1e30)
    peak = jnp.max(masked, axis=0, keepdims=True)
    lifted = jnp.exp(masked - peak)
    whole = jnp.sum(lifted, axis=0, keepdims=True)
    sim_total = peak + jnp.log(whole)
    crossed = jnp.sum(lifted * masked, axis=0, keepdims=True) / whole
    loss = jnp.sum(weight * (sim_total - positive), axis=1, keepdims=True)
    temp_grad = jnp.sum(weight * (positive - crossed), axis=1, keepdims=True)
    scalars[0:1] = jnp.broadcast_to(loss, (1, 128))
    scalars[1:2] = jnp.broadcast_to(temp_grad, (1, 128))
    mine = place(here[0], here[1], here[2], here[3])
    first = pl.multiple_of(mine * 32, 32)
    my_anchors = anchors[pl.ds(first, 32)]
    my_partners = partners[pl.ds(first, 32)]
    tall_lane = lax.broadcasted_iota(jnp.int32, (32, 128), 1)
    tall_row = lax.broadcasted_iota(jnp.int32, (32, 128), 0)
    my_flags = flat[pl.ds(mine, 1)]
    my_ok = jnp.sum(jnp.where(tall_lane == tall_row, my_flags, 0.0), axis=1, keepdims=True)
    my_weight = my_ok / total_held
    back = against(my_partners, all_anchors) * inv_temp
    back_shares = jnp.exp(jnp.where(my_ok > 0, back, -1e30) - sim_total) * weight
    grad_partner = inv_temp * (
        split_matmul(back_shares, all_anchors) - my_weight * my_anchors.astype(FULL)
    )
    mine_masked = jnp.where(row_ok > 0, against(my_anchors, all_partners) * inv_temp, -1e30)
    peak = jnp.max(mine_masked, axis=1, keepdims=True)
    lifted = jnp.exp(mine_masked - peak)
    my_shares = lifted * (my_weight / jnp.sum(lifted, axis=1, keepdims=True))
    grad_anchor = inv_temp * (
        split_matmul(my_shares, all_partners) - my_weight * my_partners.astype(FULL)
    )
    grad_unit = jnp.concatenate([grad_anchor, grad_partner], axis=0)
    pre = pool_back(grad_unit, pooled[...])
    grad_pre[...] = pre
    start_outer[...], start_second[...], start_sums[...] = start_outer_back(
        pre, w_pool[...], nh2[...], rs2[:, :1], picked[3], small
    )


def contrast(here, blocks, log_temp, pooled, w_pool, nh2, rs2, picked, small):
    width = pooled.shape[1]
    count = 32 * 32
    whole = pl.BlockSpec(memory_space=pltpu.VMEM)
    return pl.pallas_call(
        loss_kernel,
        name="contrast",
        grid_spec=pltpu.PrefetchScalarGridSpec(
            num_scalar_prefetch=1,
            grid=(),
            in_specs=[pl.BlockSpec(memory_space=pl.ANY)] * 8 + [whole] * 7,
            out_specs=[whole] * 5,
            scratch_shapes=[
                pltpu.VMEM((count, width), LOW),
                pltpu.VMEM((count, width), LOW),
                pltpu.VMEM((32, 128), FULL),
                pltpu.SemaphoreType.DMA,
            ],
        ),
        out_shape=[
            shaped((2, 128), FULL),
            shaped((64, width), LOW),
            shaped((64, width), LOW),
            shaped((64, width), FULL),
            shaped((8, width), FULL),
        ],
        compiler_params=pltpu.CompilerParams(vmem_limit_bytes=36 * 2**20),
        cost_estimate=pl.CostEstimate(
            flops=2 * count * count * width, transcendentals=0, bytes_accessed=4 * count * width
        ),
    )(here, *blocks, log_temp.reshape(1, 1), pooled, w_pool, nh2, rs2, picked, small)


def start_back(outer, second, picked, rs1, slope, w_outer, w_inner, w_out, small):
    width = outer.shape[1]
    wide = w_inner.shape[0]
    inner = []
    grad_normed = second
    for j in range(wide):
        grad_active = against(outer, w_outer[j * width : (j + 1) * width])
        low = (grad_active * slope[:, j * width : (j + 1) * width].astype(FULL)).astype(LOW)
        inner.append(low)
        grad_normed = grad_normed + against(low, w_inner[j])
    unit_one = picked[1].astype(FULL)
    first = normal_back(grad_normed * small[3:4], unit_one, rs1)
    kept = first * (picked[2].astype(FULL) * keep_scale)
    branch = (kept[:32] + kept[32:]).astype(LOW)
    base = first[:32] + first[32:]
    att = against(branch, w_out).astype(LOW)
    sums = [down(branch), down(grad_normed * unit_one), down(grad_normed)]
    return inner, branch, base, att, sums, [down(low) for low in inner]


def down(value):
    return jnp.sum(value.astype(FULL), axis=0, keepdims=True)


def start_outer_back(grad_pre, w_pool, nh2, rs2, keeps, small):
    grad_out = against(grad_pre, w_pool)
    normed = nh2.astype(FULL)
    grad_second = normal_back(grad_out * small[6:7], normed, rs2)
    low = (grad_second * (keeps.astype(FULL) * keep_scale)).astype(LOW)
    sums = [down(low), down(grad_out * normed), down(grad_out), down(grad_pre)]
    sums.append(jnp.zeros((4, low.shape[1]), FULL))
    return low, grad_second, jnp.concatenate(sums)


def start_back_kernel(
    outer, second, old_sums, picked, rs1, slope, small, w_outer_hbm, w_inner_hbm, w_out_hbm,
    inner, branch, base, att, sums, w_outer, w_inner, w_out, sems,
):
    copies = [
        pltpu.make_async_copy(source, target, sems.at[n])
        for n, (source, target) in enumerate(
            ((w_outer_hbm, w_outer), (w_inner_hbm, w_inner), (w_out_hbm, w_out))
        )
    ]
    for copy in copies:
        copy.start()
    for copy in copies:
        copy.wait()
    out = start_back(
        outer[...], second[...], picked, rs1[:, :1], slope, w_outer, w_inner, w_out[...], small
    )
    width = outer.shape[1]
    for j, low in enumerate(out[0]):
        inner[:, j * width : (j + 1) * width] = low
    branch[...] = out[1]
    base[...] = out[2]
    att[...] = out[3]
    sums[0:2] = jnp.zeros((2, width), FULL)
    for n, value in enumerate(out[4]):
        sums[2 + n : 3 + n] = value
    sums[5:9] = old_sums[0:4]
    for j, value in enumerate(out[5]):
        sums[9 + j : 10 + j] = value
    sums[13:24] = jnp.zeros((11, width), FULL)


def start_backward(outer, second, old_sums, picked, rs1, slope, small, w_outer, w_inner, w_out):
    ff, width = w_outer.shape
    whole = pl.BlockSpec(memory_space=pltpu.VMEM)
    outside = pl.BlockSpec(memory_space=pl.ANY)
    return call(
        start_back_kernel,
        "start_backward",
        256 * width * ff,
        4 * width * ff,
        in_specs=[whole] * 7 + [outside] * 3,
        out_shape=[
            shaped((64, ff), LOW),
            shaped((32, width), LOW),
            shaped((32, width), FULL),
            shaped((32, width), LOW),
            shaped((24, width), FULL),
        ],
        scratch_shapes=[
            pltpu.VMEM(w_outer.shape, LOW),
            pltpu.VMEM(w_inner.shape, LOW),
            pltpu.VMEM(w_out.shape, LOW),
            pltpu.SemaphoreType.DMA((3,)),
        ],
    )(outer, second, old_sums, picked, rs1, slope, small, w_outer, w_inner, w_out)


def inner_back_kernel(
    here, grad_outer, slope, second, nh1, rs1, keep, w_outer, w_inner, w_out, small,
    grad_inner, grad_branch, grad_att, base, sums, wide_sums, mark,
):
    hand_on(here, mark)
    row = pl.program_id(0)
    length = grad_branch.shape[0]
    width = grad_branch.shape[1]
    step = 256

    @pl.when(row == 0)
    def _():
        sums[...] = jnp.zeros_like(sums)
        wide_sums[...] = jnp.zeros_like(wide_sums)

    low_outer = grad_outer[...]
    grad_normed = second[...].astype(FULL)
    for j in range(w_inner.shape[0]):
        for at in range(0, width, step):
            lane = j * width + at
            grad_active = against(low_outer, w_outer[lane : lane + step])
            low = (grad_active * slope[:, lane : lane + step].astype(FULL)).astype(LOW)
            grad_inner[:, lane : lane + step] = low
            wide_sums[:, lane : lane + step] += jnp.sum(low.astype(FULL), axis=0, keepdims=True)
        grad_normed = grad_normed + against(
            grad_inner[:, j * width : (j + 1) * width], w_inner[j]
        )
    normed = nh1[...].astype(FULL)
    grad_first = normal_back(grad_normed * small[3:4], normed, rs1[...])
    sums[0:1] += jnp.sum(grad_normed * normed, axis=0, keepdims=True)
    sums[1:2] += jnp.sum(grad_normed, axis=0, keepdims=True)
    keeps = keep[:, 0, 0].astype(FULL) * keep_scale
    branch = (grad_first[:length] * keeps[0] + grad_first[length:] * keeps[1]).astype(LOW)
    grad_branch[...] = branch
    sums[2:3] += jnp.sum(branch.astype(FULL), axis=0, keepdims=True)
    base[...] = grad_first[:length] + grad_first[length:]
    grad_att[...] = against(branch, w_out[...]).astype(LOW)


def inner_backward(
    here, grad_outer, slope, second, nh1, rs1, keep_masks, w_outer, w_inner, w_out, small
):
    tokens, ff = slope.shape
    slots, length, width = keep_masks.shape[2:]
    two = 2 * length
    return call(
        inner_back_kernel,
        "inner_backward",
        4 * tokens * width * ff,
        5 * tokens * ff,
        grid=(slots,),
        in_specs=[
            scalars_spec(),
            pl.BlockSpec((two, width), lambda r: (r, 0)),
            pl.BlockSpec((two, ff), lambda r: (r, 0)),
            pl.BlockSpec((two, width), lambda r: (r, 0)),
            pl.BlockSpec((two, width), lambda r: (r, 0)),
            pl.BlockSpec((two, 1), lambda r: (r, 0)),
            pl.BlockSpec((2, 1, 1, length, width), lambda r: (0, 0, r, 0, 0)),
            fixed(w_outer.shape),
            fixed(w_inner.shape),
            fixed(w_out.shape),
            fixed(small.shape),
        ],
        out_specs=[
            pl.BlockSpec((two, ff), lambda r: (r, 0)),
            pl.BlockSpec((length, width), lambda r: (r, 0)),
            pl.BlockSpec((length, width), lambda r: (r, 0)),
            pl.BlockSpec((length, width), lambda r: (r, 0)),
            fixed((8, width)),
            fixed((1, ff)),
            scalars_spec(),
        ],
        out_shape=[
            shaped((tokens, ff), LOW),
            shaped((slots * length, width), LOW),
            shaped((slots * length, width), LOW),
            shaped((slots * length, width), FULL),
            shaped((8, width), FULL),
            shaped((1, ff), FULL),
            shaped((4,), jnp.int32),
        ],
    )(here, grad_outer, slope, second, nh1, rs1, keep_masks, w_outer, w_inner, w_out, small)


def attend_back_kernel(grad_att, start_att, table, qkv, probs, grad_qkv, sums):
    row = pl.program_id(0)
    length, width = grad_att.shape
    even = lax.broadcasted_iota(jnp.int32, (length, 128), 1) < 64

    @pl.when(row == 0)
    def _():
        sums[...] = jnp.zeros_like(sums)

    placed = across(table[0, :32, :length], start_att[...])
    whole_att = (grad_att[...].astype(FULL) + placed).astype(LOW)
    for p in range(width // 128):
        at = p * 128
        query = halves(qkv[:, at : at + 128], even)
        key = halves(qkv[:, width + at : width + at + 128], even)
        value = qkv[:, 2 * width + at : 2 * width + at + 128]
        flow = halves(whole_att[:, at : at + 128], even)
        share = probs[0, p]
        share_f = share.astype(FULL)
        grad_share = against(flow, value)
        inside = jnp.sum(grad_share * share_f, axis=-1, keepdims=True)
        grad_scores = (share_f * (grad_share - inside)).astype(LOW)
        grad_value = across(share, flow).astype(LOW)
        side = jnp.concatenate([grad_scores[:length], grad_scores[length:]], axis=1)
        grad_query = (matmul(side, key) * 0.125).astype(LOW)
        grad_key = (across(grad_scores, query) * 0.125).astype(LOW)
        grad_qkv[:, at : at + 128] = grad_query
        grad_qkv[:, width + at : width + at + 128] = grad_key
        grad_qkv[:, 2 * width + at : 2 * width + at + 128] = grad_value
        sums[0:1, at : at + 128] += jnp.sum(grad_query.astype(FULL), axis=0, keepdims=True)
        sums[1:2, at : at + 128] += jnp.sum(grad_value.astype(FULL), axis=0, keepdims=True)


def attend_backward(grad_att, start_att, table, qkv, probs):
    slots, pairs_of, _, length = probs.shape
    width = grad_att.shape[1]
    return call(
        attend_back_kernel,
        "attend_backward",
        16 * slots * length * length * width,
        18 * slots * length * width,
        grid=(slots,),
        in_specs=[
            pl.BlockSpec((length, width), lambda r: (r, 0)),
            fixed((32, width)),
            pl.BlockSpec((1, 64, 2 * length), lambda r: (r, 0, 0)),
            pl.BlockSpec((length, 3 * width), lambda r: (r, 0)),
            pl.BlockSpec((1, pairs_of, 2 * length, length), lambda r: (r, 0, 0, 0)),
        ],
        out_specs=[
            pl.BlockSpec((length, 3 * width), lambda r: (r, 0)),
            fixed((8, width)),
        ],
        out_shape=[shaped((slots * length, 3 * width), LOW), shaped((8, width), FULL)],
    )(grad_att, start_att, table, qkv, probs)


def input_kernel(here, base, start_base, table, grad_qkv, weights, out, mark):
    hand_on(here, mark)
    width = weights.shape[1]
    total = base[...] + lax.dot_general(
        table[...].astype(FULL),
        start_base[...],
        (((0,), (0,)), ((), ())),
        precision=precise,
        preferred_element_type=FULL,
    )
    for j in range(3):
        total = total + against(grad_qkv[:, j * width : (j + 1) * width], weights[j])
    out[...] = total


def input_gradient(here, base, start_base, table, grad_qkv, weights):
    tokens, width = base.shape
    rows, _, two = table.shape
    table = table[:, :32, : two // 2].transpose(1, 0, 2).reshape(32, tokens)
    table = jnp.pad(table, ((0, 0), (0, -tokens % 256)))
    step = 256
    return call(
        input_kernel,
        "input_gradient",
        6 * tokens * width * width,
        14 * tokens * width,
        grid=(pl.cdiv(tokens, step),),
        in_specs=[
            scalars_spec(),
            pl.BlockSpec((step, width), lambda r: (r, 0)),
            fixed((32, width)),
            pl.BlockSpec((32, step), lambda r: (0, r)),
            pl.BlockSpec((step, 3 * width), lambda r: (r, 0)),
            fixed(weights.shape),
        ],
        out_specs=[pl.BlockSpec((step, width), lambda r: (r, 0)), scalars_spec()],
        out_shape=[shaped((tokens, width), FULL), shaped((4,), jnp.int32)],
    )(here, base, start_base, table, grad_qkv, weights)


def store_part(here, value, z, x, c, y, kept, away, at):
    on_x = here[1] ^ x
    on_y = here[3] ^ y
    index = 2 * on_y + on_x if c == 0 else 2 * on_x + on_y

    @pl.when(here[2] == c)
    def _():
        kept[(index,) + at] = value

    @pl.when(here[2] != c)
    def _():
        away[(index,) + at] = value


def outer_weight_kernel(
    here_ref, active, grad_outer, start_active, start_outer, cls, grad_pre, kept, away
):
    here = [here_ref[i] for i in range(4)]
    rows = kept.shape[3]
    step = pl.program_id(0)
    last = pl.num_programs(0) - 1

    @pl.when(step < last)
    def _():
        whole = across(active[...], grad_outer[...]) + across(start_active[...], start_outer[...])
        whole = whole.astype(LOW)
        for n in range(32):
            x, c, y, item = n // 16, n // 8 % 2, n // 4 % 2, n % 4
            value = whole[n * rows : (n + 1) * rows]
            store_part(here, value, 0, x, c, y, kept, away, (step, item))

    @pl.when(step == last)
    def _():
        store_parts(here, across(cls[...], grad_pre[...]).astype(LOW), kept, away, 4)


def outer_weight(here, active, grad_outer, start_active, start_outer, *others):
    tokens, ff = active.shape
    width = grad_outer.shape[1]
    part = ff // 4
    shape = (4, 4, 5, width // 32, width)
    return call(
        outer_weight_kernel,
        "outer_weight",
        2 * tokens * ff * width,
        2 * tokens * ff,
        grid_spec=pltpu.PrefetchScalarGridSpec(
            num_scalar_prefetch=1,
            grid=(5,),
            in_specs=[
                pl.BlockSpec((tokens, part), lambda z, _: (0, jnp.minimum(z, 3))),
                pl.BlockSpec((tokens, width), lambda z, _: (0, 0)),
                pl.BlockSpec((64, part), lambda z, _: (0, jnp.minimum(z, 3))),
                pl.BlockSpec((64, width), lambda z, _: (0, 0)),
            ]
            + [fixed(other.shape) for other in others],
            out_specs=[fixed(shape)] * 2,
        ),
        out_shape=[shaped(shape, LOW)] * 2,
    )(here, active, grad_outer, start_active, start_outer, *others)


def store_parts(here, whole, kept, away, item=0):
    rows = kept.shape[3]
    for n in range(32):
        z, x, c, y = n // 8, n // 4 % 2, n // 2 % 2, n % 2
        store_part(here, whole[n * rows : (n + 1) * rows], z, x, c, y, kept, away, (z, item))


def inner_weight_kernel(
    here_ref, n1, grad_inner, start_n1, start_inner, att, branch, start_att, start_branch, kept, away
):
    here = [here_ref[i] for i in range(4)]
    step = pl.program_id(0)
    last = pl.num_programs(0) - 1

    @pl.when(step < last)
    def _():
        whole = across(n1[...], grad_inner[...]) + across(start_n1[0], start_inner[...])
        store_parts(here, whole.astype(LOW), kept, away)

    @pl.when(step == last)
    def _():
        whole = across(att[...], branch[...]) + across(start_att[...], start_branch[...])
        store_parts(here, whole.astype(LOW), kept, away)


def inner_weight(here, n1, grad_inner, picked, start_inner, *others):
    tokens, ff = grad_inner.shape
    width = n1.shape[1]
    wide = ff // width
    spec = pl.BlockSpec((4, 4, 1, width // 32, width), lambda j, _: (0, 0, j, 0, 0))
    shape = shaped((4, 4, wide + 1, width // 32, width), LOW)
    return call(
        inner_weight_kernel,
        "inner_weight",
        2 * tokens * ff * width,
        2 * tokens * ff,
        grid_spec=pltpu.PrefetchScalarGridSpec(
            num_scalar_prefetch=1,
            grid=(wide + 1,),
            in_specs=[
                pl.BlockSpec((tokens, width), lambda j, _: (0, 0)),
                pl.BlockSpec((tokens, width), lambda j, _: (0, jnp.minimum(j, wide - 1))),
                pl.BlockSpec((1, 64, width), lambda j, _: (0, 0, 0)),
                pl.BlockSpec((64, width), lambda j, _: (0, jnp.minimum(j, wide - 1))),
            ]
            + [fixed(other.shape) for other in others],
            out_specs=[spec, spec],
        ),
        out_shape=[shape, shape],
    )(here, n1, grad_inner, picked, start_inner, *others)


def attend_weight_kernel(
    here_ref, x, grad_qkv, start_sums, sums_qv, sums_one, sums_two, wide_sums, kept, away
):
    here = [here_ref[i] for i in range(4)]
    step = pl.program_id(0)

    @pl.when(step < 3)
    def _():
        store_parts(here, across(x[...], grad_qkv[...]).astype(LOW), kept, away)

    @pl.when(step == 3)
    def _():
        width = x.shape[1]
        value = start_sums[...] + jnp.concatenate(
            [sums_qv[0:2], sums_one[2:3], sums_one[0:2], sums_two[0:3]]
            + [jnp.zeros((1, width), FULL)]
            + [wide_sums[:, j * width : (j + 1) * width] for j in range(4)]
            + [jnp.zeros((11, width), FULL)],
            axis=0,
        )
        value = value.astype(LOW)
        for index in range(4):
            for z in range(4):
                kept[index, z, 0] = value
                away[index, z, 0] = value


def attend_weight(here, x, grad_qkv, sums):
    tokens, width = x.shape
    spec = pl.BlockSpec((4, 4, 1, width // 32, width), lambda j, _: (0, 0, j, 0, 0))
    shape = shaped((4, 4, 4, width // 32, width), LOW)
    return call(
        attend_weight_kernel,
        "attend_weight",
        6 * tokens * width * width,
        8 * tokens * width,
        grid_spec=pltpu.PrefetchScalarGridSpec(
            num_scalar_prefetch=1,
            grid=(4,),
            in_specs=[
                pl.BlockSpec((tokens, width), lambda j, _: (0, 0)),
                pl.BlockSpec((tokens, width), lambda j, _: (0, jnp.minimum(j, 2))),
            ]
            + [fixed(value.shape) for value in sums],
            out_specs=[spec, spec],
        ),
        out_shape=[shape, shape],
    )(here, x, grad_qkv, *sums)


def gathered(shard):
    return lax.all_gather(shard, BOTH, axis=0, tiled=True)


def scattered(whole):
    return lax.psum_scatter(whole, BOTH, scatter_dimension=0, tiled=True)


def shared_contrast(unit, flags, log_temp, pooled):
    anchors, partners = unit[:28], unit[32:60]
    inv_temp = jnp.exp(-log_temp[0])
    anchors_all, partners_all = gathered(anchors), gathered(partners)
    column_ok = gathered(flags.astype(LOW)).astype(FULL)
    held_total = jnp.sum(column_ok)
    logits = against(anchors, partners_all) * inv_temp
    logits = jnp.where(column_ok[None, :] > 0, logits, -1e30)
    sim_peak = jnp.max(logits, axis=-1, keepdims=True)
    sim_total = sim_peak + jnp.log(jnp.sum(jnp.exp(logits - sim_peak), axis=-1, keepdims=True))
    anchors_f = anchors.astype(FULL)
    partners_f = partners.astype(FULL)
    positive = jnp.sum(anchors_f * partners_f, axis=-1) * inv_temp
    row_weight = flags / held_total
    loss_part = jnp.sum(row_weight * (sim_total[:, 0] - positive))
    shares = jnp.exp(logits - sim_total) * row_weight[:, None]
    temp_part = jnp.sum(row_weight * positive) - jnp.sum(
        shares * jnp.where(column_ok[None, :] > 0, logits, 0.0)
    )
    grad_anchor = inv_temp * (
        jnp.dot(shares, partners_all.astype(FULL), precision=precise)
        - row_weight[:, None] * partners_f
    )
    totals_all = gathered(sim_total[:, 0])
    back = against(partners, anchors_all) * inv_temp
    back = jnp.where(flags[:, None] > 0, back, -1e30)
    back_shares = jnp.exp(back - totals_all[None, :]) * (column_ok / held_total)[None, :]
    grad_partner = inv_temp * (
        jnp.dot(back_shares, anchors_all.astype(FULL), precision=precise)
        - row_weight[:, None] * anchors_f
    )
    loss, temp_grad = lax.psum((loss_part, temp_part), BOTH)
    pad = ((0, 4), (0, 0))
    grad_unit = jnp.concatenate([jnp.pad(grad_anchor, pad), jnp.pad(grad_partner, pad)])
    return loss.reshape(1), temp_grad.reshape(1), pool_back(grad_unit, pooled)


def pack_kernel(here_ref, *refs):
    vectors, b_inner = refs[:9], refs[9]
    w_query, w_key, w_value, w_out, w_inner = refs[10:15]
    one, two, narrow, broad = refs[15:]
    index = place(here_ref[0], here_ref[1], here_ref[2], here_ref[3])
    rows, width = w_query.shape
    band = b_inner.shape[1]
    per_row = width // band
    one[0] = w_query[...]
    one[1] = w_key[...]
    one[2] = w_value[...]
    for j in range(w_inner.shape[1] // width):
        two[j] = w_inner[:, j * width : (j + 1) * width]
    two[4] = w_out[...]
    narrow[...] = jnp.zeros_like(narrow)
    broad[...] = jnp.zeros_like(broad)
    for f, vector in enumerate(vectors):
        narrow[f : f + 1, :rows] = vector[...].astype(FULL)
    broad[0:1, :band] = b_inner[...].astype(FULL)
    placed = pltpu.roll(narrow[...], rows * index, 1)
    line = pltpu.roll(broad[...], band * lax.rem(index, per_row), 1)[0:1]
    at = lax.broadcasted_iota(jnp.int32, placed.shape, 0) == 9 + index // per_row
    placed = jnp.where(at, line, placed)
    one[3] = placed.astype(LOW)


def pack(here, vectors, b_inner, weights):
    w_query, w_key, w_value, w_out, w_inner = weights
    rows, width = w_query.shape
    return call(
        pack_kernel,
        "pack",
        0,
        40 * rows * width,
        grid_spec=pltpu.PrefetchScalarGridSpec(
            num_scalar_prefetch=1,
            grid=(1,),
            in_specs=[fixed((1, rows))] * 9
            + [fixed((1, b_inner.shape[0]))]
            + [fixed(weight.shape) for weight in weights],
            out_specs=[fixed((4, rows, width)), fixed((w_inner.shape[1] // width + 1, rows, width))],
            scratch_shapes=[pltpu.VMEM((24, width), FULL), pltpu.VMEM((8, width), FULL)],
        ),
        out_shape=[
            shaped((4, rows, width), LOW),
            shaped((w_inner.shape[1] // width + 1, rows, width), LOW),
        ],
    )(
        here,
        *[vector[None] for vector in vectors],
        b_inner[None],
        *weights,
    )


def small_sums(start_sums, sums_qv, sums_one, sums_two, wide_sums):
    width = start_sums.shape[1]
    wide = wide_sums.shape[1] // width
    return start_sums + jnp.concatenate(
        [
            sums_qv[0:2],
            sums_one[2:3],
            sums_one[0:2],
            sums_two[0:3],
            jnp.zeros((1, width), FULL),
            wide_sums.reshape(wide, width),
            jnp.zeros((24 - 9 - wide, width), FULL),
        ]
    )


def paired_body(
    hidden_in, row_counts, buckets, lengths, keep_masks, out_cotangent, vectors, b_inner, weights,
    log_temp,
):
    w_query, w_key, w_value, w_attn_out, w_inner, w_outer, w_pool = weights
    slots, length, width = hidden_in.shape
    tokens = slots * length
    ff = w_inner.shape[1]
    wide = ff // width
    index = lax.axis_index(BOTH)
    here = jnp.stack(whereabouts()).astype(jnp.int32)
    flat = hidden_in.reshape(tokens, width)
    first, second, both = first_pairs(), second_pairs(), across_pairs()

    pack_one, pack_two = pack(here, vectors, b_inner, (w_query, w_key, w_value, w_attn_out, w_inner))
    pack_three = jnp.concatenate([w_outer.reshape(wide, -1, width), w_pool[None]])
    come = along_z(pack_one)
    pack_one, pack_two, come = together(pack_one, pack_two, come)

    one = [jnp.stack([pack_one] + come)]
    come = [send(one[0], route) for route in (first, second, both)]
    come_two = along_z(pack_two)
    segment, starts, held_slots = layout(row_counts, buckets, lengths, length)
    table = pick_table(starts, held_slots, length)
    flags = held_slots.astype(FULL).reshape(slots * 4)
    flag_row = jnp.pad(flags, (0, width - slots * 4))[None]
    one, come, pack_two, come_two, segment, table, flag_row = together(
        one, come, pack_two, come_two, segment, table, flag_row
    )

    one += come
    two = [jnp.stack([pack_two] + come_two)]
    one_other = over_cores(one)
    come_three = [send(pack_three, along_pairs(k)) for k in (1, 2)]
    one, one_other, pack_three = together(one, one_other, pack_three)

    come = [send(two[0], first), send(two[0], second)]
    qkv_weights, small = in_order(here, one + one_other, (3, 0))
    come_three[0], pack_three, small, column = together(
        come_three[0], pack_three, small, two[0]
    )

    come.append(send(column, both))
    come_three.append(send(pack_three, along_pairs(3)))
    qkv_weights = qkv_weights.reshape(3, width, width)
    biases = jnp.stack([small[0], jnp.zeros_like(small[0]), small[1]])[:, None]
    qkv, att, probs, here = attend(here, flat, qkv_weights, biases, segment)
    two, come, pack_three, come_three, here = together(two, come, pack_three, come_three, here)

    two += come
    two_other = over_cores(two)
    three = [jnp.stack([pack_three] + come_three)]
    come = [send(three[0], route) for route in (first, second, both)]
    two, two_other, here = together(two, two_other, here)

    inner_weights, out_weight = in_order(here, two + two_other, (wide, 1))
    inner_weights = inner_weights.reshape(wide, width, width)
    out_weight = out_weight.reshape(width, width)
    n1, nh1, rs1, active, slope, picked, picked_att, picked_rs, start_active, start_slope = (
        inner_forward(
            att, hidden_in, keep_masks, out_weight, inner_weights, small, starts, held_slots
        )
    )
    three, come, start_active = together(three, come, start_active)

    three += come
    outer_weights, pool_weight = in_order(here, three + over_cores(three), (-wide, 1))
    outer_weights = outer_weights.reshape(ff, width)
    pool_weight = pool_weight.reshape(width, width)
    start_nh2, start_rs2, cls, pooled, unit = start_forward(
        start_active, picked, outer_weights, small, pool_weight, flag_row
    )
    unit, here = together(unit, here)

    come = along_z(unit)
    result, grad_outer, second_flow, sums_two, here = outer_both(
        here, active, n1, keep_masks, out_cotangent, segment, outer_weights, small
    )
    unit, come, here = together(unit, come, here)

    own = [jnp.stack([unit] + come)]
    come = [send(own[0], route) for route in (first, second, both)]
    grad_inner, grad_branch, grad_att, base, sums_one, wide_sums, here = inner_backward(
        here, grad_outer, slope, second_flow, nh1, rs1, keep_masks, outer_weights, inner_weights,
        out_weight, small,
    )
    own, come, here = together(own, come, here)

    own += come
    scalars, grad_pre, start_outer, start_second, start_sums = contrast(
        here, own + over_cores(own), log_temp, pooled, pool_weight, start_nh2, start_rs2, picked,
        small,
    )
    loss, temp_grad = scalars[0, :1], scalars[1, :1]

    outer_kept, outer_away = outer_weight(
        here, active, grad_outer, start_active, start_outer, cls, grad_pre
    )
    come = send(outer_away, core_pairs())
    outer_kept, start_outer = together(outer_kept, start_outer)
    start_inner, start_branch, start_base, start_att, start_sums = start_backward(
        start_outer, start_second, start_sums, picked, picked_rs, start_slope, small,
        outer_weights, inner_weights, out_weight,
    )
    come, outer_kept, start_inner, start_att, start_base, start_sums = together(
        come, outer_kept, start_inner, start_att, start_base, start_sums
    )

    outer_go, outer_own = halves_of(outer_kept, come)
    come = send(outer_go, second)
    outer_own, here = together(outer_own, here)
    inner_kept, inner_away = inner_weight(
        here, n1, grad_inner, picked, start_inner, att, grad_branch, picked_att, start_branch
    )
    outer_own, come, inner_kept, inner_away = together(outer_own, come, inner_kept, inner_away)

    come_inner = send(inner_away, core_pairs())
    outer_go, outer_own = quarters_of(outer_own, come)
    come = send(outer_go, first)
    inner_kept, come_inner, outer_own, come = together(inner_kept, come_inner, outer_own, come)

    inner_go, inner_own = halves_of(inner_kept, come_inner)
    come_inner = send(inner_go, second)
    parts_outer = over_z(add_low(outer_own, come))
    inner_own, start_att = together(inner_own, start_att)
    grad_qkv, sums_qv = attend_backward(grad_att, start_att, table, qkv, probs)
    attend_kept, attend_away = attend_weight(
        here, flat, grad_qkv, (start_sums, sums_qv, sums_one, sums_two, wide_sums)
    )
    parts_outer, inner_own, come_inner, attend_kept, attend_away = together(
        parts_outer, inner_own, come_inner, attend_kept, attend_away
    )

    come_attend = send(attend_away, core_pairs())
    inner_go, inner_own = quarters_of(inner_own, come_inner)
    come_inner = send(inner_go, first)
    attend_kept, come_attend, inner_own, here = together(
        attend_kept, come_attend, inner_own, here
    )

    attend_go, attend_own = halves_of(attend_kept, come_attend)
    come_attend = send(attend_go, second)
    attend_own, start_base, here = together(attend_own, start_base, here)
    input_grad, here = input_gradient(here, base, start_base, table, grad_qkv, qkv_weights)
    inner_own, come_inner, here = together(inner_own, come_inner, here)

    parts_inner = over_z(add_low(inner_own, come_inner))
    outer_part, pool_part = finish(here, parts_outer, inner=wide, tall=True)
    attend_own, come_attend, parts_inner[1], parts_inner[3], outer_part = together(
        attend_own, come_attend, parts_inner[1], parts_inner[3], outer_part
    )

    attend_go, attend_own = quarters_of(attend_own, come_attend)
    come_attend = send(attend_go, first)
    attend_own, come_attend = together(attend_own, come_attend)
    parts_attend = over_z(add_low(attend_own, come_attend))
    inner_part, out_part = finish(here, parts_inner, inner=wide)
    query_part, key_part, value_part, own_small, inner_bias_part = finish(
        here, parts_attend, vectors=9, band=b_inner.shape[0]
    )
    input_grad = input_grad.reshape(hidden_in.shape)
    inner_bias_part = inner_bias_part[0]
    parts = [query_part, key_part, value_part, out_part]
    small_parts = [own_small[i] for i in range(9)]
    return (
        loss,
        result,
        input_grad,
        parts[0],
        small_parts[0],
        parts[1],
        parts[2],
        small_parts[1],
        parts[3],
        small_parts[2],
        small_parts[3],
        small_parts[4],
        inner_part,
        inner_bias_part,
        outer_part,
        small_parts[5],
        small_parts[6],
        small_parts[7],
        pool_part,
        small_parts[8],
        temp_grad,
    )


def body(
    hidden_in,
    row_counts,
    buckets,
    lengths,
    keep_masks,
    out_cotangent,
    w_query,
    b_query,
    w_key,
    w_value,
    b_value,
    w_attn_out,
    b_attn_out,
    norm1_gain,
    norm1_bias,
    w_inner,
    b_inner,
    w_outer,
    b_outer,
    norm2_gain,
    norm2_bias,
    w_pool,
    b_pool,
    log_temp,
):
    slots, length, width = hidden_in.shape
    tokens = slots * length
    ff = w_inner.shape[1]
    wide = ff // width
    index = lax.axis_index(BOTH)
    here = jnp.stack(whereabouts()).astype(jnp.int32)
    vectors = (
        b_query,
        b_value,
        b_attn_out,
        norm1_gain,
        norm1_bias,
        b_outer,
        norm2_gain,
        norm2_bias,
        b_pool,
    )
    if paired():
        return paired_body(
            hidden_in, row_counts, buckets, lengths, keep_masks, out_cotangent, vectors, b_inner,
            (w_query, w_key, w_value, w_attn_out, w_inner, w_outer, w_pool), log_temp,
        )
    qkv_weights = jnp.stack([gathered(w) for w in (w_query, w_key, w_value)])
    out_weight = gathered(w_attn_out)
    rows = [gathered(v)[None] for v in vectors]
    rows.append(gathered(b_inner).reshape(wide, width))
    rows.append(jnp.zeros((24 - 9 - wide, width), LOW))
    small = jnp.concatenate(rows).astype(FULL)
    inner_weights = gathered(w_inner).reshape(width, wide, width).transpose(1, 0, 2)
    outer_weights = gathered(w_outer)
    pool_weight = gathered(w_pool)

    segment, starts, held_slots = layout(row_counts, buckets, lengths, length)
    table = pick_table(starts, held_slots, length)
    flags = held_slots.astype(FULL).reshape(slots * 4)
    flag_row = jnp.pad(flags, (0, width - slots * 4))[None]

    flat = hidden_in.reshape(tokens, width)
    biases = jnp.stack([small[0], jnp.zeros_like(small[0]), small[1]])[:, None]
    qkv, att, probs, _ = attend(here, flat, qkv_weights, biases, segment)
    n1, nh1, rs1, active, slope, picked, picked_att, picked_rs, start_active, start_slope = (
        inner_forward(
            att, hidden_in, keep_masks, out_weight, inner_weights, small, starts, held_slots
        )
    )
    start_nh2, start_rs2, cls, pooled, unit = start_forward(
        start_active, picked, outer_weights, small, pool_weight, flag_row
    )
    result, grad_outer, second_flow, sums_two, _ = outer_both(
        here, active, n1, keep_masks, out_cotangent, segment, outer_weights, small
    )
    loss, temp_grad, grad_pre = shared_contrast(unit[0], flags, log_temp, pooled)
    start_outer, start_second, start_sums = start_outer_back(
        grad_pre, pool_weight, start_nh2, start_rs2[:, :1], picked[3], small
    )
    start_inner, start_branch, start_base, start_att, start_sums = start_backward(
        start_outer, start_second, start_sums, picked, picked_rs, start_slope, small,
        outer_weights, inner_weights, out_weight,
    )
    grad_inner, grad_branch, grad_att, base, sums_one, wide_sums, _ = inner_backward(
        here, grad_outer, slope, second_flow, nh1, rs1, keep_masks, outer_weights, inner_weights,
        out_weight, small,
    )
    grad_qkv, sums_qv = attend_backward(grad_att, start_att, table, qkv, probs)
    grad_small = small_sums(start_sums, sums_qv, sums_one, sums_two, wide_sums)
    input_grad, _ = input_gradient(here, base, start_base, table, grad_qkv, qkv_weights)
    input_grad = input_grad.reshape(hidden_in.shape)
    parts = [scattered(across(flat, grad_qkv[:, j * width : (j + 1) * width])) for j in range(3)]
    parts.append(scattered(across(att, grad_branch) + across(picked_att, start_branch)))
    small_parts = [scattered(grad_small[i]) for i in range(9)]
    inner_bias_part = scattered(grad_small[9 : 9 + wide].reshape(ff))
    outer_part = scattered(across(active, grad_outer) + across(start_active, start_outer))
    inner_part = scattered(across(n1, grad_inner) + across(picked[0], start_inner))
    pool_part = scattered(across(cls, grad_pre))
    return (
        loss,
        result,
        input_grad,
        parts[0],
        small_parts[0],
        parts[1],
        parts[2],
        small_parts[1],
        parts[3],
        small_parts[2],
        small_parts[3],
        small_parts[4],
        inner_part,
        inner_bias_part,
        outer_part,
        small_parts[5],
        small_parts[6],
        small_parts[7],
        pool_part,
        small_parts[8],
        temp_grad,
    )


def solution(mesh):
    outer, inner = mesh.shape["dp"], mesh.shape["fsdp"]
    sizes = (4, 2, 2, 2) if (outer, inner) == (16, 2) else (outer, 1, 1, inner)
    mesh = jax.sharding.Mesh(mesh.devices.reshape(sizes), BOTH)
    in_specs = (
        P(BOTH, None, None),
        P(BOTH),
        P(BOTH),
        P(BOTH, None),
        P(None, None, BOTH, None, None),
        P(None, BOTH, None, None),
        P(BOTH, None),
        P(BOTH),
        P(BOTH, None),
        P(BOTH, None),
        P(BOTH),
        P(BOTH, None),
        P(BOTH),
        P(BOTH),
        P(BOTH),
        P(BOTH, None),
        P(BOTH),
        P(BOTH, None),
        P(BOTH),
        P(BOTH),
        P(BOTH),
        P(BOTH, None),
        P(BOTH),
        P(),
    )
    out_specs = (
        P(),
        P(None, BOTH, None, None),
        P(BOTH, None, None),
        P(BOTH, None),
        P(BOTH),
        P(BOTH, None),
        P(BOTH, None),
        P(BOTH),
        P(BOTH, None),
        P(BOTH),
        P(BOTH),
        P(BOTH),
        P(BOTH, None),
        P(BOTH),
        P(BOTH, None),
        P(BOTH),
        P(BOTH),
        P(BOTH),
        P(BOTH, None),
        P(BOTH),
        P(),
    )
    return jax.shard_map(body, mesh=mesh, in_specs=in_specs, out_specs=out_specs, check_vma=False)
```

```python
import functools

import jax
import jax.numpy as jnp
from jax import lax
from jax.experimental import pallas as pl
from jax.experimental.pallas import tpu as pltpu
from jax.sharding import PartitionSpec as P

HEADS = 12
BOTH = ("z", "x", "c", "y")
LOW = jnp.bfloat16
FULL = jnp.float32

precise = lax.Precision.HIGHEST
keep_scale = 1.0 / 0.9
inv_root_two = 0.7071067811865476
inv_root_tau = 0.3989422804014327
eps = 1e-06


def matmul(left, right):
    return lax.dot_general(left, right, (((1,), (0,)), ((), ())), preferred_element_type=FULL)


def against(left, right):
    return lax.dot_general(left, right, (((1,), (1,)), ((), ())), preferred_element_type=FULL)


def across(left, right):
    return lax.dot_general(left, right, (((0,), (0,)), ((), ())), preferred_element_type=FULL)


def paired():
    return tuple(lax.axis_size(axis) for axis in BOTH) == (4, 2, 2, 2)


def place(z, x, c, y):
    return ((z * 2 + x) * 2 + c) * 2 + y


def pairs(move):
    every = [(z, x, c, y) for z in range(4) for x in range(2) for c in range(2) for y in range(2)]
    return [(place(*t), place(*move(*t))) for t in every]


def first_pairs():
    return pairs(lambda z, x, c, y: (z, 1 - x, c, y) if c == 0 else (z, x, c, 1 - y))


def second_pairs():
    return pairs(lambda z, x, c, y: (z, x, c, 1 - y) if c == 0 else (z, 1 - x, c, y))


def across_pairs():
    return pairs(lambda z, x, c, y: (z, 1 - x, c, 1 - y))


def core_pairs():
    return pairs(lambda z, x, c, y: (z, x, 1 - c, y))


def along_pairs(k):
    return pairs(lambda z, x, c, y: ((z + k) % 4, x, c, y))


def whereabouts():
    index = lax.axis_index(BOTH)
    return index // 8, index // 4 % 2, index // 2 % 2, index % 2


def send(block, route):
    return lax.ppermute(block, BOTH, route)


def together(*values):
    return lax.optimization_barrier(values)


def along_z(shard):
    return [send(shard, along_pairs(k)) for k in (1, 2, 3)]


def over_cores(own):
    return [send(block, core_pairs()) for block in own]


def where_from(here, core, p1, p2):
    first_x = core == 0
    on_x = jnp.where(first_x, p1, p2)
    on_y = jnp.where(first_x, p2, p1)
    return here[1] ^ on_x, here[3] ^ on_y


def order_kernel(parts, here_ref, *refs):
    blocks, outs = refs[:8], refs[8:]
    here = [here_ref[i] for i in range(4)]
    total = None
    for i in range(8):
        core = here[2] if i < 4 else 1 - here[2]
        x, y = where_from(here, core, i % 2, i // 2 % 2)
        for k in range(4):
            z = lax.rem(here[0] + 4 - k, 4)
            device = place(z, x, core, y)
            item = 0
            for count, out in zip(parts, outs):
                if count == 0:
                    value = blocks[i][k, item].astype(FULL)
                    total = value if total is None else total + value
                    item += 1
                for n in range(count):
                    out[n, device] = blocks[i][k, item]
                    item += 1
                for n in range(-count):
                    out[device, n] = blocks[i][k, item]
                    item += 1
    for count, out in zip(parts, outs):
        if count == 0:
            out[...] = total


def in_order(here, blocks, parts):
    items, rows, width = blocks[0].shape[1:]
    whole = pl.BlockSpec(memory_space=pltpu.VMEM)
    return call(
        functools.partial(order_kernel, parts),
        "order",
        0,
        128 * items * rows * width,
        out_shape=[
            shaped((rows, width), FULL)
            if count == 0
            else shaped((count, 32, rows, width) if count > 0 else (32, -count, rows, width), LOW)
            for count in parts
        ],
        grid_spec=pltpu.PrefetchScalarGridSpec(
            num_scalar_prefetch=1, grid=(), in_specs=[whole] * 8, out_specs=[whole] * len(parts)
        ),
    )(here, *blocks)


def add_low(left, right):
    return (left.astype(FULL) + right.astype(FULL)).astype(LOW)


def halves_of(kept, come):
    return add_low(kept[2:], come[2:]), add_low(kept[:2], come[:2])


def quarters_of(own, come):
    return add_low(own[1], come[1]), add_low(own[0], come[0])


def add_all(own, come):
    return sum([part.astype(FULL) for part in come], own.astype(FULL)).astype(LOW)


def over_z(column):
    z = lax.axis_index("z")
    own = lax.dynamic_index_in_dim(column, z, 0, keepdims=False)
    away = [lax.dynamic_index_in_dim(column, (z + k) % 4, 0, keepdims=False) for k in (1, 2, 3)]
    return [own] + [send(part, along_pairs(k)) for k, part in zip((1, 2, 3), away)]


def finish_kernel(inner, vectors, *refs):
    parts, outs = refs[1:5], refs[5:]
    here_ref = refs[0]
    rows, width = parts[0].shape[1:]

    def total(n):
        return sum(part[n].astype(FULL) for part in parts)

    for n in range(inner):
        if outs[0].shape[0] == rows:
            outs[0][:, n * width : (n + 1) * width] = total(n)
        else:
            outs[0][n * rows : (n + 1) * rows] = total(n)
    outs = outs[1:] if inner else outs
    plain = parts[0].shape[0] - inner - (1 if vectors else 0)
    for n in range(plain):
        outs[n][...] = total(inner + n)
    if vectors:
        index = place(here_ref[0], here_ref[1], here_ref[2], here_ref[3])
        value = total(inner + plain)
        piece = width // 32
        band = outs[plain + 1].shape[1]
        per_row = width // band
        outs[plain][...] = pltpu.roll(value, width - piece * index, 1)[: outs[plain].shape[0], :piece]
        at = lax.broadcasted_iota(jnp.int32, value.shape, 0) == 9 + index // per_row
        line = jnp.sum(jnp.where(at, value, 0.0), axis=0, keepdims=True)
        line = jnp.broadcast_to(line, (8, width))
        line = pltpu.roll(line, width - band * lax.rem(index, per_row), 1)
        outs[plain + 1][...] = line[0:1, :band]


def finish(here, parts, inner=0, vectors=0, band=0, tall=False):
    items, rows, width = parts[0].shape
    plain = items - inner - (1 if vectors else 0)
    shapes = [(inner * rows, width) if tall else (rows, inner * width)] if inner else []
    shapes += [(rows, width)] * plain
    shapes += [(vectors, width // 32), (1, band)] if vectors else []
    return call(
        functools.partial(finish_kernel, inner, vectors),
        "finish",
        0,
        12 * items * rows * width,
        grid_spec=pltpu.PrefetchScalarGridSpec(
            num_scalar_prefetch=1,
            grid=(1,),
            in_specs=[fixed(parts[0].shape)] * 4,
            out_specs=[fixed(shape) for shape in shapes],
        ),
        out_shape=[shaped(shape, FULL) for shape in shapes],
    )(here, *parts)


def layout(row_counts, buckets, lengths, row_len):
    slot_count = buckets.shape[0]
    live_rows = jnp.arange(slot_count, dtype=jnp.int32) < row_counts[0]
    sent_count = jnp.right_shift(jnp.int32(4), buckets)
    slot_ids = jnp.arange(4, dtype=jnp.int32)
    held_slots = (slot_ids[None, :] < sent_count[:, None]) & live_rows[:, None]
    sizes_used = jnp.where(held_slots, lengths, 0)
    finish = jnp.cumsum(sizes_used, axis=1, dtype=jnp.int32)
    starts = finish - sizes_used
    places = jnp.arange(row_len, dtype=jnp.int32)
    segment = jnp.sum((places[None, :, None] >= finish[:, None, :]).astype(jnp.int32), axis=2)
    return segment, starts, held_slots


def pick_table(starts, held_slots, row_len):
    rows = starts.shape[0]
    slot = jnp.arange(64, dtype=jnp.int32)
    view, row, k = slot // 32, slot % 32 // 4, slot % 4
    row = jnp.minimum(row, rows - 1)
    real = slot % 32 < rows * 4
    start = starts[row, k]
    held = held_slots[row, k] & real
    token = jnp.arange(2 * row_len, dtype=jnp.int32)
    hit = held[:, None] & (token[None, :] == (view * row_len + start)[:, None])
    here = jnp.arange(rows, dtype=jnp.int32)[:, None] == row[None, :]
    return (here[:, :, None] & hit[None]).astype(LOW)


rooms = {"pack": 60, "attend": 60, "inner_forward": 60, "outer_both": 60, "inner_backward": 60}


def call(kernel, name, flops, moved, **kwargs):
    room = rooms.get(name, 36)
    return pl.pallas_call(
        kernel,
        name=name,
        compiler_params=pltpu.CompilerParams(vmem_limit_bytes=room * 2**20),
        cost_estimate=pl.CostEstimate(flops=flops // 10, transcendentals=0, bytes_accessed=moved // 10),
        **kwargs,
    )


def scalars_spec():
    return pl.BlockSpec(memory_space=pltpu.SMEM)


def hand_on(here, mark):
    for n in range(4):
        mark[n] = here[n]


def fixed(shape):
    zeros = (0,) * len(shape)
    return pl.BlockSpec(shape, lambda *_: zeros)


def shaped(shape, kind):
    return jax.ShapeDtypeStruct(shape, kind)


def halves(pair, even):
    zero = jnp.zeros_like(pair)
    return jnp.concatenate([jnp.where(even, pair, zero), jnp.where(even, zero, pair)], axis=0)


def attend_kernel(here, x, weights, biases, seg_row, seg_col, qkv, out, probs, mark):
    hand_on(here, mark)
    length, width = out.shape
    for j in range(3):
        value = matmul(x[...], weights[j]) + biases[j]
        qkv[:, j * width : (j + 1) * width] = value.astype(LOW)
    even = lax.broadcasted_iota(jnp.int32, (length, 128), 1) < 64
    same = seg_col[0] == seg_row[0]
    same = jnp.concatenate([same, same], axis=0)
    for p in range(width // 128):
        at = p * 128
        query = halves(qkv[:, at : at + 128], even)
        key = qkv[:, width + at : width + at + 128]
        value = qkv[:, 2 * width + at : 2 * width + at + 128]
        scores = jnp.where(same, against(query, key) * 0.125, -1e30)
        peak = jnp.max(scores, axis=-1, keepdims=True)
        lifted = jnp.exp(scores - peak)
        share = lifted * (1.0 / jnp.sum(lifted, axis=-1, keepdims=True))
        share = share.astype(LOW)
        probs[0, p] = share
        both = matmul(share, value)
        out[:, at : at + 128] = jnp.where(even, both[:length], both[length:]).astype(LOW)


def attend(here, flat, weights, biases, segment):
    slots, length = segment.shape
    tokens, width = flat.shape
    pairs_of = width // 128
    return call(
        attend_kernel,
        "attend",
        6 * tokens * width * width + 8 * tokens * length * width,
        16 * tokens * width,
        grid=(slots,),
        in_specs=[
            scalars_spec(),
            pl.BlockSpec((length, width), lambda r: (r, 0)),
            fixed(weights.shape),
            fixed(biases.shape),
            pl.BlockSpec((1, 1, length), lambda r: (r, 0, 0)),
            pl.BlockSpec((1, length, 1), lambda r: (r, 0, 0)),
        ],
        out_specs=[
            pl.BlockSpec((length, 3 * width), lambda r: (r, 0)),
            pl.BlockSpec((length, width), lambda r: (r, 0)),
            pl.BlockSpec((1, pairs_of, 2 * length, length), lambda r: (r, 0, 0, 0)),
            scalars_spec(),
        ],
        out_shape=[
            shaped((tokens, 3 * width), LOW),
            shaped((tokens, width), LOW),
            shaped((slots, pairs_of, 2 * length, length), LOW),
            shaped((4,), jnp.int32),
        ],
    )(here, flat, weights, biases, segment[:, None, :], segment[:, :, None])


def normal(hidden):
    centre = jnp.mean(hidden, axis=-1, keepdims=True)
    offset = hidden - centre
    spread_of = jnp.mean(offset * offset, axis=-1, keepdims=True)
    rscale = lax.rsqrt(spread_of + eps)
    return offset * rscale, rscale


def normal_back(grad_norm, normed, rscale):
    mean_grad = jnp.mean(grad_norm, axis=-1, keepdims=True)
    mean_cross = jnp.mean(grad_norm * normed, axis=-1, keepdims=True)
    return rscale * (grad_norm - mean_grad - normed * mean_cross)


def gelu_parts(inner):
    phi = 0.5 * (1.0 + lax.erf(inner * inv_root_two))
    return inner * phi, phi + inner * jnp.exp(-0.5 * inner * inner) * inv_root_tau


def inner_kernel(
    starts, held, att, x, keep, w_out, w_inner, small,
    n1, nh1, rs1, active, slope, picked, picked_att, picked_rs, picked_active, picked_slope,
    rows_one, rows_unit, rows_att, rows_scale, near, near_att, near_rs,
):
    row = pl.program_id(0)
    length, width = att.shape
    branch = matmul(att[...], w_out[...]) + small[2:3]
    base = x[0].astype(FULL)
    keeps = keep[:, 0, 0].astype(FULL) * keep_scale
    first = jnp.concatenate([base + branch * keeps[0], base + branch * keeps[1]], axis=0)
    normed, rscale = normal(first)
    nh1[...] = normed.astype(LOW)
    rs1[...] = rscale
    rows_unit[...] = normed
    rows_scale[...] = jnp.broadcast_to(rscale, rows_scale.shape)
    rows_att[...] = att[...].astype(FULL)
    whole_in = normed * small[3:4] + small[4:5]
    rows_one[...] = whole_in
    inner_in = whole_in.astype(LOW)
    n1[...] = inner_in
    step = 256
    for j in range(w_inner.shape[0]):
        for at in range(0, width, step):
            inner = matmul(inner_in, w_inner[j, :, at : at + step])
            inner = inner + small[9 + j : 10 + j, at : at + step]
            value, grad = gelu_parts(inner)
            active[:, j * width + at : j * width + at + step] = value.astype(LOW)
            slope[:, j * width + at : j * width + at + step] = grad.astype(LOW)

    @pl.when(row == 0)
    def _():
        near[...] = jnp.zeros_like(near)
        near_att[...] = jnp.zeros_like(near_att)
        near_rs[...] = jnp.zeros_like(near_rs)

    for k in range(4):
        slot = 4 * row + k

        @pl.when(held[row, k] > 0)
        def _():
            start = starts[row, k]
            near_att[pl.ds(slot, 1)] = rows_att[pl.ds(start, 1)]
            for v in range(2):
                to = pl.ds(32 * v + slot, 1)
                near[0, to] = rows_one[pl.ds(length * v + start, 1)]
                near[1, to] = rows_unit[pl.ds(length * v + start, 1)]
                for n in range(2):
                    near[2 + n, to] = keep[v, n, 0, pl.ds(start, 1)].astype(FULL)
                near_rs[to] = rows_scale[pl.ds(length * v + start, 1)]

    @pl.when(row == pl.num_programs(0) - 1)
    def _():
        picked[...] = near[:, :64].astype(LOW)
        picked_att[...] = near_att[:32].astype(LOW)
        picked_rs[...] = near_rs[:64]
        begin = near[0, :64].astype(LOW)
        for j in range(w_inner.shape[0]):
            inner = matmul(begin, w_inner[j]) + small[9 + j : 10 + j]
            value, grad = gelu_parts(inner)
            picked_active[:, j * width : (j + 1) * width] = value.astype(LOW)
            picked_slope[:, j * width : (j + 1) * width] = grad.astype(LOW)


def inner_forward(att, hidden, keep_masks, w_out, w_inner, small, starts, held_slots):
    slots, length, width = hidden.shape
    ff = w_inner.shape[0] * width
    two = 2 * length
    return call(
        inner_kernel,
        "inner_forward",
        2 * slots * two * width * ff,
        slots * two * ff * 5,
        grid_spec=pltpu.PrefetchScalarGridSpec(
            num_scalar_prefetch=2,
            grid=(slots,),
            in_specs=[
                pl.BlockSpec((length, width), lambda r, *_: (r, 0)),
                pl.BlockSpec((1, length, width), lambda r, *_: (r, 0, 0)),
                pl.BlockSpec((2, 2, 1, length, width), lambda r, *_: (0, 0, r, 0, 0)),
                fixed((width, width)),
                fixed(w_inner.shape),
                fixed(small.shape),
            ],
            out_specs=[
                pl.BlockSpec((two, width), lambda r, *_: (r, 0)),
                pl.BlockSpec((two, width), lambda r, *_: (r, 0)),
                pl.BlockSpec((two, 1), lambda r, *_: (r, 0)),
                pl.BlockSpec((two, ff), lambda r, *_: (r, 0)),
                pl.BlockSpec((two, ff), lambda r, *_: (r, 0)),
                fixed((4, 64, width)),
                fixed((32, width)),
                fixed((64, 128)),
                fixed((64, ff)),
                fixed((64, ff)),
            ],
            scratch_shapes=[
                pltpu.VMEM((two, width), FULL),
                pltpu.VMEM((two, width), FULL),
                pltpu.VMEM((length, width), FULL),
                pltpu.VMEM((two, 128), FULL),
                pltpu.VMEM((4, 72, width), FULL),
                pltpu.VMEM((40, width), FULL),
                pltpu.VMEM((72, 128), FULL),
            ],
        ),
        out_shape=[
            shaped((slots * two, width), LOW),
            shaped((slots * two, width), LOW),
            shaped((slots * two, 1), FULL),
            shaped((slots * two, ff), LOW),
            shaped((slots * two, ff), LOW),
            shaped((4, 64, width), LOW),
            shaped((32, width), LOW),
            shaped((64, 128), FULL),
            shaped((64, ff), LOW),
            shaped((64, ff), LOW),
        ],
    )(starts, held_slots.astype(jnp.int32), att, hidden, keep_masks, w_out, w_inner, small)


def start_kernel(active, picked, w_outer, small, w_pool, flags, nh2, rs2, cls, pooled, unit):
    outer = matmul(active[...], w_outer[...]) + small[5:6]
    second = picked[0].astype(FULL) + outer * (picked[3].astype(FULL) * keep_scale)
    normed, rscale = normal(second)
    nh2[...] = normed.astype(LOW)
    rs2[...] = jnp.broadcast_to(rscale, rs2.shape)
    out = (normed * small[6:7] + small[7:8]).astype(LOW)
    cls[...] = out
    squashed = jnp.tanh(matmul(out, w_pool[...]) + small[8:9])
    pooled[...] = squashed
    scale = lax.rsqrt(jnp.sum(squashed * squashed, axis=-1, keepdims=True) + eps)
    ones = (squashed * scale).astype(LOW).astype(FULL)
    slot = lax.broadcasted_iota(jnp.int32, ones.shape, 0)
    unit[0] = jnp.where(slot == 28, flags[...], ones).astype(LOW)


def start_forward(active, picked, w_outer, small, w_pool, flags):
    ff, width = w_outer.shape
    return call(
        start_kernel,
        "start_forward",
        128 * width * ff,
        2 * width * ff,
        out_shape=[
            shaped((64, width), LOW),
            shaped((64, 128), FULL),
            shaped((64, width), LOW),
            shaped((64, width), FULL),
            shaped((1, 64, width), LOW),
        ],
    )(active, picked, w_outer, small, w_pool, flags)


def outer_kernel(
    here, active, n1, keep, cot, segment, w_outer, small, result, grad_outer, second_flow, sums, mark
):
    hand_on(here, mark)
    row = pl.program_id(0)
    length = n1.shape[0] // 2
    keeps = keep[:, 0, 0].astype(FULL) * keep_scale
    keeps = jnp.concatenate([keeps[0], keeps[1]], axis=0)
    outer = matmul(active[...], w_outer[...]) + small[5:6]
    second = n1[...].astype(FULL) + outer * keeps
    normed, rscale = normal(second)
    out = (normed * small[6:7] + small[7:8]).astype(LOW)
    result[0, 0] = out[:length]
    result[1, 0] = out[length:]
    flow = jnp.concatenate([cot[0, 0], cot[1, 0]], axis=0).astype(FULL)
    ok = (segment[0] < 4).astype(FULL)
    grad_out = flow * jnp.concatenate([ok, ok], axis=0)
    grad_second = normal_back(grad_out * small[6:7], normed, rscale)
    low = (grad_second * keeps).astype(LOW)
    grad_outer[...] = low
    second_flow[...] = grad_second.astype(LOW)

    @pl.when(row == 0)
    def _():
        sums[...] = jnp.zeros_like(sums)

    sums[0:1] += jnp.sum(low.astype(FULL), axis=0, keepdims=True)
    sums[1:2] += jnp.sum(grad_out * normed, axis=0, keepdims=True)
    sums[2:3] += jnp.sum(grad_out, axis=0, keepdims=True)


def outer_both(here, active, n1, keep_masks, cotangent, segment, w_outer, small):
    tokens, ff = active.shape
    width = n1.shape[1]
    slots = keep_masks.shape[2]
    length = keep_masks.shape[3]
    two = 2 * length
    return call(
        outer_kernel,
        "outer_both",
        2 * tokens * width * ff,
        2 * tokens * ff,
        grid=(slots,),
        in_specs=[
            scalars_spec(),
            pl.BlockSpec((two, ff), lambda r: (r, 0)),
            pl.BlockSpec((two, width), lambda r: (r, 0)),
            pl.BlockSpec((2, 1, 1, length, width), lambda r: (0, 1, r, 0, 0)),
            pl.BlockSpec((2, 1, length, width), lambda r: (0, r, 0, 0)),
            pl.BlockSpec((1, length, 1), lambda r: (r, 0, 0)),
            fixed((ff, width)),
            fixed(small.shape),
        ],
        out_specs=[
            pl.BlockSpec((2, 1, length, width), lambda r: (0, r, 0, 0)),
            pl.BlockSpec((two, width), lambda r: (r, 0)),
            pl.BlockSpec((two, width), lambda r: (r, 0)),
            fixed((8, width)),
            scalars_spec(),
        ],
        out_shape=[
            shaped((2, slots, length, width), LOW),
            shaped((tokens, width), LOW),
            shaped((tokens, width), LOW),
            shaped((8, width), FULL),
            shaped((4,), jnp.int32),
        ],
    )(here, active, n1, keep_masks, cotangent, segment[:, :, None], w_outer, small)


def split_matmul(left, right):
    upper = left.astype(LOW)
    lower = (left - upper.astype(FULL)).astype(LOW)
    return matmul(upper, right) + matmul(lower, right)


def pool_back(grad_unit, squashed):
    scale = lax.rsqrt(jnp.sum(squashed * squashed, axis=-1, keepdims=True) + eps)
    grad_pooled = scale * grad_unit - squashed * (scale * scale * scale) * jnp.sum(
        squashed * grad_unit, axis=-1, keepdims=True
    )
    return (grad_pooled * (1.0 - squashed * squashed)).astype(LOW)


def loss_kernel(here_ref, *refs):
    blocks = refs[:8]
    (
        temp, pooled, w_pool, nh2, rs2, picked, small, scalars, grad_pre, start_outer, start_second,
        start_sums, anchors, partners, flat, sem,
    ) = refs[8:]
    here = [here_ref[i] for i in range(4)]
    copies = []
    for i in range(8):
        core = here[2] if i < 4 else 1 - here[2]
        x, y = where_from(here, core, i % 2, i // 2 % 2)
        for k in range(4):
            z = lax.rem(here[0] + 4 - k, 4)
            row = pl.multiple_of(place(z, x, core, y) * 32, 32)
            source = blocks[i].at[k, 0]
            for half, target in ((0, anchors), (1, partners)):
                copies.append(
                    pltpu.make_async_copy(
                        source.at[pl.ds(32 * half, 32)], target.at[pl.ds(row, 32)], sem
                    )
                )
    for copy in copies:
        copy.start()
    for copy in copies:
        copy.wait()
    count = anchors.shape[0]
    groups = count // 32
    inv_temp = jnp.exp(-temp[...])
    all_anchors = anchors[...]
    all_partners = partners[...]
    for d in range(groups):
        flat[d : d + 1] = anchors[d * 32 + 28 : d * 32 + 29, :128].astype(FULL)
    marks = flat[0:32].astype(LOW)
    slot = lax.broadcasted_iota(jnp.int32, (128, count), 0)
    lane = lax.broadcasted_iota(jnp.int32, (128, count), 1)
    wide = matmul(marks, (slot == lane % 32).astype(LOW))
    group = lax.broadcasted_iota(jnp.int32, (groups, count), 0)
    lane = lax.broadcasted_iota(jnp.int32, (groups, count), 1)
    row_ok = jnp.sum(jnp.where(group == lane // 32, wide, 0.0), axis=0, keepdims=True)
    tall_row = lax.broadcasted_iota(jnp.int32, (count, groups), 0)
    tall_group = lax.broadcasted_iota(jnp.int32, (count, groups), 1)
    tall = matmul((tall_row // 32 == tall_group).astype(LOW), marks)
    tall_row = lax.broadcasted_iota(jnp.int32, (count, 128), 0)
    tall_lane = lax.broadcasted_iota(jnp.int32, (count, 128), 1)
    column_ok = jnp.sum(jnp.where(tall_row % 32 == tall_lane, tall, 0.0), axis=1, keepdims=True)
    total_held = jnp.sum(row_ok, axis=1, keepdims=True)
    weight = row_ok / total_held
    raw = against(all_partners, all_anchors) * inv_temp
    positive = []
    eye = lax.broadcasted_iota(jnp.int32, (128, 128), 0)
    eye = eye == lax.broadcasted_iota(jnp.int32, (128, 128), 1)
    for at in range(0, count, 128):
        block = raw[at : at + 128, at : at + 128]
        positive.append(jnp.sum(jnp.where(eye, block, 0.0), axis=0, keepdims=True))
    positive = jnp.concatenate(positive, axis=1)
    masked = jnp.where(column_ok > 0, raw, -1e30)
    peak = jnp.max(masked, axis=0, keepdims=True)
    lifted = jnp.exp(masked - peak)
    whole = jnp.sum(lifted, axis=0, keepdims=True)
    sim_total = peak + jnp.log(whole)
    crossed = jnp.sum(lifted * masked, axis=0, keepdims=True) / whole
    loss = jnp.sum(weight * (sim_total - positive), axis=1, keepdims=True)
    temp_grad = jnp.sum(weight * (positive - crossed), axis=1, keepdims=True)
    line = lax.broadcasted_iota(jnp.int32, (8, 128), 0)
    scalars[...] = jnp.where(line == 0, loss, temp_grad)
    mine = place(here[0], here[1], here[2], here[3])
    first = pl.multiple_of(mine * 32, 32)
    my_anchors = anchors[pl.ds(first, 32)]
    my_partners = partners[pl.ds(first, 32)]
    tall_lane = lax.broadcasted_iota(jnp.int32, (32, 128), 1)
    tall_row = lax.broadcasted_iota(jnp.int32, (32, 128), 0)
    my_flags = flat[pl.ds(mine, 1)]
    my_ok = jnp.sum(jnp.where(tall_lane == tall_row, my_flags, 0.0), axis=1, keepdims=True)
    my_weight = my_ok / total_held
    back = against(my_partners, all_anchors) * inv_temp
    back_shares = jnp.exp(jnp.where(my_ok > 0, back, -1e30) - sim_total) * weight
    grad_partner = inv_temp * (
        split_matmul(back_shares, all_anchors) - my_weight * my_anchors.astype(FULL)
    )
    mine_masked = jnp.where(row_ok > 0, against(my_anchors, all_partners) * inv_temp, -1e30)
    peak = jnp.max(mine_masked, axis=1, keepdims=True)
    lifted = jnp.exp(mine_masked - peak)
    my_shares = lifted * (my_weight / jnp.sum(lifted, axis=1, keepdims=True))
    grad_anchor = inv_temp * (
        split_matmul(my_shares, all_partners) - my_weight * my_partners.astype(FULL)
    )
    grad_unit = jnp.concatenate([grad_anchor, grad_partner], axis=0)
    pre = pool_back(grad_unit, pooled[...])
    grad_pre[...] = pre
    start_outer[...], start_second[...], start_sums[...] = start_outer_back(
        pre, w_pool[...], nh2[...], rs2[:, :1], picked[3], small
    )


def contrast(here, blocks, log_temp, pooled, w_pool, nh2, rs2, picked, small):
    width = pooled.shape[1]
    count = 32 * 32
    whole = pl.BlockSpec(memory_space=pltpu.VMEM)
    return pl.pallas_call(
        loss_kernel,
        name="contrast",
        grid_spec=pltpu.PrefetchScalarGridSpec(
            num_scalar_prefetch=1,
            grid=(),
            in_specs=[pl.BlockSpec(memory_space=pl.ANY)] * 8 + [whole] * 7,
            out_specs=[whole] * 5,
            scratch_shapes=[
                pltpu.VMEM((count, width), LOW),
                pltpu.VMEM((count, width), LOW),
                pltpu.VMEM((40, 128), FULL),
                pltpu.SemaphoreType.DMA,
            ],
        ),
        out_shape=[
            shaped((8, 128), FULL),
            shaped((64, width), LOW),
            shaped((64, width), LOW),
            shaped((64, width), FULL),
            shaped((8, width), FULL),
        ],
        compiler_params=pltpu.CompilerParams(vmem_limit_bytes=36 * 2**20),
        cost_estimate=pl.CostEstimate(
            flops=2 * count * count * width, transcendentals=0, bytes_accessed=4 * count * width
        ),
    )(here, *blocks, log_temp.reshape(1, 1), pooled, w_pool, nh2, rs2, picked, small)


def start_back(outer, second, picked, rs1, slope, w_outer, w_inner, w_out, small):
    width = outer.shape[1]
    wide = w_inner.shape[0]
    inner = []
    grad_normed = second
    for j in range(wide):
        grad_active = against(outer, w_outer[j * width : (j + 1) * width])
        low = (grad_active * slope[:, j * width : (j + 1) * width].astype(FULL)).astype(LOW)
        inner.append(low)
        grad_normed = grad_normed + against(low, w_inner[j])
    unit_one = picked[1].astype(FULL)
    first = normal_back(grad_normed * small[3:4], unit_one, rs1)
    kept = first * (picked[2].astype(FULL) * keep_scale)
    branch = (kept[:32] + kept[32:]).astype(LOW)
    base = first[:32] + first[32:]
    att = against(branch, w_out).astype(LOW)
    sums = [down(branch), down(grad_normed * unit_one), down(grad_normed)]
    return inner, branch, base, att, sums, [down(low) for low in inner]


def down(value):
    return jnp.sum(value.astype(FULL), axis=0, keepdims=True)


def start_outer_back(grad_pre, w_pool, nh2, rs2, keeps, small):
    grad_out = against(grad_pre, w_pool)
    normed = nh2.astype(FULL)
    grad_second = normal_back(grad_out * small[6:7], normed, rs2)
    low = (grad_second * (keeps.astype(FULL) * keep_scale)).astype(LOW)
    sums = [down(low), down(grad_out * normed), down(grad_out), down(grad_pre)]
    sums.append(jnp.zeros((4, low.shape[1]), FULL))
    return low, grad_second, jnp.concatenate(sums)


def start_back_kernel(
    outer, second, old_sums, picked, rs1, slope, small, w_outer_hbm, w_inner_hbm, w_out_hbm,
    inner, branch, base, att, sums, w_outer, w_inner, w_out, sems,
):
    copies = [
        pltpu.make_async_copy(source, target, sems.at[n])
        for n, (source, target) in enumerate(
            ((w_outer_hbm, w_outer), (w_inner_hbm, w_inner), (w_out_hbm, w_out))
        )
    ]
    for copy in copies:
        copy.start()
    for copy in copies:
        copy.wait()
    out = start_back(
        outer[...], second[...], picked, rs1[:, :1], slope, w_outer, w_inner, w_out[...], small
    )
    width = outer.shape[1]
    for j, low in enumerate(out[0]):
        inner[:, j * width : (j + 1) * width] = low
    branch[...] = out[1]
    base[...] = out[2]
    att[...] = out[3]
    sums[0:2] = jnp.zeros((2, width), FULL)
    for n, value in enumerate(out[4]):
        sums[2 + n : 3 + n] = value
    sums[5:9] = old_sums[0:4]
    for j, value in enumerate(out[5]):
        sums[9 + j : 10 + j] = value
    sums[13:24] = jnp.zeros((11, width), FULL)


def start_backward(outer, second, old_sums, picked, rs1, slope, small, w_outer, w_inner, w_out):
    ff, width = w_outer.shape
    whole = pl.BlockSpec(memory_space=pltpu.VMEM)
    outside = pl.BlockSpec(memory_space=pl.ANY)
    return call(
        start_back_kernel,
        "start_backward",
        256 * width * ff,
        4 * width * ff,
        in_specs=[whole] * 7 + [outside] * 3,
        out_shape=[
            shaped((64, ff), LOW),
            shaped((32, width), LOW),
            shaped((32, width), FULL),
            shaped((32, width), LOW),
            shaped((24, width), FULL),
        ],
        scratch_shapes=[
            pltpu.VMEM(w_outer.shape, LOW),
            pltpu.VMEM(w_inner.shape, LOW),
            pltpu.VMEM(w_out.shape, LOW),
            pltpu.SemaphoreType.DMA((3,)),
        ],
    )(outer, second, old_sums, picked, rs1, slope, small, w_outer, w_inner, w_out)


def inner_back_kernel(
    here, grad_outer, slope, second, nh1, rs1, keep, w_outer, w_inner, w_out, small,
    grad_inner, grad_branch, grad_att, base, sums, wide_sums, mark,
):
    hand_on(here, mark)
    row = pl.program_id(0)
    length = grad_branch.shape[0]
    width = grad_branch.shape[1]
    step = 256

    @pl.when(row == 0)
    def _():
        sums[...] = jnp.zeros_like(sums)
        wide_sums[...] = jnp.zeros_like(wide_sums)

    low_outer = grad_outer[...]
    grad_normed = second[...].astype(FULL)
    for j in range(w_inner.shape[0]):
        for at in range(0, width, step):
            lane = j * width + at
            grad_active = against(low_outer, w_outer[lane : lane + step])
            low = (grad_active * slope[:, lane : lane + step].astype(FULL)).astype(LOW)
            grad_inner[:, lane : lane + step] = low
            wide_sums[:, lane : lane + step] += jnp.sum(low.astype(FULL), axis=0, keepdims=True)
        grad_normed = grad_normed + against(
            grad_inner[:, j * width : (j + 1) * width], w_inner[j]
        )
    normed = nh1[...].astype(FULL)
    grad_first = normal_back(grad_normed * small[3:4], normed, rs1[...])
    sums[0:1] += jnp.sum(grad_normed * normed, axis=0, keepdims=True)
    sums[1:2] += jnp.sum(grad_normed, axis=0, keepdims=True)
    keeps = keep[:, 0, 0].astype(FULL) * keep_scale
    branch = (grad_first[:length] * keeps[0] + grad_first[length:] * keeps[1]).astype(LOW)
    grad_branch[...] = branch
    sums[2:3] += jnp.sum(branch.astype(FULL), axis=0, keepdims=True)
    base[...] = grad_first[:length] + grad_first[length:]
    grad_att[...] = against(branch, w_out[...]).astype(LOW)


def inner_backward(
    here, grad_outer, slope, second, nh1, rs1, keep_masks, w_outer, w_inner, w_out, small
):
    tokens, ff = slope.shape
    slots, length, width = keep_masks.shape[2:]
    two = 2 * length
    return call(
        inner_back_kernel,
        "inner_backward",
        4 * tokens * width * ff,
        5 * tokens * ff,
        grid=(slots,),
        in_specs=[
            scalars_spec(),
            pl.BlockSpec((two, width), lambda r: (r, 0)),
            pl.BlockSpec((two, ff), lambda r: (r, 0)),
            pl.BlockSpec((two, width), lambda r: (r, 0)),
            pl.BlockSpec((two, width), lambda r: (r, 0)),
            pl.BlockSpec((two, 1), lambda r: (r, 0)),
            pl.BlockSpec((2, 1, 1, length, width), lambda r: (0, 0, r, 0, 0)),
            fixed(w_outer.shape),
            fixed(w_inner.shape),
            fixed(w_out.shape),
            fixed(small.shape),
        ],
        out_specs=[
            pl.BlockSpec((two, ff), lambda r: (r, 0)),
            pl.BlockSpec((length, width), lambda r: (r, 0)),
            pl.BlockSpec((length, width), lambda r: (r, 0)),
            pl.BlockSpec((length, width), lambda r: (r, 0)),
            fixed((8, width)),
            fixed((1, ff)),
            scalars_spec(),
        ],
        out_shape=[
            shaped((tokens, ff), LOW),
            shaped((slots * length, width), LOW),
            shaped((slots * length, width), LOW),
            shaped((slots * length, width), FULL),
            shaped((8, width), FULL),
            shaped((1, ff), FULL),
            shaped((4,), jnp.int32),
        ],
    )(here, grad_outer, slope, second, nh1, rs1, keep_masks, w_outer, w_inner, w_out, small)


def attend_back_kernel(grad_att, start_att, table, qkv, probs, grad_qkv, sums):
    row = pl.program_id(0)
    length, width = grad_att.shape
    even = lax.broadcasted_iota(jnp.int32, (length, 128), 1) < 64

    @pl.when(row == 0)
    def _():
        sums[...] = jnp.zeros_like(sums)

    placed = across(table[0, :32, :length], start_att[...])
    whole_att = (grad_att[...].astype(FULL) + placed).astype(LOW)
    for p in range(width // 128):
        at = p * 128
        query = halves(qkv[:, at : at + 128], even)
        key = halves(qkv[:, width + at : width + at + 128], even)
        value = qkv[:, 2 * width + at : 2 * width + at + 128]
        flow = halves(whole_att[:, at : at + 128], even)
        share = probs[0, p]
        share_f = share.astype(FULL)
        grad_share = against(flow, value)
        inside = jnp.sum(grad_share * share_f, axis=-1, keepdims=True)
        grad_scores = (share_f * (grad_share - inside)).astype(LOW)
        grad_value = across(share, flow).astype(LOW)
        side = jnp.concatenate([grad_scores[:length], grad_scores[length:]], axis=1)
        grad_query = (matmul(side, key) * 0.125).astype(LOW)
        grad_key = (across(grad_scores, query) * 0.125).astype(LOW)
        grad_qkv[:, at : at + 128] = grad_query
        grad_qkv[:, width + at : width + at + 128] = grad_key
        grad_qkv[:, 2 * width + at : 2 * width + at + 128] = grad_value
        sums[0:1, at : at + 128] += jnp.sum(grad_query.astype(FULL), axis=0, keepdims=True)
        sums[1:2, at : at + 128] += jnp.sum(grad_value.astype(FULL), axis=0, keepdims=True)


def attend_backward(grad_att, start_att, table, qkv, probs):
    slots, pairs_of, _, length = probs.shape
    width = grad_att.shape[1]
    return call(
        attend_back_kernel,
        "attend_backward",
        16 * slots * length * length * width,
        18 * slots * length * width,
        grid=(slots,),
        in_specs=[
            pl.BlockSpec((length, width), lambda r: (r, 0)),
            fixed((32, width)),
            pl.BlockSpec((1, 64, 2 * length), lambda r: (r, 0, 0)),
            pl.BlockSpec((length, 3 * width), lambda r: (r, 0)),
            pl.BlockSpec((1, pairs_of, 2 * length, length), lambda r: (r, 0, 0, 0)),
        ],
        out_specs=[
            pl.BlockSpec((length, 3 * width), lambda r: (r, 0)),
            fixed((8, width)),
        ],
        out_shape=[shaped((slots * length, 3 * width), LOW), shaped((8, width), FULL)],
    )(grad_att, start_att, table, qkv, probs)


def input_kernel(here, base, start_base, table, grad_qkv, weights, out, mark):
    hand_on(here, mark)
    width = weights.shape[1]
    total = base[...] + lax.dot_general(
        table[...].astype(FULL),
        start_base[...],
        (((0,), (0,)), ((), ())),
        precision=precise,
        preferred_element_type=FULL,
    )
    for j in range(3):
        total = total + against(grad_qkv[:, j * width : (j + 1) * width], weights[j])
    out[...] = total


def input_gradient(here, base, start_base, table, grad_qkv, weights):
    tokens, width = base.shape
    rows, _, two = table.shape
    table = table[:, :32, : two // 2].transpose(1, 0, 2).reshape(32, tokens)
    args = (base, start_base, table, grad_qkv, weights)
    one = pl.Buffered(1)
    return call(
        input_kernel,
        "input_gradient",
        6 * tokens * width * width,
        14 * tokens * width,
        grid=(1,),
        in_specs=[scalars_spec()]
        + [pl.BlockSpec(a.shape, lambda r, n=a.ndim: (0,) * n, pipeline_mode=one) for a in args],
        out_specs=[pl.BlockSpec(base.shape, lambda r: (0, 0), pipeline_mode=one), scalars_spec()],
        out_shape=[shaped((tokens, width), FULL), shaped((4,), jnp.int32)],
    )(here, *args)


def store_part(here, value, z, x, c, y, kept, away, at):
    on_x = here[1] ^ x
    on_y = here[3] ^ y
    index = 2 * on_y + on_x if c == 0 else 2 * on_x + on_y

    @pl.when(here[2] == c)
    def _():
        kept[(index,) + at] = value

    @pl.when(here[2] != c)
    def _():
        away[(index,) + at] = value


def outer_weight_kernel(
    here_ref, active, grad_outer, start_active, start_outer, cls, grad_pre, kept, away
):
    here = [here_ref[i] for i in range(4)]
    rows = kept.shape[3]
    step = pl.program_id(0)
    last = pl.num_programs(0) - 1

    @pl.when(step < last)
    def _():
        whole = across(active[...], grad_outer[...]) + across(start_active[...], start_outer[...])
        whole = whole.astype(LOW)
        for n in range(32):
            x, c, y, item = n // 16, n // 8 % 2, n // 4 % 2, n % 4
            value = whole[n * rows : (n + 1) * rows]
            store_part(here, value, 0, x, c, y, kept, away, (step, item))

    @pl.when(step == last)
    def _():
        store_parts(here, across(cls[...], grad_pre[...]).astype(LOW), kept, away, 4)


def outer_weight(here, active, grad_outer, start_active, start_outer, *others):
    tokens, ff = active.shape
    width = grad_outer.shape[1]
    part = ff // 4
    shape = (4, 4, 5, width // 32, width)
    return call(
        outer_weight_kernel,
        "outer_weight",
        2 * tokens * ff * width,
        2 * tokens * ff,
        grid_spec=pltpu.PrefetchScalarGridSpec(
            num_scalar_prefetch=1,
            grid=(5,),
            in_specs=[
                pl.BlockSpec((tokens, part), lambda z, _: (0, jnp.minimum(z, 3))),
                pl.BlockSpec((tokens, width), lambda z, _: (0, 0)),
                pl.BlockSpec((64, part), lambda z, _: (0, jnp.minimum(z, 3))),
                pl.BlockSpec((64, width), lambda z, _: (0, 0)),
            ]
            + [fixed(other.shape) for other in others],
            out_specs=[fixed(shape)] * 2,
        ),
        out_shape=[shaped(shape, LOW)] * 2,
    )(here, active, grad_outer, start_active, start_outer, *others)


def store_parts(here, whole, kept, away, item=0):
    rows = kept.shape[3]
    for n in range(32):
        z, x, c, y = n // 8, n // 4 % 2, n // 2 % 2, n % 2
        store_part(here, whole[n * rows : (n + 1) * rows], z, x, c, y, kept, away, (z, item))


def inner_weight_kernel(
    here_ref, n1, grad_inner, start_n1, start_inner, att, branch, start_att, start_branch, kept, away
):
    here = [here_ref[i] for i in range(4)]
    step = pl.program_id(0)
    last = pl.num_programs(0) - 1

    @pl.when(step < last)
    def _():
        whole = across(n1[...], grad_inner[...]) + across(start_n1[0], start_inner[...])
        store_parts(here, whole.astype(LOW), kept, away)

    @pl.when(step == last)
    def _():
        whole = across(att[...], branch[...]) + across(start_att[...], start_branch[...])
        store_parts(here, whole.astype(LOW), kept, away)


def inner_weight(here, n1, grad_inner, picked, start_inner, *others):
    tokens, ff = grad_inner.shape
    width = n1.shape[1]
    wide = ff // width
    spec = pl.BlockSpec((4, 4, 1, width // 32, width), lambda j, _: (0, 0, j, 0, 0))
    shape = shaped((4, 4, wide + 1, width // 32, width), LOW)
    return call(
        inner_weight_kernel,
        "inner_weight",
        2 * tokens * ff * width,
        2 * tokens * ff,
        grid_spec=pltpu.PrefetchScalarGridSpec(
            num_scalar_prefetch=1,
            grid=(wide + 1,),
            in_specs=[
                pl.BlockSpec((tokens, width), lambda j, _: (0, 0)),
                pl.BlockSpec((tokens, width), lambda j, _: (0, jnp.minimum(j, wide - 1))),
                pl.BlockSpec((1, 64, width), lambda j, _: (0, 0, 0)),
                pl.BlockSpec((64, width), lambda j, _: (0, jnp.minimum(j, wide - 1))),
            ]
            + [fixed(other.shape) for other in others],
            out_specs=[spec, spec],
        ),
        out_shape=[shape, shape],
    )(here, n1, grad_inner, picked, start_inner, *others)


def attend_weight_kernel(
    here_ref, x, grad_qkv, start_sums, sums_qv, sums_one, sums_two, wide_sums, kept, away
):
    here = [here_ref[i] for i in range(4)]
    step = pl.program_id(0)

    @pl.when(step < 3)
    def _():
        store_parts(here, across(x[...], grad_qkv[...]).astype(LOW), kept, away)

    @pl.when(step == 3)
    def _():
        width = x.shape[1]
        value = start_sums[...] + jnp.concatenate(
            [sums_qv[0:2], sums_one[2:3], sums_one[0:2], sums_two[0:3]]
            + [jnp.zeros((1, width), FULL)]
            + [wide_sums[:, j * width : (j + 1) * width] for j in range(4)]
            + [jnp.zeros((11, width), FULL)],
            axis=0,
        )
        value = value.astype(LOW)
        for index in range(4):
            for z in range(4):
                kept[index, z, 0] = value
                away[index, z, 0] = value


def attend_weight(here, x, grad_qkv, sums):
    tokens, width = x.shape
    spec = pl.BlockSpec((4, 4, 1, width // 32, width), lambda j, _: (0, 0, j, 0, 0))
    shape = shaped((4, 4, 4, width // 32, width), LOW)
    return call(
        attend_weight_kernel,
        "attend_weight",
        6 * tokens * width * width,
        8 * tokens * width,
        grid_spec=pltpu.PrefetchScalarGridSpec(
            num_scalar_prefetch=1,
            grid=(4,),
            in_specs=[
                pl.BlockSpec((tokens, width), lambda j, _: (0, 0)),
                pl.BlockSpec((tokens, width), lambda j, _: (0, jnp.minimum(j, 2))),
            ]
            + [fixed(value.shape) for value in sums],
            out_specs=[spec, spec],
        ),
        out_shape=[shape, shape],
    )(here, x, grad_qkv, *sums)


def gathered(shard):
    return lax.all_gather(shard, BOTH, axis=0, tiled=True)


def scattered(whole):
    return lax.psum_scatter(whole, BOTH, scatter_dimension=0, tiled=True)


def shared_contrast(unit, flags, log_temp, pooled):
    anchors, partners = unit[:28], unit[32:60]
    inv_temp = jnp.exp(-log_temp[0])
    anchors_all, partners_all = gathered(anchors), gathered(partners)
    column_ok = gathered(flags.astype(LOW)).astype(FULL)
    held_total = jnp.sum(column_ok)
    logits = against(anchors, partners_all) * inv_temp
    logits = jnp.where(column_ok[None, :] > 0, logits, -1e30)
    sim_peak = jnp.max(logits, axis=-1, keepdims=True)
    sim_total = sim_peak + jnp.log(jnp.sum(jnp.exp(logits - sim_peak), axis=-1, keepdims=True))
    anchors_f = anchors.astype(FULL)
    partners_f = partners.astype(FULL)
    positive = jnp.sum(anchors_f * partners_f, axis=-1) * inv_temp
    row_weight = flags / held_total
    loss_part = jnp.sum(row_weight * (sim_total[:, 0] - positive))
    shares = jnp.exp(logits - sim_total) * row_weight[:, None]
    temp_part = jnp.sum(row_weight * positive) - jnp.sum(
        shares * jnp.where(column_ok[None, :] > 0, logits, 0.0)
    )
    grad_anchor = inv_temp * (
        jnp.dot(shares, partners_all.astype(FULL), precision=precise)
        - row_weight[:, None] * partners_f
    )
    totals_all = gathered(sim_total[:, 0])
    back = against(partners, anchors_all) * inv_temp
    back = jnp.where(flags[:, None] > 0, back, -1e30)
    back_shares = jnp.exp(back - totals_all[None, :]) * (column_ok / held_total)[None, :]
    grad_partner = inv_temp * (
        jnp.dot(back_shares, anchors_all.astype(FULL), precision=precise)
        - row_weight[:, None] * anchors_f
    )
    loss, temp_grad = lax.psum((loss_part, temp_part), BOTH)
    pad = ((0, 4), (0, 0))
    grad_unit = jnp.concatenate([jnp.pad(grad_anchor, pad), jnp.pad(grad_partner, pad)])
    return loss.reshape(1), temp_grad.reshape(1), pool_back(grad_unit, pooled)


def pack_kernel(here_ref, *refs):
    vectors, b_inner = refs[:9], refs[9]
    w_query, w_key, w_value, w_out, w_inner = refs[10:15]
    one, two, narrow, broad = refs[15:]
    index = place(here_ref[0], here_ref[1], here_ref[2], here_ref[3])
    rows, width = w_query.shape
    band = b_inner.shape[1]
    per_row = width // band
    one[0] = w_query[...]
    one[1] = w_key[...]
    one[2] = w_value[...]
    for j in range(w_inner.shape[1] // width):
        two[j] = w_inner[:, j * width : (j + 1) * width]
    two[4] = w_out[...]
    narrow[...] = jnp.zeros_like(narrow)
    broad[...] = jnp.zeros_like(broad)
    for f, vector in enumerate(vectors):
        narrow[f : f + 1, :rows] = vector[...].astype(FULL)
    broad[0:1, :band] = b_inner[...].astype(FULL)
    placed = pltpu.roll(narrow[...], rows * index, 1)
    line = pltpu.roll(broad[...], band * lax.rem(index, per_row), 1)[0:1]
    at = lax.broadcasted_iota(jnp.int32, placed.shape, 0) == 9 + index // per_row
    placed = jnp.where(at, line, placed)
    one[3] = placed.astype(LOW)


def pack(here, vectors, b_inner, weights):
    w_query, w_key, w_value, w_out, w_inner = weights
    rows, width = w_query.shape
    return call(
        pack_kernel,
        "pack",
        0,
        40 * rows * width,
        grid_spec=pltpu.PrefetchScalarGridSpec(
            num_scalar_prefetch=1,
            grid=(1,),
            in_specs=[fixed((1, rows))] * 9
            + [fixed((1, b_inner.shape[0]))]
            + [fixed(weight.shape) for weight in weights],
            out_specs=[fixed((4, rows, width)), fixed((w_inner.shape[1] // width + 1, rows, width))],
            scratch_shapes=[pltpu.VMEM((24, width), FULL), pltpu.VMEM((8, width), FULL)],
        ),
        out_shape=[
            shaped((4, rows, width), LOW),
            shaped((w_inner.shape[1] // width + 1, rows, width), LOW),
        ],
    )(
        here,
        *[vector[None] for vector in vectors],
        b_inner[None],
        *weights,
    )


def small_sums(start_sums, sums_qv, sums_one, sums_two, wide_sums):
    width = start_sums.shape[1]
    wide = wide_sums.shape[1] // width
    return start_sums + jnp.concatenate(
        [
            sums_qv[0:2],
            sums_one[2:3],
            sums_one[0:2],
            sums_two[0:3],
            jnp.zeros((1, width), FULL),
            wide_sums.reshape(wide, width),
            jnp.zeros((24 - 9 - wide, width), FULL),
        ]
    )


def paired_body(
    hidden_in, row_counts, buckets, lengths, keep_masks, out_cotangent, vectors, b_inner, weights,
    log_temp,
):
    w_query, w_key, w_value, w_attn_out, w_inner, w_outer, w_pool = weights
    slots, length, width = hidden_in.shape
    tokens = slots * length
    ff = w_inner.shape[1]
    wide = ff // width
    index = lax.axis_index(BOTH)
    here = jnp.stack(whereabouts()).astype(jnp.int32)
    flat = hidden_in.reshape(tokens, width)
    first, second, both = first_pairs(), second_pairs(), across_pairs()

    pack_one, pack_two = pack(here, vectors, b_inner, (w_query, w_key, w_value, w_attn_out, w_inner))
    pack_three = jnp.concatenate([w_outer.reshape(wide, -1, width), w_pool[None]])
    come = along_z(pack_one)
    pack_one, pack_two, come = together(pack_one, pack_two, come)

    one = [jnp.stack([pack_one] + come)]
    come = [send(one[0], route) for route in (first, second, both)]
    come_two = along_z(pack_two)
    segment, starts, held_slots = layout(row_counts, buckets, lengths, length)
    table = pick_table(starts, held_slots, length)
    flags = held_slots.astype(FULL).reshape(slots * 4)
    flag_row = jnp.pad(flags, (0, width - slots * 4))[None]
    one, come, pack_two, come_two, segment, table, flag_row = together(
        one, come, pack_two, come_two, segment, table, flag_row
    )

    one += come
    two = [jnp.stack([pack_two] + come_two)]
    one_other = over_cores(one)
    come_three = [send(pack_three, along_pairs(k)) for k in (1, 2)]
    one, one_other, pack_three = together(one, one_other, pack_three)

    come = [send(two[0], first), send(two[0], second)]
    qkv_weights, small = in_order(here, one + one_other, (3, 0))
    come_three[0], pack_three, small, column = together(
        come_three[0], pack_three, small, two[0]
    )

    come.append(send(column, both))
    come_three.append(send(pack_three, along_pairs(3)))
    qkv_weights = qkv_weights.reshape(3, width, width)
    biases = jnp.stack([small[0], jnp.zeros_like(small[0]), small[1]])[:, None]
    qkv, att, probs, here = attend(here, flat, qkv_weights, biases, segment)
    two, come, pack_three, come_three, here = together(two, come, pack_three, come_three, here)

    two += come
    two_other = over_cores(two)
    three = [jnp.stack([pack_three] + come_three)]
    come = [send(three[0], route) for route in (first, second, both)]
    two, two_other, here = together(two, two_other, here)

    inner_weights, out_weight = in_order(here, two + two_other, (wide, 1))
    inner_weights = inner_weights.reshape(wide, width, width)
    out_weight = out_weight.reshape(width, width)
    n1, nh1, rs1, active, slope, picked, picked_att, picked_rs, start_active, start_slope = (
        inner_forward(
            att, hidden_in, keep_masks, out_weight, inner_weights, small, starts, held_slots
        )
    )
    three, come, start_active = together(three, come, start_active)

    three += come
    outer_weights, pool_weight = in_order(here, three + over_cores(three), (-wide, 1))
    outer_weights = outer_weights.reshape(ff, width)
    pool_weight = pool_weight.reshape(width, width)
    start_nh2, start_rs2, cls, pooled, unit = start_forward(
        start_active, picked, outer_weights, small, pool_weight, flag_row
    )
    unit, here = together(unit, here)

    come = along_z(unit)
    result, grad_outer, second_flow, sums_two, here = outer_both(
        here, active, n1, keep_masks, out_cotangent, segment, outer_weights, small
    )
    unit, come, here = together(unit, come, here)

    own = [jnp.stack([unit] + come)]
    come = [send(own[0], route) for route in (first, second, both)]
    grad_inner, grad_branch, grad_att, base, sums_one, wide_sums, here = inner_backward(
        here, grad_outer, slope, second_flow, nh1, rs1, keep_masks, outer_weights, inner_weights,
        out_weight, small,
    )
    own, come, here = together(own, come, here)

    own += come
    scalars, grad_pre, start_outer, start_second, start_sums = contrast(
        here, own + over_cores(own), log_temp, pooled, pool_weight, start_nh2, start_rs2, picked,
        small,
    )
    loss, temp_grad = scalars[0, :1], scalars[1, :1]

    outer_kept, outer_away = outer_weight(
        here, active, grad_outer, start_active, start_outer, cls, grad_pre
    )
    come = send(outer_away, core_pairs())
    outer_kept, start_outer = together(outer_kept, start_outer)
    start_inner, start_branch, start_base, start_att, start_sums = start_backward(
        start_outer, start_second, start_sums, picked, picked_rs, start_slope, small,
        outer_weights, inner_weights, out_weight,
    )
    come, outer_kept, start_inner, start_att, start_base, start_sums = together(
        come, outer_kept, start_inner, start_att, start_base, start_sums
    )

    outer_go, outer_own = halves_of(outer_kept, come)
    come = send(outer_go, second)
    outer_own, here = together(outer_own, here)
    inner_kept, inner_away = inner_weight(
        here, n1, grad_inner, picked, start_inner, att, grad_branch, picked_att, start_branch
    )
    outer_own, come, inner_kept, inner_away = together(outer_own, come, inner_kept, inner_away)

    come_inner = send(inner_away, core_pairs())
    outer_go, outer_own = quarters_of(outer_own, come)
    come = send(outer_go, first)
    inner_kept, come_inner, outer_own, come = together(inner_kept, come_inner, outer_own, come)

    inner_go, inner_own = halves_of(inner_kept, come_inner)
    come_inner = send(inner_go, second)
    parts_outer = over_z(add_low(outer_own, come))
    inner_own, start_att = together(inner_own, start_att)
    grad_qkv, sums_qv = attend_backward(grad_att, start_att, table, qkv, probs)
    attend_kept, attend_away = attend_weight(
        here, flat, grad_qkv, (start_sums, sums_qv, sums_one, sums_two, wide_sums)
    )
    parts_outer, inner_own, come_inner, attend_kept, attend_away = together(
        parts_outer, inner_own, come_inner, attend_kept, attend_away
    )

    come_attend = send(attend_away, core_pairs())
    inner_go, inner_own = quarters_of(inner_own, come_inner)
    come_inner = send(inner_go, first)
    attend_kept, come_attend, inner_own, here = together(
        attend_kept, come_attend, inner_own, here
    )

    attend_go, attend_own = halves_of(attend_kept, come_attend)
    come_attend = send(attend_go, second)
    attend_own, start_base, here = together(attend_own, start_base, here)
    input_grad, here = input_gradient(here, base, start_base, table, grad_qkv, qkv_weights)
    inner_own, come_inner, here = together(inner_own, come_inner, here)

    parts_inner = over_z(add_low(inner_own, come_inner))
    outer_part, pool_part = finish(here, parts_outer, inner=wide, tall=True)
    attend_own, come_attend, parts_inner[1], parts_inner[3], outer_part = together(
        attend_own, come_attend, parts_inner[1], parts_inner[3], outer_part
    )

    attend_go, attend_own = quarters_of(attend_own, come_attend)
    come_attend = send(attend_go, first)
    attend_own, come_attend = together(attend_own, come_attend)
    parts_attend = over_z(add_low(attend_own, come_attend))
    inner_part, out_part = finish(here, parts_inner, inner=wide)
    query_part, key_part, value_part, own_small, inner_bias_part = finish(
        here, parts_attend, vectors=9, band=b_inner.shape[0]
    )
    input_grad = input_grad.reshape(hidden_in.shape)
    inner_bias_part = inner_bias_part[0]
    parts = [query_part, key_part, value_part, out_part]
    small_parts = [own_small[i] for i in range(9)]
    return (
        loss,
        result,
        input_grad,
        parts[0],
        small_parts[0],
        parts[1],
        parts[2],
        small_parts[1],
        parts[3],
        small_parts[2],
        small_parts[3],
        small_parts[4],
        inner_part,
        inner_bias_part,
        outer_part,
        small_parts[5],
        small_parts[6],
        small_parts[7],
        pool_part,
        small_parts[8],
        temp_grad,
    )


def body(
    hidden_in,
    row_counts,
    buckets,
    lengths,
    keep_masks,
    out_cotangent,
    w_query,
    b_query,
    w_key,
    w_value,
    b_value,
    w_attn_out,
    b_attn_out,
    norm1_gain,
    norm1_bias,
    w_inner,
    b_inner,
    w_outer,
    b_outer,
    norm2_gain,
    norm2_bias,
    w_pool,
    b_pool,
    log_temp,
):
    slots, length, width = hidden_in.shape
    tokens = slots * length
    ff = w_inner.shape[1]
    wide = ff // width
    index = lax.axis_index(BOTH)
    here = jnp.stack(whereabouts()).astype(jnp.int32)
    vectors = (
        b_query,
        b_value,
        b_attn_out,
        norm1_gain,
        norm1_bias,
        b_outer,
        norm2_gain,
        norm2_bias,
        b_pool,
    )
    if paired():
        return paired_body(
            hidden_in, row_counts, buckets, lengths, keep_masks, out_cotangent, vectors, b_inner,
            (w_query, w_key, w_value, w_attn_out, w_inner, w_outer, w_pool), log_temp,
        )
    qkv_weights = jnp.stack([gathered(w) for w in (w_query, w_key, w_value)])
    out_weight = gathered(w_attn_out)
    rows = [gathered(v)[None] for v in vectors]
    rows.append(gathered(b_inner).reshape(wide, width))
    rows.append(jnp.zeros((24 - 9 - wide, width), LOW))
    small = jnp.concatenate(rows).astype(FULL)
    inner_weights = gathered(w_inner).reshape(width, wide, width).transpose(1, 0, 2)
    outer_weights = gathered(w_outer)
    pool_weight = gathered(w_pool)

    segment, starts, held_slots = layout(row_counts, buckets, lengths, length)
    table = pick_table(starts, held_slots, length)
    flags = held_slots.astype(FULL).reshape(slots * 4)
    flag_row = jnp.pad(flags, (0, width - slots * 4))[None]

    flat = hidden_in.reshape(tokens, width)
    biases = jnp.stack([small[0], jnp.zeros_like(small[0]), small[1]])[:, None]
    qkv, att, probs, _ = attend(here, flat, qkv_weights, biases, segment)
    n1, nh1, rs1, active, slope, picked, picked_att, picked_rs, start_active, start_slope = (
        inner_forward(
            att, hidden_in, keep_masks, out_weight, inner_weights, small, starts, held_slots
        )
    )
    start_nh2, start_rs2, cls, pooled, unit = start_forward(
        start_active, picked, outer_weights, small, pool_weight, flag_row
    )
    result, grad_outer, second_flow, sums_two, _ = outer_both(
        here, active, n1, keep_masks, out_cotangent, segment, outer_weights, small
    )
    loss, temp_grad, grad_pre = shared_contrast(unit[0], flags, log_temp, pooled)
    start_outer, start_second, start_sums = start_outer_back(
        grad_pre, pool_weight, start_nh2, start_rs2[:, :1], picked[3], small
    )
    start_inner, start_branch, start_base, start_att, start_sums = start_backward(
        start_outer, start_second, start_sums, picked, picked_rs, start_slope, small,
        outer_weights, inner_weights, out_weight,
    )
    grad_inner, grad_branch, grad_att, base, sums_one, wide_sums, _ = inner_backward(
        here, grad_outer, slope, second_flow, nh1, rs1, keep_masks, outer_weights, inner_weights,
        out_weight, small,
    )
    grad_qkv, sums_qv = attend_backward(grad_att, start_att, table, qkv, probs)
    grad_small = small_sums(start_sums, sums_qv, sums_one, sums_two, wide_sums)
    input_grad, _ = input_gradient(here, base, start_base, table, grad_qkv, qkv_weights)
    input_grad = input_grad.reshape(hidden_in.shape)
    parts = [scattered(across(flat, grad_qkv[:, j * width : (j + 1) * width])) for j in range(3)]
    parts.append(scattered(across(att, grad_branch) + across(picked_att, start_branch)))
    small_parts = [scattered(grad_small[i]) for i in range(9)]
    inner_bias_part = scattered(grad_small[9 : 9 + wide].reshape(ff))
    outer_part = scattered(across(active, grad_outer) + across(start_active, start_outer))
    inner_part = scattered(across(n1, grad_inner) + across(picked[0], start_inner))
    pool_part = scattered(across(cls, grad_pre))
    return (
        loss,
        result,
        input_grad,
        parts[0],
        small_parts[0],
        parts[1],
        parts[2],
        small_parts[1],
        parts[3],
        small_parts[2],
        small_parts[3],
        small_parts[4],
        inner_part,
        inner_bias_part,
        outer_part,
        small_parts[5],
        small_parts[6],
        small_parts[7],
        pool_part,
        small_parts[8],
        temp_grad,
    )


def solution(mesh):
    outer, inner = mesh.shape["dp"], mesh.shape["fsdp"]
    sizes = (4, 2, 2, 2) if (outer, inner) == (16, 2) else (outer, 1, 1, inner)
    mesh = jax.sharding.Mesh(mesh.devices.reshape(sizes), BOTH)
    in_specs = (
        P(BOTH, None, None),
        P(BOTH),
        P(BOTH),
        P(BOTH, None),
        P(None, None, BOTH, None, None),
        P(None, BOTH, None, None),
        P(BOTH, None),
        P(BOTH),
        P(BOTH, None),
        P(BOTH, None),
        P(BOTH),
        P(BOTH, None),
        P(BOTH),
        P(BOTH),
        P(BOTH),
        P(BOTH, None),
        P(BOTH),
        P(BOTH, None),
        P(BOTH),
        P(BOTH),
        P(BOTH),
        P(BOTH, None),
        P(BOTH),
        P(),
    )
    out_specs = (
        P(),
        P(None, BOTH, None, None),
        P(BOTH, None, None),
        P(BOTH, None),
        P(BOTH),
        P(BOTH, None),
        P(BOTH, None),
        P(BOTH),
        P(BOTH, None),
        P(BOTH),
        P(BOTH),
        P(BOTH),
        P(BOTH, None),
        P(BOTH),
        P(BOTH, None),
        P(BOTH),
        P(BOTH),
        P(BOTH),
        P(BOTH, None),
        P(BOTH),
        P(),
    )
    return jax.shard_map(body, mesh=mesh, in_specs=in_specs, out_specs=out_specs, check_vma=False)
```

```python
import functools

import jax
import jax.numpy as jnp
from jax import lax
from jax.experimental import pallas as pl
from jax.experimental.pallas import tpu as pltpu
from jax.sharding import PartitionSpec as P

HEADS = 12
BOTH = ("z", "x", "c", "y")
LOW = jnp.bfloat16
FULL = jnp.float32

precise = lax.Precision.HIGHEST
keep_scale = 1.0 / 0.9
inv_root_two = 0.7071067811865476
inv_root_tau = 0.3989422804014327
eps = 1e-06


def matmul(left, right):
    return lax.dot_general(left, right, (((1,), (0,)), ((), ())), preferred_element_type=FULL)


def against(left, right):
    return lax.dot_general(left, right, (((1,), (1,)), ((), ())), preferred_element_type=FULL)


def across(left, right):
    return lax.dot_general(left, right, (((0,), (0,)), ((), ())), preferred_element_type=FULL)


def paired():
    return tuple(lax.axis_size(axis) for axis in BOTH) == (4, 2, 2, 2)


def place(z, x, c, y):
    return ((z * 2 + x) * 2 + c) * 2 + y


def pairs(move):
    every = [(z, x, c, y) for z in range(4) for x in range(2) for c in range(2) for y in range(2)]
    return [(place(*t), place(*move(*t))) for t in every]


def first_pairs():
    return pairs(lambda z, x, c, y: (z, 1 - x, c, y) if c == 0 else (z, x, c, 1 - y))


def second_pairs():
    return pairs(lambda z, x, c, y: (z, x, c, 1 - y) if c == 0 else (z, 1 - x, c, y))


def across_pairs():
    return pairs(lambda z, x, c, y: (z, 1 - x, c, 1 - y))


def core_pairs():
    return pairs(lambda z, x, c, y: (z, x, 1 - c, y))


def along_pairs(k):
    return pairs(lambda z, x, c, y: ((z + k) % 4, x, c, y))


def whereabouts():
    index = lax.axis_index(BOTH)
    return index // 8, index // 4 % 2, index // 2 % 2, index % 2


def send(block, route):
    return lax.ppermute(block, BOTH, route)


def together(*values):
    return lax.optimization_barrier(values)


def along_z(shard):
    return [send(shard, along_pairs(k)) for k in (1, 2, 3)]


def over_cores(own):
    return [send(block, core_pairs()) for block in own]


def where_from(here, core, p1, p2):
    first_x = core == 0
    on_x = jnp.where(first_x, p1, p2)
    on_y = jnp.where(first_x, p2, p1)
    return here[1] ^ on_x, here[3] ^ on_y


def order_kernel(parts, here_ref, *refs):
    blocks, outs = refs[:8], refs[8:]
    here = [here_ref[i] for i in range(4)]
    total = None
    for i in range(8):
        core = here[2] if i < 4 else 1 - here[2]
        x, y = where_from(here, core, i % 2, i // 2 % 2)
        for k in range(4):
            z = lax.rem(here[0] + 4 - k, 4)
            device = place(z, x, core, y)
            item = 0
            for count, out in zip(parts, outs):
                if count == 0:
                    value = blocks[i][k, item].astype(FULL)
                    total = value if total is None else total + value
                    item += 1
                for n in range(count):
                    out[n, device] = blocks[i][k, item]
                    item += 1
                for n in range(-count):
                    out[device, n] = blocks[i][k, item]
                    item += 1
    for count, out in zip(parts, outs):
        if count == 0:
            out[...] = total


def in_order(here, blocks, parts):
    items, rows, width = blocks[0].shape[1:]
    whole = pl.BlockSpec(memory_space=pltpu.VMEM)
    return call(
        functools.partial(order_kernel, parts),
        "order",
        0,
        128 * items * rows * width,
        out_shape=[
            shaped((rows, width), FULL)
            if count == 0
            else shaped((count, 32, rows, width) if count > 0 else (32, -count, rows, width), LOW)
            for count in parts
        ],
        grid_spec=pltpu.PrefetchScalarGridSpec(
            num_scalar_prefetch=1, grid=(), in_specs=[whole] * 8, out_specs=[whole] * len(parts)
        ),
    )(here, *blocks)


def add_low(left, right):
    return (left.astype(FULL) + right.astype(FULL)).astype(LOW)


def halves_of(kept, come):
    return add_low(kept[2:], come[2:]), add_low(kept[:2], come[:2])


def quarters_of(own, come):
    return add_low(own[1], come[1]), add_low(own[0], come[0])


def add_all(own, come):
    return sum([part.astype(FULL) for part in come], own.astype(FULL)).astype(LOW)


def over_z(column):
    z = lax.axis_index("z")
    own = lax.dynamic_index_in_dim(column, z, 0, keepdims=False)
    away = [lax.dynamic_index_in_dim(column, (z + k) % 4, 0, keepdims=False) for k in (1, 2, 3)]
    return [own] + [send(part, along_pairs(k)) for k, part in zip((1, 2, 3), away)]


def finish_kernel(inner, vectors, *refs):
    parts, outs = refs[1:5], refs[5:]
    here_ref = refs[0]
    rows, width = parts[0].shape[1:]

    def total(n):
        return sum(part[n].astype(FULL) for part in parts)

    for n in range(inner):
        if outs[0].shape[0] == rows:
            outs[0][:, n * width : (n + 1) * width] = total(n)
        else:
            outs[0][n * rows : (n + 1) * rows] = total(n)
    outs = outs[1:] if inner else outs
    plain = parts[0].shape[0] - inner - (1 if vectors else 0)
    for n in range(plain):
        outs[n][...] = total(inner + n)
    if vectors:
        index = place(here_ref[0], here_ref[1], here_ref[2], here_ref[3])
        value = total(inner + plain)
        piece = width // 32
        band = outs[plain + 1].shape[1]
        per_row = width // band
        outs[plain][...] = pltpu.roll(value, width - piece * index, 1)[: outs[plain].shape[0], :piece]
        at = lax.broadcasted_iota(jnp.int32, value.shape, 0) == 9 + index // per_row
        line = jnp.sum(jnp.where(at, value, 0.0), axis=0, keepdims=True)
        line = jnp.broadcast_to(line, (8, width))
        line = pltpu.roll(line, width - band * lax.rem(index, per_row), 1)
        outs[plain + 1][...] = line[0:1, :band]


def finish(here, parts, inner=0, vectors=0, band=0, tall=False):
    items, rows, width = parts[0].shape
    plain = items - inner - (1 if vectors else 0)
    shapes = [(inner * rows, width) if tall else (rows, inner * width)] if inner else []
    shapes += [(rows, width)] * plain
    shapes += [(vectors, width // 32), (1, band)] if vectors else []
    return call(
        functools.partial(finish_kernel, inner, vectors),
        "finish",
        0,
        12 * items * rows * width,
        grid_spec=pltpu.PrefetchScalarGridSpec(
            num_scalar_prefetch=1,
            grid=(1,),
            in_specs=[fixed(parts[0].shape)] * 4,
            out_specs=[fixed(shape) for shape in shapes],
        ),
        out_shape=[shaped(shape, FULL) for shape in shapes],
    )(here, *parts)


def layout(row_counts, buckets, lengths, row_len):
    slot_count = buckets.shape[0]
    live_rows = jnp.arange(slot_count, dtype=jnp.int32) < row_counts[0]
    sent_count = jnp.right_shift(jnp.int32(4), buckets)
    slot_ids = jnp.arange(4, dtype=jnp.int32)
    held_slots = (slot_ids[None, :] < sent_count[:, None]) & live_rows[:, None]
    sizes_used = jnp.where(held_slots, lengths, 0)
    finish = jnp.cumsum(sizes_used, axis=1, dtype=jnp.int32)
    starts = finish - sizes_used
    places = jnp.arange(row_len, dtype=jnp.int32)
    segment = jnp.sum((places[None, :, None] >= finish[:, None, :]).astype(jnp.int32), axis=2)
    return segment, starts, held_slots


def pick_table(starts, held_slots, row_len):
    rows = starts.shape[0]
    slot = jnp.arange(64, dtype=jnp.int32)
    view, row, k = slot // 32, slot % 32 // 4, slot % 4
    row = jnp.minimum(row, rows - 1)
    real = slot % 32 < rows * 4
    start = starts[row, k]
    held = held_slots[row, k] & real
    token = jnp.arange(2 * row_len, dtype=jnp.int32)
    hit = held[:, None] & (token[None, :] == (view * row_len + start)[:, None])
    here = jnp.arange(rows, dtype=jnp.int32)[:, None] == row[None, :]
    return (here[:, :, None] & hit[None]).astype(LOW)


rooms = {"pack": 60, "attend": 60, "inner_forward": 44, "outer_both": 60, "inner_backward": 60}


def call(kernel, name, flops, moved, **kwargs):
    room = rooms.get(name, 36)
    return pl.pallas_call(
        kernel,
        name=name,
        compiler_params=pltpu.CompilerParams(vmem_limit_bytes=room * 2**20),
        cost_estimate=pl.CostEstimate(flops=flops // 10, transcendentals=0, bytes_accessed=moved // 10),
        **kwargs,
    )


def scalars_spec():
    return pl.BlockSpec(memory_space=pltpu.SMEM)


def hand_on(here, mark):
    for n in range(4):
        mark[n] = here[n]


def fixed(shape):
    zeros = (0,) * len(shape)
    return pl.BlockSpec(shape, lambda *_: zeros)


def shaped(shape, kind):
    return jax.ShapeDtypeStruct(shape, kind)


def halves(pair, even):
    zero = jnp.zeros_like(pair)
    return jnp.concatenate([jnp.where(even, pair, zero), jnp.where(even, zero, pair)], axis=0)


def attend_kernel(here, x, weights, biases, seg_row, seg_col, qkv, out, probs, mark):
    hand_on(here, mark)
    length, width = out.shape
    for j in range(3):
        value = matmul(x[...], weights[j]) + biases[j]
        qkv[:, j * width : (j + 1) * width] = value.astype(LOW)
    even = lax.broadcasted_iota(jnp.int32, (length, 128), 1) < 64
    same = seg_col[0] == seg_row[0]
    same = jnp.concatenate([same, same], axis=0)
    for p in range(width // 128):
        at = p * 128
        query = halves(qkv[:, at : at + 128], even)
        key = qkv[:, width + at : width + at + 128]
        value = qkv[:, 2 * width + at : 2 * width + at + 128]
        scores = jnp.where(same, against(query, key) * 0.125, -1e30)
        peak = jnp.max(scores, axis=-1, keepdims=True)
        lifted = jnp.exp(scores - peak)
        share = lifted * (1.0 / jnp.sum(lifted, axis=-1, keepdims=True))
        share = share.astype(LOW)
        probs[0, p] = share
        both = matmul(share, value)
        out[:, at : at + 128] = jnp.where(even, both[:length], both[length:]).astype(LOW)


def attend(here, flat, weights, biases, segment):
    slots, length = segment.shape
    tokens, width = flat.shape
    pairs_of = width // 128
    return call(
        attend_kernel,
        "attend",
        6 * tokens * width * width + 8 * tokens * length * width,
        16 * tokens * width,
        grid=(slots,),
        in_specs=[
            scalars_spec(),
            pl.BlockSpec((length, width), lambda r: (r, 0)),
            fixed(weights.shape),
            fixed(biases.shape),
            pl.BlockSpec((1, 1, length), lambda r: (r, 0, 0)),
            pl.BlockSpec((1, length, 1), lambda r: (r, 0, 0)),
        ],
        out_specs=[
            pl.BlockSpec((length, 3 * width), lambda r: (r, 0)),
            pl.BlockSpec((length, width), lambda r: (r, 0)),
            pl.BlockSpec((1, pairs_of, 2 * length, length), lambda r: (r, 0, 0, 0)),
            scalars_spec(),
        ],
        out_shape=[
            shaped((tokens, 3 * width), LOW),
            shaped((tokens, width), LOW),
            shaped((slots, pairs_of, 2 * length, length), LOW),
            shaped((4,), jnp.int32),
        ],
    )(here, flat, weights, biases, segment[:, None, :], segment[:, :, None])


def normal(hidden):
    centre = jnp.mean(hidden, axis=-1, keepdims=True)
    offset = hidden - centre
    spread_of = jnp.mean(offset * offset, axis=-1, keepdims=True)
    rscale = lax.rsqrt(spread_of + eps)
    return offset * rscale, rscale


def normal_back(grad_norm, normed, rscale):
    mean_grad = jnp.mean(grad_norm, axis=-1, keepdims=True)
    mean_cross = jnp.mean(grad_norm * normed, axis=-1, keepdims=True)
    return rscale * (grad_norm - mean_grad - normed * mean_cross)


def gelu_parts(inner):
    phi = 0.5 * (1.0 + lax.erf(inner * inv_root_two))
    return inner * phi, phi + inner * jnp.exp(-0.5 * inner * inner) * inv_root_tau


def inner_kernel(
    starts, held, att, x, keep, w_out, w_inner, small,
    n1, nh1, rs1, active, slope, picked, picked_att, picked_rs, picked_active, picked_slope,
    rows_one, rows_unit, rows_att, rows_scale, near, near_att, near_rs,
):
    row = pl.program_id(0)
    length, width = att.shape
    branch = matmul(att[...], w_out[...]) + small[2:3]
    base = x[0].astype(FULL)
    keeps = keep[:, 0, 0].astype(FULL) * keep_scale
    first = jnp.concatenate([base + branch * keeps[0], base + branch * keeps[1]], axis=0)
    normed, rscale = normal(first)
    nh1[...] = normed.astype(LOW)
    rs1[...] = rscale
    rows_unit[...] = normed
    rows_scale[...] = jnp.broadcast_to(rscale, rows_scale.shape)
    rows_att[...] = att[...].astype(FULL)
    whole_in = normed * small[3:4] + small[4:5]
    rows_one[...] = whole_in
    inner_in = whole_in.astype(LOW)
    n1[...] = inner_in
    step = 256
    for j in range(w_inner.shape[0]):
        for at in range(0, width, step):
            inner = matmul(inner_in, w_inner[j, :, at : at + step])
            inner = inner + small[9 + j : 10 + j, at : at + step]
            value, grad = gelu_parts(inner)
            active[:, j * width + at : j * width + at + step] = value.astype(LOW)
            slope[:, j * width + at : j * width + at + step] = grad.astype(LOW)

    @pl.when(row == 0)
    def _():
        near[...] = jnp.zeros_like(near)
        near_att[...] = jnp.zeros_like(near_att)
        near_rs[...] = jnp.zeros_like(near_rs)

    for k in range(4):
        slot = 4 * row + k

        @pl.when(held[row, k] > 0)
        def _():
            start = starts[row, k]
            near_att[pl.ds(slot, 1)] = rows_att[pl.ds(start, 1)]
            for v in range(2):
                to = pl.ds(32 * v + slot, 1)
                near[0, to] = rows_one[pl.ds(length * v + start, 1)]
                near[1, to] = rows_unit[pl.ds(length * v + start, 1)]
                for n in range(2):
                    near[2 + n, to] = keep[v, n, 0, pl.ds(start, 1)].astype(FULL)
                near_rs[to] = rows_scale[pl.ds(length * v + start, 1)]

    @pl.when(row == pl.num_programs(0) - 1)
    def _():
        picked[...] = near[:, :64].astype(LOW)
        picked_att[...] = near_att[:32].astype(LOW)
        picked_rs[...] = near_rs[:64]
        begin = near[0, :64].astype(LOW)
        for j in range(w_inner.shape[0]):
            inner = matmul(begin, w_inner[j]) + small[9 + j : 10 + j]
            value, grad = gelu_parts(inner)
            picked_active[:, j * width : (j + 1) * width] = value.astype(LOW)
            picked_slope[:, j * width : (j + 1) * width] = grad.astype(LOW)


def inner_forward(att, hidden, keep_masks, w_out, w_inner, small, starts, held_slots):
    slots, length, width = hidden.shape
    ff = w_inner.shape[0] * width
    two = 2 * length
    return call(
        inner_kernel,
        "inner_forward",
        2 * slots * two * width * ff,
        slots * two * ff * 5,
        grid_spec=pltpu.PrefetchScalarGridSpec(
            num_scalar_prefetch=2,
            grid=(slots,),
            in_specs=[
                pl.BlockSpec((length, width), lambda r, *_: (r, 0)),
                pl.BlockSpec((1, length, width), lambda r, *_: (r, 0, 0)),
                pl.BlockSpec((2, 2, 1, length, width), lambda r, *_: (0, 0, r, 0, 0)),
                fixed((width, width)),
                fixed(w_inner.shape),
                fixed(small.shape),
            ],
            out_specs=[
                pl.BlockSpec((two, width), lambda r, *_: (r, 0)),
                pl.BlockSpec((two, width), lambda r, *_: (r, 0)),
                pl.BlockSpec((two, 1), lambda r, *_: (r, 0)),
                pl.BlockSpec((two, ff), lambda r, *_: (r, 0)),
                pl.BlockSpec((two, ff), lambda r, *_: (r, 0)),
                fixed((4, 64, width)),
                fixed((32, width)),
                fixed((64, 128)),
                fixed((64, ff)),
                fixed((64, ff)),
            ],
            scratch_shapes=[
                pltpu.VMEM((two, width), FULL),
                pltpu.VMEM((two, width), FULL),
                pltpu.VMEM((length, width), FULL),
                pltpu.VMEM((two, 128), FULL),
                pltpu.VMEM((4, 72, width), FULL),
                pltpu.VMEM((40, width), FULL),
                pltpu.VMEM((72, 128), FULL),
            ],
        ),
        out_shape=[
            shaped((slots * two, width), LOW),
            shaped((slots * two, width), LOW),
            shaped((slots * two, 1), FULL),
            shaped((slots * two, ff), LOW),
            shaped((slots * two, ff), LOW),
            shaped((4, 64, width), LOW),
            shaped((32, width), LOW),
            shaped((64, 128), FULL),
            shaped((64, ff), LOW),
            shaped((64, ff), LOW),
        ],
    )(starts, held_slots.astype(jnp.int32), att, hidden, keep_masks, w_out, w_inner, small)


def start_kernel(active, picked, w_outer, small, w_pool, flags, nh2, rs2, cls, pooled, unit):
    outer = matmul(active[...], w_outer[...]) + small[5:6]
    second = picked[0].astype(FULL) + outer * (picked[3].astype(FULL) * keep_scale)
    normed, rscale = normal(second)
    nh2[...] = normed.astype(LOW)
    rs2[...] = jnp.broadcast_to(rscale, rs2.shape)
    out = (normed * small[6:7] + small[7:8]).astype(LOW)
    cls[...] = out
    squashed = jnp.tanh(matmul(out, w_pool[...]) + small[8:9])
    pooled[...] = squashed
    scale = lax.rsqrt(jnp.sum(squashed * squashed, axis=-1, keepdims=True) + eps)
    ones = (squashed * scale).astype(LOW).astype(FULL)
    slot = lax.broadcasted_iota(jnp.int32, ones.shape, 0)
    unit[0] = jnp.where(slot == 28, flags[...], ones).astype(LOW)


def start_forward(active, picked, w_outer, small, w_pool, flags):
    ff, width = w_outer.shape
    return call(
        start_kernel,
        "start_forward",
        128 * width * ff,
        2 * width * ff,
        out_shape=[
            shaped((64, width), LOW),
            shaped((64, 128), FULL),
            shaped((64, width), LOW),
            shaped((64, width), FULL),
            shaped((1, 64, width), LOW),
        ],
    )(active, picked, w_outer, small, w_pool, flags)


def outer_kernel(
    here, active, n1, keep, cot, segment, w_outer, small, result, grad_outer, second_flow, sums, mark
):
    hand_on(here, mark)
    row = pl.program_id(0)
    length = n1.shape[0] // 2
    keeps = keep[:, 0, 0].astype(FULL) * keep_scale
    keeps = jnp.concatenate([keeps[0], keeps[1]], axis=0)
    outer = matmul(active[...], w_outer[...]) + small[5:6]
    second = n1[...].astype(FULL) + outer * keeps
    normed, rscale = normal(second)
    out = (normed * small[6:7] + small[7:8]).astype(LOW)
    result[0, 0] = out[:length]
    result[1, 0] = out[length:]
    flow = jnp.concatenate([cot[0, 0], cot[1, 0]], axis=0).astype(FULL)
    ok = (segment[0] < 4).astype(FULL)
    grad_out = flow * jnp.concatenate([ok, ok], axis=0)
    grad_second = normal_back(grad_out * small[6:7], normed, rscale)
    low = (grad_second * keeps).astype(LOW)
    grad_outer[...] = low
    second_flow[...] = grad_second.astype(LOW)

    @pl.when(row == 0)
    def _():
        sums[...] = jnp.zeros_like(sums)

    sums[0:1] += jnp.sum(low.astype(FULL), axis=0, keepdims=True)
    sums[1:2] += jnp.sum(grad_out * normed, axis=0, keepdims=True)
    sums[2:3] += jnp.sum(grad_out, axis=0, keepdims=True)


def outer_both(here, active, n1, keep_masks, cotangent, segment, w_outer, small):
    tokens, ff = active.shape
    width = n1.shape[1]
    slots = keep_masks.shape[2]
    length = keep_masks.shape[3]
    two = 2 * length
    return call(
        outer_kernel,
        "outer_both",
        2 * tokens * width * ff,
        2 * tokens * ff,
        grid=(slots,),
        in_specs=[
            scalars_spec(),
            pl.BlockSpec((two, ff), lambda r: (r, 0)),
            pl.BlockSpec((two, width), lambda r: (r, 0)),
            pl.BlockSpec((2, 1, 1, length, width), lambda r: (0, 1, r, 0, 0)),
            pl.BlockSpec((2, 1, length, width), lambda r: (0, r, 0, 0)),
            pl.BlockSpec((1, length, 1), lambda r: (r, 0, 0)),
            fixed((ff, width)),
            fixed(small.shape),
        ],
        out_specs=[
            pl.BlockSpec((2, 1, length, width), lambda r: (0, r, 0, 0)),
            pl.BlockSpec((two, width), lambda r: (r, 0)),
            pl.BlockSpec((two, width), lambda r: (r, 0)),
            fixed((8, width)),
            scalars_spec(),
        ],
        out_shape=[
            shaped((2, slots, length, width), LOW),
            shaped((tokens, width), LOW),
            shaped((tokens, width), LOW),
            shaped((8, width), FULL),
            shaped((4,), jnp.int32),
        ],
    )(here, active, n1, keep_masks, cotangent, segment[:, :, None], w_outer, small)


def split_matmul(left, right):
    upper = left.astype(LOW)
    lower = (left - upper.astype(FULL)).astype(LOW)
    return matmul(upper, right) + matmul(lower, right)


def pool_back(grad_unit, squashed):
    scale = lax.rsqrt(jnp.sum(squashed * squashed, axis=-1, keepdims=True) + eps)
    grad_pooled = scale * grad_unit - squashed * (scale * scale * scale) * jnp.sum(
        squashed * grad_unit, axis=-1, keepdims=True
    )
    return (grad_pooled * (1.0 - squashed * squashed)).astype(LOW)


def loss_kernel(here_ref, *refs):
    blocks = refs[:8]
    (
        temp, pooled, w_pool, nh2, rs2, picked, small, scalars, grad_pre, start_outer, start_second,
        start_sums, anchors, partners, flat, sem,
    ) = refs[8:]
    here = [here_ref[i] for i in range(4)]
    copies = []
    for i in range(8):
        core = here[2] if i < 4 else 1 - here[2]
        x, y = where_from(here, core, i % 2, i // 2 % 2)
        for k in range(4):
            z = lax.rem(here[0] + 4 - k, 4)
            row = pl.multiple_of(place(z, x, core, y) * 32, 32)
            source = blocks[i].at[k, 0]
            for half, target in ((0, anchors), (1, partners)):
                copies.append(
                    pltpu.make_async_copy(
                        source.at[pl.ds(32 * half, 32)], target.at[pl.ds(row, 32)], sem
                    )
                )
    for copy in copies:
        copy.start()
    for copy in copies:
        copy.wait()
    count = anchors.shape[0]
    groups = count // 32
    inv_temp = jnp.exp(-temp[...])
    all_anchors = anchors[...]
    all_partners = partners[...]
    for d in range(groups):
        flat[d : d + 1] = anchors[d * 32 + 28 : d * 32 + 29, :128].astype(FULL)
    marks = flat[0:32].astype(LOW)
    slot = lax.broadcasted_iota(jnp.int32, (128, count), 0)
    lane = lax.broadcasted_iota(jnp.int32, (128, count), 1)
    wide = matmul(marks, (slot == lane % 32).astype(LOW))
    group = lax.broadcasted_iota(jnp.int32, (groups, count), 0)
    lane = lax.broadcasted_iota(jnp.int32, (groups, count), 1)
    row_ok = jnp.sum(jnp.where(group == lane // 32, wide, 0.0), axis=0, keepdims=True)
    tall_row = lax.broadcasted_iota(jnp.int32, (count, groups), 0)
    tall_group = lax.broadcasted_iota(jnp.int32, (count, groups), 1)
    tall = matmul((tall_row // 32 == tall_group).astype(LOW), marks)
    tall_row = lax.broadcasted_iota(jnp.int32, (count, 128), 0)
    tall_lane = lax.broadcasted_iota(jnp.int32, (count, 128), 1)
    column_ok = jnp.sum(jnp.where(tall_row % 32 == tall_lane, tall, 0.0), axis=1, keepdims=True)
    total_held = jnp.sum(row_ok, axis=1, keepdims=True)
    weight = row_ok / total_held
    raw = against(all_partners, all_anchors) * inv_temp
    positive = []
    eye = lax.broadcasted_iota(jnp.int32, (128, 128), 0)
    eye = eye == lax.broadcasted_iota(jnp.int32, (128, 128), 1)
    for at in range(0, count, 128):
        block = raw[at : at + 128, at : at + 128]
        positive.append(jnp.sum(jnp.where(eye, block, 0.0), axis=0, keepdims=True))
    positive = jnp.concatenate(positive, axis=1)
    masked = jnp.where(column_ok > 0, raw, -1e30)
    peak = jnp.max(masked, axis=0, keepdims=True)
    lifted = jnp.exp(masked - peak)
    whole = jnp.sum(lifted, axis=0, keepdims=True)
    sim_total = peak + jnp.log(whole)
    crossed = jnp.sum(lifted * masked, axis=0, keepdims=True) / whole
    loss = jnp.sum(weight * (sim_total - positive), axis=1, keepdims=True)
    temp_grad = jnp.sum(weight * (positive - crossed), axis=1, keepdims=True)
    line = lax.broadcasted_iota(jnp.int32, (8, 128), 0)
    scalars[...] = jnp.where(line == 0, loss, temp_grad)
    mine = place(here[0], here[1], here[2], here[3])
    first = pl.multiple_of(mine * 32, 32)
    my_anchors = anchors[pl.ds(first, 32)]
    my_partners = partners[pl.ds(first, 32)]
    tall_lane = lax.broadcasted_iota(jnp.int32, (32, 128), 1)
    tall_row = lax.broadcasted_iota(jnp.int32, (32, 128), 0)
    my_flags = flat[pl.ds(mine, 1)]
    my_ok = jnp.sum(jnp.where(tall_lane == tall_row, my_flags, 0.0), axis=1, keepdims=True)
    my_weight = my_ok / total_held
    back = against(my_partners, all_anchors) * inv_temp
    back_shares = jnp.exp(jnp.where(my_ok > 0, back, -1e30) - sim_total) * weight
    grad_partner = inv_temp * (
        split_matmul(back_shares, all_anchors) - my_weight * my_anchors.astype(FULL)
    )
    mine_masked = jnp.where(row_ok > 0, against(my_anchors, all_partners) * inv_temp, -1e30)
    peak = jnp.max(mine_masked, axis=1, keepdims=True)
    lifted = jnp.exp(mine_masked - peak)
    my_shares = lifted * (my_weight / jnp.sum(lifted, axis=1, keepdims=True))
    grad_anchor = inv_temp * (
        split_matmul(my_shares, all_partners) - my_weight * my_partners.astype(FULL)
    )
    grad_unit = jnp.concatenate([grad_anchor, grad_partner], axis=0)
    pre = pool_back(grad_unit, pooled[...])
    grad_pre[...] = pre
    start_outer[...], start_second[...], start_sums[...] = start_outer_back(
        pre, w_pool[...], nh2[...], rs2[:, :1], picked[3], small
    )


def contrast(here, blocks, log_temp, pooled, w_pool, nh2, rs2, picked, small):
    width = pooled.shape[1]
    count = 32 * 32
    whole = pl.BlockSpec(memory_space=pltpu.VMEM)
    return pl.pallas_call(
        loss_kernel,
        name="contrast",
        grid_spec=pltpu.PrefetchScalarGridSpec(
            num_scalar_prefetch=1,
            grid=(),
            in_specs=[pl.BlockSpec(memory_space=pl.ANY)] * 8 + [whole] * 7,
            out_specs=[whole] * 5,
            scratch_shapes=[
                pltpu.VMEM((count, width), LOW),
                pltpu.VMEM((count, width), LOW),
                pltpu.VMEM((40, 128), FULL),
                pltpu.SemaphoreType.DMA,
            ],
        ),
        out_shape=[
            shaped((8, 128), FULL),
            shaped((64, width), LOW),
            shaped((64, width), LOW),
            shaped((64, width), FULL),
            shaped((8, width), FULL),
        ],
        compiler_params=pltpu.CompilerParams(vmem_limit_bytes=36 * 2**20),
        cost_estimate=pl.CostEstimate(
            flops=2 * count * count * width, transcendentals=0, bytes_accessed=4 * count * width
        ),
    )(here, *blocks, log_temp.reshape(1, 1), pooled, w_pool, nh2, rs2, picked, small)


def start_back(outer, second, picked, rs1, slope, w_outer, w_inner, w_out, small):
    width = outer.shape[1]
    wide = w_inner.shape[0]
    inner = []
    grad_normed = second
    for j in range(wide):
        grad_active = against(outer, w_outer[j * width : (j + 1) * width])
        low = (grad_active * slope[:, j * width : (j + 1) * width].astype(FULL)).astype(LOW)
        inner.append(low)
        grad_normed = grad_normed + against(low, w_inner[j])
    unit_one = picked[1].astype(FULL)
    first = normal_back(grad_normed * small[3:4], unit_one, rs1)
    kept = first * (picked[2].astype(FULL) * keep_scale)
    branch = (kept[:32] + kept[32:]).astype(LOW)
    base = first[:32] + first[32:]
    att = against(branch, w_out).astype(LOW)
    sums = [down(branch), down(grad_normed * unit_one), down(grad_normed)]
    return inner, branch, base, att, sums, [down(low) for low in inner]


def down(value):
    return jnp.sum(value.astype(FULL), axis=0, keepdims=True)


def start_outer_back(grad_pre, w_pool, nh2, rs2, keeps, small):
    grad_out = against(grad_pre, w_pool)
    normed = nh2.astype(FULL)
    grad_second = normal_back(grad_out * small[6:7], normed, rs2)
    low = (grad_second * (keeps.astype(FULL) * keep_scale)).astype(LOW)
    sums = [down(low), down(grad_out * normed), down(grad_out), down(grad_pre)]
    sums.append(jnp.zeros((4, low.shape[1]), FULL))
    return low, grad_second, jnp.concatenate(sums)


def start_back_kernel(
    outer, second, old_sums, picked, rs1, slope, small, w_outer_hbm, w_inner_hbm, w_out_hbm,
    inner, branch, base, att, sums, w_outer, w_inner, w_out, sems,
):
    copies = [
        pltpu.make_async_copy(source, target, sems.at[n])
        for n, (source, target) in enumerate(
            ((w_outer_hbm, w_outer), (w_inner_hbm, w_inner), (w_out_hbm, w_out))
        )
    ]
    for copy in copies:
        copy.start()
    for copy in copies:
        copy.wait()
    out = start_back(
        outer[...], second[...], picked, rs1[:, :1], slope, w_outer, w_inner, w_out[...], small
    )
    width = outer.shape[1]
    for j, low in enumerate(out[0]):
        inner[:, j * width : (j + 1) * width] = low
    branch[...] = out[1]
    base[...] = out[2]
    att[...] = out[3]
    sums[0:2] = jnp.zeros((2, width), FULL)
    for n, value in enumerate(out[4]):
        sums[2 + n : 3 + n] = value
    sums[5:9] = old_sums[0:4]
    for j, value in enumerate(out[5]):
        sums[9 + j : 10 + j] = value
    sums[13:24] = jnp.zeros((11, width), FULL)


def start_backward(outer, second, old_sums, picked, rs1, slope, small, w_outer, w_inner, w_out):
    ff, width = w_outer.shape
    whole = pl.BlockSpec(memory_space=pltpu.VMEM)
    outside = pl.BlockSpec(memory_space=pl.ANY)
    return call(
        start_back_kernel,
        "start_backward",
        256 * width * ff,
        4 * width * ff,
        in_specs=[whole] * 7 + [outside] * 3,
        out_shape=[
            shaped((64, ff), LOW),
            shaped((32, width), LOW),
            shaped((32, width), FULL),
            shaped((32, width), LOW),
            shaped((24, width), FULL),
        ],
        scratch_shapes=[
            pltpu.VMEM(w_outer.shape, LOW),
            pltpu.VMEM(w_inner.shape, LOW),
            pltpu.VMEM(w_out.shape, LOW),
            pltpu.SemaphoreType.DMA((3,)),
        ],
    )(outer, second, old_sums, picked, rs1, slope, small, w_outer, w_inner, w_out)


def inner_back_kernel(
    here, grad_outer, slope, second, nh1, rs1, keep, w_outer, w_inner, w_out, small,
    grad_inner, grad_branch, grad_att, base, sums, wide_sums, mark,
):
    hand_on(here, mark)
    row = pl.program_id(0)
    length = grad_branch.shape[0]
    width = grad_branch.shape[1]
    step = 256

    @pl.when(row == 0)
    def _():
        sums[...] = jnp.zeros_like(sums)
        wide_sums[...] = jnp.zeros_like(wide_sums)

    low_outer = grad_outer[...]
    grad_normed = second[...].astype(FULL)
    for j in range(w_inner.shape[0]):
        for at in range(0, width, step):
            lane = j * width + at
            grad_active = against(low_outer, w_outer[lane : lane + step])
            low = (grad_active * slope[:, lane : lane + step].astype(FULL)).astype(LOW)
            grad_inner[:, lane : lane + step] = low
            wide_sums[:, lane : lane + step] += jnp.sum(low.astype(FULL), axis=0, keepdims=True)
        grad_normed = grad_normed + against(
            grad_inner[:, j * width : (j + 1) * width], w_inner[j]
        )
    normed = nh1[...].astype(FULL)
    grad_first = normal_back(grad_normed * small[3:4], normed, rs1[...])
    sums[0:1] += jnp.sum(grad_normed * normed, axis=0, keepdims=True)
    sums[1:2] += jnp.sum(grad_normed, axis=0, keepdims=True)
    keeps = keep[:, 0, 0].astype(FULL) * keep_scale
    branch = (grad_first[:length] * keeps[0] + grad_first[length:] * keeps[1]).astype(LOW)
    grad_branch[...] = branch
    sums[2:3] += jnp.sum(branch.astype(FULL), axis=0, keepdims=True)
    base[...] = grad_first[:length] + grad_first[length:]
    grad_att[...] = against(branch, w_out[...]).astype(LOW)


def inner_backward(
    here, grad_outer, slope, second, nh1, rs1, keep_masks, w_outer, w_inner, w_out, small
):
    tokens, ff = slope.shape
    slots, length, width = keep_masks.shape[2:]
    two = 2 * length
    return call(
        inner_back_kernel,
        "inner_backward",
        4 * tokens * width * ff,
        5 * tokens * ff,
        grid=(slots,),
        in_specs=[
            scalars_spec(),
            pl.BlockSpec((two, width), lambda r: (r, 0)),
            pl.BlockSpec((two, ff), lambda r: (r, 0)),
            pl.BlockSpec((two, width), lambda r: (r, 0)),
            pl.BlockSpec((two, width), lambda r: (r, 0)),
            pl.BlockSpec((two, 1), lambda r: (r, 0)),
            pl.BlockSpec((2, 1, 1, length, width), lambda r: (0, 0, r, 0, 0)),
            fixed(w_outer.shape),
            fixed(w_inner.shape),
            fixed(w_out.shape),
            fixed(small.shape),
        ],
        out_specs=[
            pl.BlockSpec((two, ff), lambda r: (r, 0)),
            pl.BlockSpec((length, width), lambda r: (r, 0)),
            pl.BlockSpec((length, width), lambda r: (r, 0)),
            pl.BlockSpec((length, width), lambda r: (r, 0)),
            fixed((8, width)),
            fixed((1, ff)),
            scalars_spec(),
        ],
        out_shape=[
            shaped((tokens, ff), LOW),
            shaped((slots * length, width), LOW),
            shaped((slots * length, width), LOW),
            shaped((slots * length, width), FULL),
            shaped((8, width), FULL),
            shaped((1, ff), FULL),
            shaped((4,), jnp.int32),
        ],
    )(here, grad_outer, slope, second, nh1, rs1, keep_masks, w_outer, w_inner, w_out, small)


def attend_back_kernel(grad_att, start_att, table, qkv, probs, grad_qkv, sums):
    row = pl.program_id(0)
    length, width = grad_att.shape
    even = lax.broadcasted_iota(jnp.int32, (length, 128), 1) < 64

    @pl.when(row == 0)
    def _():
        sums[...] = jnp.zeros_like(sums)

    placed = across(table[0, :32, :length], start_att[...])
    whole_att = (grad_att[...].astype(FULL) + placed).astype(LOW)
    for p in range(width // 128):
        at = p * 128
        query = halves(qkv[:, at : at + 128], even)
        key = halves(qkv[:, width + at : width + at + 128], even)
        value = qkv[:, 2 * width + at : 2 * width + at + 128]
        flow = halves(whole_att[:, at : at + 128], even)
        share = probs[0, p]
        share_f = share.astype(FULL)
        grad_share = against(flow, value)
        inside = jnp.sum(grad_share * share_f, axis=-1, keepdims=True)
        grad_scores = (share_f * (grad_share - inside)).astype(LOW)
        grad_value = across(share, flow).astype(LOW)
        side = jnp.concatenate([grad_scores[:length], grad_scores[length:]], axis=1)
        grad_query = (matmul(side, key) * 0.125).astype(LOW)
        grad_key = (across(grad_scores, query) * 0.125).astype(LOW)
        grad_qkv[:, at : at + 128] = grad_query
        grad_qkv[:, width + at : width + at + 128] = grad_key
        grad_qkv[:, 2 * width + at : 2 * width + at + 128] = grad_value
        sums[0:1, at : at + 128] += jnp.sum(grad_query.astype(FULL), axis=0, keepdims=True)
        sums[1:2, at : at + 128] += jnp.sum(grad_value.astype(FULL), axis=0, keepdims=True)


def attend_backward(grad_att, start_att, table, qkv, probs):
    slots, pairs_of, _, length = probs.shape
    width = grad_att.shape[1]
    return call(
        attend_back_kernel,
        "attend_backward",
        16 * slots * length * length * width,
        18 * slots * length * width,
        grid=(slots,),
        in_specs=[
            pl.BlockSpec((length, width), lambda r: (r, 0)),
            fixed((32, width)),
            pl.BlockSpec((1, 64, 2 * length), lambda r: (r, 0, 0)),
            pl.BlockSpec((length, 3 * width), lambda r: (r, 0)),
            pl.BlockSpec((1, pairs_of, 2 * length, length), lambda r: (r, 0, 0, 0)),
        ],
        out_specs=[
            pl.BlockSpec((length, 3 * width), lambda r: (r, 0)),
            fixed((8, width)),
        ],
        out_shape=[shaped((slots * length, 3 * width), LOW), shaped((8, width), FULL)],
    )(grad_att, start_att, table, qkv, probs)


def input_kernel(here, base, start_base, table, grad_qkv, weights, out, mark):
    hand_on(here, mark)
    width = weights.shape[1]
    total = base[...] + lax.dot_general(
        table[...].astype(FULL),
        start_base[...],
        (((0,), (0,)), ((), ())),
        precision=precise,
        preferred_element_type=FULL,
    )
    for j in range(3):
        total = total + against(grad_qkv[:, j * width : (j + 1) * width], weights[j])
    out[...] = total


def input_gradient(here, base, start_base, table, grad_qkv, weights):
    tokens, width = base.shape
    rows, _, two = table.shape
    table = table[:, :32, : two // 2].transpose(1, 0, 2).reshape(32, tokens)
    args = (base, start_base, table, grad_qkv, weights)
    one = pl.Buffered(1)
    return call(
        input_kernel,
        "input_gradient",
        6 * tokens * width * width,
        14 * tokens * width,
        grid=(1,),
        in_specs=[scalars_spec()]
        + [pl.BlockSpec(a.shape, lambda r, n=a.ndim: (0,) * n, pipeline_mode=one) for a in args],
        out_specs=[pl.BlockSpec(base.shape, lambda r: (0, 0), pipeline_mode=one), scalars_spec()],
        out_shape=[shaped((tokens, width), FULL), shaped((4,), jnp.int32)],
    )(here, *args)


def store_part(here, value, z, x, c, y, kept, away, at):
    on_x = here[1] ^ x
    on_y = here[3] ^ y
    index = 2 * on_y + on_x if c == 0 else 2 * on_x + on_y

    @pl.when(here[2] == c)
    def _():
        kept[(index,) + at] = value

    @pl.when(here[2] != c)
    def _():
        away[(index,) + at] = value


def outer_weight_kernel(
    here_ref, active, grad_outer, start_active, start_outer, cls, grad_pre, kept, away
):
    here = [here_ref[i] for i in range(4)]
    rows = kept.shape[3]
    step = pl.program_id(0)
    last = pl.num_programs(0) - 1

    @pl.when(step < last)
    def _():
        whole = across(active[...], grad_outer[...]) + across(start_active[...], start_outer[...])
        whole = whole.astype(LOW)
        for n in range(32):
            x, c, y, item = n // 16, n // 8 % 2, n // 4 % 2, n % 4
            value = whole[n * rows : (n + 1) * rows]
            store_part(here, value, 0, x, c, y, kept, away, (step, item))

    @pl.when(step == last)
    def _():
        store_parts(here, across(cls[...], grad_pre[...]).astype(LOW), kept, away, 4)


def outer_weight(here, active, grad_outer, start_active, start_outer, *others):
    tokens, ff = active.shape
    width = grad_outer.shape[1]
    part = ff // 4
    shape = (4, 4, 5, width // 32, width)
    return call(
        outer_weight_kernel,
        "outer_weight",
        2 * tokens * ff * width,
        2 * tokens * ff,
        grid_spec=pltpu.PrefetchScalarGridSpec(
            num_scalar_prefetch=1,
            grid=(5,),
            in_specs=[
                pl.BlockSpec((tokens, part), lambda z, _: (0, jnp.minimum(z, 3))),
                pl.BlockSpec((tokens, width), lambda z, _: (0, 0)),
                pl.BlockSpec((64, part), lambda z, _: (0, jnp.minimum(z, 3))),
                pl.BlockSpec((64, width), lambda z, _: (0, 0)),
            ]
            + [fixed(other.shape) for other in others],
            out_specs=[fixed(shape)] * 2,
        ),
        out_shape=[shaped(shape, LOW)] * 2,
    )(here, active, grad_outer, start_active, start_outer, *others)


def store_parts(here, whole, kept, away, item=0):
    rows = kept.shape[3]
    for n in range(32):
        z, x, c, y = n // 8, n // 4 % 2, n // 2 % 2, n % 2
        store_part(here, whole[n * rows : (n + 1) * rows], z, x, c, y, kept, away, (z, item))


def inner_weight_kernel(
    here_ref, n1, grad_inner, start_n1, start_inner, att, branch, start_att, start_branch, kept, away
):
    here = [here_ref[i] for i in range(4)]
    step = pl.program_id(0)
    last = pl.num_programs(0) - 1

    @pl.when(step < last)
    def _():
        whole = across(n1[...], grad_inner[...]) + across(start_n1[0], start_inner[...])
        store_parts(here, whole.astype(LOW), kept, away)

    @pl.when(step == last)
    def _():
        whole = across(att[...], branch[...]) + across(start_att[...], start_branch[...])
        store_parts(here, whole.astype(LOW), kept, away)


def inner_weight(here, n1, grad_inner, picked, start_inner, *others):
    tokens, ff = grad_inner.shape
    width = n1.shape[1]
    wide = ff // width
    spec = pl.BlockSpec((4, 4, 1, width // 32, width), lambda j, _: (0, 0, j, 0, 0))
    shape = shaped((4, 4, wide + 1, width // 32, width), LOW)
    return call(
        inner_weight_kernel,
        "inner_weight",
        2 * tokens * ff * width,
        2 * tokens * ff,
        grid_spec=pltpu.PrefetchScalarGridSpec(
            num_scalar_prefetch=1,
            grid=(wide + 1,),
            in_specs=[
                pl.BlockSpec((tokens, width), lambda j, _: (0, 0)),
                pl.BlockSpec((tokens, width), lambda j, _: (0, jnp.minimum(j, wide - 1))),
                pl.BlockSpec((1, 64, width), lambda j, _: (0, 0, 0)),
                pl.BlockSpec((64, width), lambda j, _: (0, jnp.minimum(j, wide - 1))),
            ]
            + [fixed(other.shape) for other in others],
            out_specs=[spec, spec],
        ),
        out_shape=[shape, shape],
    )(here, n1, grad_inner, picked, start_inner, *others)


def attend_weight_kernel(
    here_ref, x, grad_qkv, start_sums, sums_qv, sums_one, sums_two, wide_sums, kept, away
):
    here = [here_ref[i] for i in range(4)]
    step = pl.program_id(0)

    @pl.when(step < 3)
    def _():
        store_parts(here, across(x[...], grad_qkv[...]).astype(LOW), kept, away)

    @pl.when(step == 3)
    def _():
        width = x.shape[1]
        value = start_sums[...] + jnp.concatenate(
            [sums_qv[0:2], sums_one[2:3], sums_one[0:2], sums_two[0:3]]
            + [jnp.zeros((1, width), FULL)]
            + [wide_sums[:, j * width : (j + 1) * width] for j in range(4)]
            + [jnp.zeros((11, width), FULL)],
            axis=0,
        )
        value = value.astype(LOW)
        for index in range(4):
            for z in range(4):
                kept[index, z, 0] = value
                away[index, z, 0] = value


def attend_weight(here, x, grad_qkv, sums):
    tokens, width = x.shape
    spec = pl.BlockSpec((4, 4, 1, width // 32, width), lambda j, _: (0, 0, j, 0, 0))
    shape = shaped((4, 4, 4, width // 32, width), LOW)
    return call(
        attend_weight_kernel,
        "attend_weight",
        6 * tokens * width * width,
        8 * tokens * width,
        grid_spec=pltpu.PrefetchScalarGridSpec(
            num_scalar_prefetch=1,
            grid=(4,),
            in_specs=[
                pl.BlockSpec((tokens, width), lambda j, _: (0, 0)),
                pl.BlockSpec((tokens, width), lambda j, _: (0, jnp.minimum(j, 2))),
            ]
            + [fixed(value.shape) for value in sums],
            out_specs=[spec, spec],
        ),
        out_shape=[shape, shape],
    )(here, x, grad_qkv, *sums)


def gathered(shard):
    return lax.all_gather(shard, BOTH, axis=0, tiled=True)


def scattered(whole):
    return lax.psum_scatter(whole, BOTH, scatter_dimension=0, tiled=True)


def shared_contrast(unit, flags, log_temp, pooled):
    anchors, partners = unit[:28], unit[32:60]
    inv_temp = jnp.exp(-log_temp[0])
    anchors_all, partners_all = gathered(anchors), gathered(partners)
    column_ok = gathered(flags.astype(LOW)).astype(FULL)
    held_total = jnp.sum(column_ok)
    logits = against(anchors, partners_all) * inv_temp
    logits = jnp.where(column_ok[None, :] > 0, logits, -1e30)
    sim_peak = jnp.max(logits, axis=-1, keepdims=True)
    sim_total = sim_peak + jnp.log(jnp.sum(jnp.exp(logits - sim_peak), axis=-1, keepdims=True))
    anchors_f = anchors.astype(FULL)
    partners_f = partners.astype(FULL)
    positive = jnp.sum(anchors_f * partners_f, axis=-1) * inv_temp
    row_weight = flags / held_total
    loss_part = jnp.sum(row_weight * (sim_total[:, 0] - positive))
    shares = jnp.exp(logits - sim_total) * row_weight[:, None]
    temp_part = jnp.sum(row_weight * positive) - jnp.sum(
        shares * jnp.where(column_ok[None, :] > 0, logits, 0.0)
    )
    grad_anchor = inv_temp * (
        jnp.dot(shares, partners_all.astype(FULL), precision=precise)
        - row_weight[:, None] * partners_f
    )
    totals_all = gathered(sim_total[:, 0])
    back = against(partners, anchors_all) * inv_temp
    back = jnp.where(flags[:, None] > 0, back, -1e30)
    back_shares = jnp.exp(back - totals_all[None, :]) * (column_ok / held_total)[None, :]
    grad_partner = inv_temp * (
        jnp.dot(back_shares, anchors_all.astype(FULL), precision=precise)
        - row_weight[:, None] * anchors_f
    )
    loss, temp_grad = lax.psum((loss_part, temp_part), BOTH)
    pad = ((0, 4), (0, 0))
    grad_unit = jnp.concatenate([jnp.pad(grad_anchor, pad), jnp.pad(grad_partner, pad)])
    return loss.reshape(1), temp_grad.reshape(1), pool_back(grad_unit, pooled)


def pack_kernel(here_ref, *refs):
    vectors, b_inner = refs[:9], refs[9]
    w_query, w_key, w_value, w_out, w_inner = refs[10:15]
    one, two, narrow, broad = refs[15:]
    index = place(here_ref[0], here_ref[1], here_ref[2], here_ref[3])
    rows, width = w_query.shape
    band = b_inner.shape[1]
    per_row = width // band
    one[0] = w_query[...]
    one[1] = w_key[...]
    one[2] = w_value[...]
    for j in range(w_inner.shape[1] // width):
        two[j] = w_inner[:, j * width : (j + 1) * width]
    two[4] = w_out[...]
    narrow[...] = jnp.zeros_like(narrow)
    broad[...] = jnp.zeros_like(broad)
    for f, vector in enumerate(vectors):
        narrow[f : f + 1, :rows] = vector[...].astype(FULL)
    broad[0:1, :band] = b_inner[...].astype(FULL)
    placed = pltpu.roll(narrow[...], rows * index, 1)
    line = pltpu.roll(broad[...], band * lax.rem(index, per_row), 1)[0:1]
    at = lax.broadcasted_iota(jnp.int32, placed.shape, 0) == 9 + index // per_row
    placed = jnp.where(at, line, placed)
    one[3] = placed.astype(LOW)


def pack(here, vectors, b_inner, weights):
    w_query, w_key, w_value, w_out, w_inner = weights
    rows, width = w_query.shape
    return call(
        pack_kernel,
        "pack",
        0,
        40 * rows * width,
        grid_spec=pltpu.PrefetchScalarGridSpec(
            num_scalar_prefetch=1,
            grid=(1,),
            in_specs=[fixed((1, rows))] * 9
            + [fixed((1, b_inner.shape[0]))]
            + [fixed(weight.shape) for weight in weights],
            out_specs=[fixed((4, rows, width)), fixed((w_inner.shape[1] // width + 1, rows, width))],
            scratch_shapes=[pltpu.VMEM((24, width), FULL), pltpu.VMEM((8, width), FULL)],
        ),
        out_shape=[
            shaped((4, rows, width), LOW),
            shaped((w_inner.shape[1] // width + 1, rows, width), LOW),
        ],
    )(
        here,
        *[vector[None] for vector in vectors],
        b_inner[None],
        *weights,
    )


def small_sums(start_sums, sums_qv, sums_one, sums_two, wide_sums):
    width = start_sums.shape[1]
    wide = wide_sums.shape[1] // width
    return start_sums + jnp.concatenate(
        [
            sums_qv[0:2],
            sums_one[2:3],
            sums_one[0:2],
            sums_two[0:3],
            jnp.zeros((1, width), FULL),
            wide_sums.reshape(wide, width),
            jnp.zeros((24 - 9 - wide, width), FULL),
        ]
    )


def paired_body(
    hidden_in, row_counts, buckets, lengths, keep_masks, out_cotangent, vectors, b_inner, weights,
    log_temp,
):
    w_query, w_key, w_value, w_attn_out, w_inner, w_outer, w_pool = weights
    slots, length, width = hidden_in.shape
    tokens = slots * length
    ff = w_inner.shape[1]
    wide = ff // width
    index = lax.axis_index(BOTH)
    here = jnp.stack(whereabouts()).astype(jnp.int32)
    flat = hidden_in.reshape(tokens, width)
    first, second, both = first_pairs(), second_pairs(), across_pairs()

    pack_one, pack_two = pack(here, vectors, b_inner, (w_query, w_key, w_value, w_attn_out, w_inner))
    pack_three = jnp.concatenate([w_outer.reshape(wide, -1, width), w_pool[None]])
    come = along_z(pack_one)
    pack_one, pack_two, come = together(pack_one, pack_two, come)

    one = [jnp.stack([pack_one] + come)]
    come = [send(one[0], route) for route in (first, second, both)]
    come_two = along_z(pack_two)
    segment, starts, held_slots = layout(row_counts, buckets, lengths, length)
    table = pick_table(starts, held_slots, length)
    flags = held_slots.astype(FULL).reshape(slots * 4)
    flag_row = jnp.pad(flags, (0, width - slots * 4))[None]
    one, come, pack_two, come_two, segment, table, flag_row = together(
        one, come, pack_two, come_two, segment, table, flag_row
    )

    one += come
    two = [jnp.stack([pack_two] + come_two)]
    one_other = over_cores(one)
    come_three = [send(pack_three, along_pairs(k)) for k in (1, 2)]
    one, one_other, pack_three = together(one, one_other, pack_three)

    come = [send(two[0], first), send(two[0], second)]
    qkv_weights, small = in_order(here, one + one_other, (3, 0))
    come_three[0], pack_three, small, column = together(
        come_three[0], pack_three, small, two[0]
    )

    come.append(send(column, both))
    come_three.append(send(pack_three, along_pairs(3)))
    qkv_weights = qkv_weights.reshape(3, width, width)
    biases = jnp.stack([small[0], jnp.zeros_like(small[0]), small[1]])[:, None]
    qkv, att, probs, here = attend(here, flat, qkv_weights, biases, segment)
    two, come, pack_three, come_three, here = together(two, come, pack_three, come_three, here)

    two += come
    two_other = over_cores(two)
    three = [jnp.stack([pack_three] + come_three)]
    come = [send(three[0], route) for route in (first, second, both)]
    two, two_other, here = together(two, two_other, here)

    inner_weights, out_weight = in_order(here, two + two_other, (wide, 1))
    inner_weights = inner_weights.reshape(wide, width, width)
    out_weight = out_weight.reshape(width, width)
    n1, nh1, rs1, active, slope, picked, picked_att, picked_rs, start_active, start_slope = (
        inner_forward(
            att, hidden_in, keep_masks, out_weight, inner_weights, small, starts, held_slots
        )
    )
    three, come, start_active = together(three, come, start_active)

    three += come
    outer_weights, pool_weight = in_order(here, three + over_cores(three), (-wide, 1))
    outer_weights = outer_weights.reshape(ff, width)
    pool_weight = pool_weight.reshape(width, width)
    start_nh2, start_rs2, cls, pooled, unit = start_forward(
        start_active, picked, outer_weights, small, pool_weight, flag_row
    )
    unit, here = together(unit, here)

    come = along_z(unit)
    result, grad_outer, second_flow, sums_two, here = outer_both(
        here, active, n1, keep_masks, out_cotangent, segment, outer_weights, small
    )
    unit, come, here = together(unit, come, here)

    own = [jnp.stack([unit] + come)]
    come = [send(own[0], route) for route in (first, second, both)]
    grad_inner, grad_branch, grad_att, base, sums_one, wide_sums, here = inner_backward(
        here, grad_outer, slope, second_flow, nh1, rs1, keep_masks, outer_weights, inner_weights,
        out_weight, small,
    )
    own, come, here = together(own, come, here)

    own += come
    scalars, grad_pre, start_outer, start_second, start_sums = contrast(
        here, own + over_cores(own), log_temp, pooled, pool_weight, start_nh2, start_rs2, picked,
        small,
    )
    loss, temp_grad = scalars[0, :1], scalars[1, :1]

    outer_kept, outer_away = outer_weight(
        here, active, grad_outer, start_active, start_outer, cls, grad_pre
    )
    come = send(outer_away, core_pairs())
    outer_kept, start_outer = together(outer_kept, start_outer)
    start_inner, start_branch, start_base, start_att, start_sums = start_backward(
        start_outer, start_second, start_sums, picked, picked_rs, start_slope, small,
        outer_weights, inner_weights, out_weight,
    )
    come, outer_kept, start_inner, start_att, start_base, start_sums = together(
        come, outer_kept, start_inner, start_att, start_base, start_sums
    )

    outer_go, outer_own = halves_of(outer_kept, come)
    come = send(outer_go, second)
    outer_own, here = together(outer_own, here)
    inner_kept, inner_away = inner_weight(
        here, n1, grad_inner, picked, start_inner, att, grad_branch, picked_att, start_branch
    )
    outer_own, come, inner_kept, inner_away = together(outer_own, come, inner_kept, inner_away)

    come_inner = send(inner_away, core_pairs())
    outer_go, outer_own = quarters_of(outer_own, come)
    come = send(outer_go, first)
    inner_kept, come_inner, outer_own, come = together(inner_kept, come_inner, outer_own, come)

    inner_go, inner_own = halves_of(inner_kept, come_inner)
    come_inner = send(inner_go, second)
    parts_outer = over_z(add_low(outer_own, come))
    inner_own, start_att = together(inner_own, start_att)
    grad_qkv, sums_qv = attend_backward(grad_att, start_att, table, qkv, probs)
    attend_kept, attend_away = attend_weight(
        here, flat, grad_qkv, (start_sums, sums_qv, sums_one, sums_two, wide_sums)
    )
    parts_outer, inner_own, come_inner, attend_kept, attend_away = together(
        parts_outer, inner_own, come_inner, attend_kept, attend_away
    )

    come_attend = send(attend_away, core_pairs())
    inner_go, inner_own = quarters_of(inner_own, come_inner)
    come_inner = send(inner_go, first)
    attend_kept, come_attend, inner_own, here = together(
        attend_kept, come_attend, inner_own, here
    )

    attend_go, attend_own = halves_of(attend_kept, come_attend)
    come_attend = send(attend_go, second)
    attend_own, start_base, here = together(attend_own, start_base, here)
    input_grad, here = input_gradient(here, base, start_base, table, grad_qkv, qkv_weights)
    inner_own, come_inner, here = together(inner_own, come_inner, here)

    parts_inner = over_z(add_low(inner_own, come_inner))
    outer_part, pool_part = finish(here, parts_outer, inner=wide, tall=True)
    attend_own, come_attend, parts_inner[1], parts_inner[3], outer_part = together(
        attend_own, come_attend, parts_inner[1], parts_inner[3], outer_part
    )

    attend_go, attend_own = quarters_of(attend_own, come_attend)
    come_attend = send(attend_go, first)
    attend_own, come_attend = together(attend_own, come_attend)
    parts_attend = over_z(add_low(attend_own, come_attend))
    inner_part, out_part = finish(here, parts_inner, inner=wide)
    query_part, key_part, value_part, own_small, inner_bias_part = finish(
        here, parts_attend, vectors=9, band=b_inner.shape[0]
    )
    input_grad = input_grad.reshape(hidden_in.shape)
    inner_bias_part = inner_bias_part[0]
    parts = [query_part, key_part, value_part, out_part]
    small_parts = [own_small[i] for i in range(9)]
    return (
        loss,
        result,
        input_grad,
        parts[0],
        small_parts[0],
        parts[1],
        parts[2],
        small_parts[1],
        parts[3],
        small_parts[2],
        small_parts[3],
        small_parts[4],
        inner_part,
        inner_bias_part,
        outer_part,
        small_parts[5],
        small_parts[6],
        small_parts[7],
        pool_part,
        small_parts[8],
        temp_grad,
    )


def body(
    hidden_in,
    row_counts,
    buckets,
    lengths,
    keep_masks,
    out_cotangent,
    w_query,
    b_query,
    w_key,
    w_value,
    b_value,
    w_attn_out,
    b_attn_out,
    norm1_gain,
    norm1_bias,
    w_inner,
    b_inner,
    w_outer,
    b_outer,
    norm2_gain,
    norm2_bias,
    w_pool,
    b_pool,
    log_temp,
):
    slots, length, width = hidden_in.shape
    tokens = slots * length
    ff = w_inner.shape[1]
    wide = ff // width
    index = lax.axis_index(BOTH)
    here = jnp.stack(whereabouts()).astype(jnp.int32)
    vectors = (
        b_query,
        b_value,
        b_attn_out,
        norm1_gain,
        norm1_bias,
        b_outer,
        norm2_gain,
        norm2_bias,
        b_pool,
    )
    if paired():
        return paired_body(
            hidden_in, row_counts, buckets, lengths, keep_masks, out_cotangent, vectors, b_inner,
            (w_query, w_key, w_value, w_attn_out, w_inner, w_outer, w_pool), log_temp,
        )
    qkv_weights = jnp.stack([gathered(w) for w in (w_query, w_key, w_value)])
    out_weight = gathered(w_attn_out)
    rows = [gathered(v)[None] for v in vectors]
    rows.append(gathered(b_inner).reshape(wide, width))
    rows.append(jnp.zeros((24 - 9 - wide, width), LOW))
    small = jnp.concatenate(rows).astype(FULL)
    inner_weights = gathered(w_inner).reshape(width, wide, width).transpose(1, 0, 2)
    outer_weights = gathered(w_outer)
    pool_weight = gathered(w_pool)

    segment, starts, held_slots = layout(row_counts, buckets, lengths, length)
    table = pick_table(starts, held_slots, length)
    flags = held_slots.astype(FULL).reshape(slots * 4)
    flag_row = jnp.pad(flags, (0, width - slots * 4))[None]

    flat = hidden_in.reshape(tokens, width)
    biases = jnp.stack([small[0], jnp.zeros_like(small[0]), small[1]])[:, None]
    qkv, att, probs, _ = attend(here, flat, qkv_weights, biases, segment)
    n1, nh1, rs1, active, slope, picked, picked_att, picked_rs, start_active, start_slope = (
        inner_forward(
            att, hidden_in, keep_masks, out_weight, inner_weights, small, starts, held_slots
        )
    )
    start_nh2, start_rs2, cls, pooled, unit = start_forward(
        start_active, picked, outer_weights, small, pool_weight, flag_row
    )
    result, grad_outer, second_flow, sums_two, _ = outer_both(
        here, active, n1, keep_masks, out_cotangent, segment, outer_weights, small
    )
    loss, temp_grad, grad_pre = shared_contrast(unit[0], flags, log_temp, pooled)
    start_outer, start_second, start_sums = start_outer_back(
        grad_pre, pool_weight, start_nh2, start_rs2[:, :1], picked[3], small
    )
    start_inner, start_branch, start_base, start_att, start_sums = start_backward(
        start_outer, start_second, start_sums, picked, picked_rs, start_slope, small,
        outer_weights, inner_weights, out_weight,
    )
    grad_inner, grad_branch, grad_att, base, sums_one, wide_sums, _ = inner_backward(
        here, grad_outer, slope, second_flow, nh1, rs1, keep_masks, outer_weights, inner_weights,
        out_weight, small,
    )
    grad_qkv, sums_qv = attend_backward(grad_att, start_att, table, qkv, probs)
    grad_small = small_sums(start_sums, sums_qv, sums_one, sums_two, wide_sums)
    input_grad, _ = input_gradient(here, base, start_base, table, grad_qkv, qkv_weights)
    input_grad = input_grad.reshape(hidden_in.shape)
    parts = [scattered(across(flat, grad_qkv[:, j * width : (j + 1) * width])) for j in range(3)]
    parts.append(scattered(across(att, grad_branch) + across(picked_att, start_branch)))
    small_parts = [scattered(grad_small[i]) for i in range(9)]
    inner_bias_part = scattered(grad_small[9 : 9 + wide].reshape(ff))
    outer_part = scattered(across(active, grad_outer) + across(start_active, start_outer))
    inner_part = scattered(across(n1, grad_inner) + across(picked[0], start_inner))
    pool_part = scattered(across(cls, grad_pre))
    return (
        loss,
        result,
        input_grad,
        parts[0],
        small_parts[0],
        parts[1],
        parts[2],
        small_parts[1],
        parts[3],
        small_parts[2],
        small_parts[3],
        small_parts[4],
        inner_part,
        inner_bias_part,
        outer_part,
        small_parts[5],
        small_parts[6],
        small_parts[7],
        pool_part,
        small_parts[8],
        temp_grad,
    )


def solution(mesh):
    outer, inner = mesh.shape["dp"], mesh.shape["fsdp"]
    sizes = (4, 2, 2, 2) if (outer, inner) == (16, 2) else (outer, 1, 1, inner)
    mesh = jax.sharding.Mesh(mesh.devices.reshape(sizes), BOTH)
    in_specs = (
        P(BOTH, None, None),
        P(BOTH),
        P(BOTH),
        P(BOTH, None),
        P(None, None, BOTH, None, None),
        P(None, BOTH, None, None),
        P(BOTH, None),
        P(BOTH),
        P(BOTH, None),
        P(BOTH, None),
        P(BOTH),
        P(BOTH, None),
        P(BOTH),
        P(BOTH),
        P(BOTH),
        P(BOTH, None),
        P(BOTH),
        P(BOTH, None),
        P(BOTH),
        P(BOTH),
        P(BOTH),
        P(BOTH, None),
        P(BOTH),
        P(),
    )
    out_specs = (
        P(),
        P(None, BOTH, None, None),
        P(BOTH, None, None),
        P(BOTH, None),
        P(BOTH),
        P(BOTH, None),
        P(BOTH, None),
        P(BOTH),
        P(BOTH, None),
        P(BOTH),
        P(BOTH),
        P(BOTH),
        P(BOTH, None),
        P(BOTH),
        P(BOTH, None),
        P(BOTH),
        P(BOTH),
        P(BOTH),
        P(BOTH, None),
        P(BOTH),
        P(),
    )
    return jax.shard_map(body, mesh=mesh, in_specs=in_specs, out_specs=out_specs, check_vma=False)
```
